32 devices in a mesh: fsdp: 8 (over z, y), dp: 4 (over x, core).
Axes of the slice: x: 2, y: 2, z: 4, core: 2. Of those that a mesh axis runs over, the one named last changes fastest.
Arguments:
- features: bfloat16 [4, 32, 192, 2048], P('dp', 'fsdp'), may hold values from -6 to 6
- crop_scale: int32 [8], replicated, may hold values from 2 to 8, as said below
- crop_group: int32 [8], replicated, may hold values from 0 to 3, as said below
- labels: int32 [3, 4, 32, 192], P(None, 'dp', 'fsdp'), may hold values from 0 to 20
- w_reduce: bfloat16 [2048, 512], P('fsdp'), may hold values from -0.125 to 0.125
- gain_reduce: float32 [512], replicated, may hold values from 0.5 to 1.5
- bias_reduce: float32 [512], replicated, may hold values from -2 to 2
- w_middle: bfloat16 [512, 9, 512], P('fsdp'), may hold values from -0.09375 to 0.09375
- gain_middle: float32 [512], replicated, may hold values from 0.5 to 1.5
- bias_middle: float32 [512], replicated, may hold values from -2 to 2
- w_expand: bfloat16 [512, 2048], P('fsdp'), may hold values from -0.25 to 0.25
- gain_expand: float32 [2048], replicated, may hold values from 0.5 to 1.5
- bias_expand: float32 [2048], replicated, may hold values from -2 to 2
- w_heads: bfloat16 [2048, 3, 9, 256], P('fsdp'), may hold values from -0.046875 to 0.046875
- gain_heads: float32 [3, 256], replicated, may hold values from 0.5 to 1.5
- bias_heads: float32 [3, 256], replicated, may hold values from -2 to 2
- w_class: bfloat16 [3, 256, 21], replicated, may hold values from -0.75 to 0.75
- b_class: float32 [3, 21], replicated, may hold values from -3 to 3
Outputs:
- grad_features: float32 [4, 32, 192, 2048], P('dp', 'fsdp')
- grad_reduce: float32 [2048, 512], P('fsdp')
- grad_middle: float32 [512, 9, 512], P('fsdp')
- grad_expand: float32 [512, 2048], P('fsdp')
- grad_heads: float32 [2048, 3, 9, 256], P('fsdp')
- grad_gain_reduce: float32 [512], replicated
- grad_bias_reduce: float32 [512], replicated
- grad_gain_middle: float32 [512], replicated
- grad_bias_middle: float32 [512], replicated
- grad_gain_expand: float32 [2048], replicated
- grad_bias_expand: float32 [2048], replicated
- grad_gain_heads: float32 [3, 256], replicated
- grad_bias_heads: float32 [3, 256], replicated
- grad_class: float32 [3, 256, 21], replicated
- grad_class_bias: float32 [3, 21], replicated
- task_weights: float32 [3], replicated
The draws below stay inside these ranges and needn't reach their ends.
Inputs may be any that keep to these rules, and one draw needn't show every extreme that they name: `crop_group`: every index of dp receives exactly 2 crops. `crop_scale`: code 8 occurs in every draw.
All inputs are finite; a program needn't handle non-finite values.
Results may differ from the reference program's by a relative error of at most 0.02.
Values may be sent and summed in bfloat16 or wider, within the bound.
No kernel may reach another device: no remote copies, remote signals or barrier semaphores. Data moves between devices by JAX's collectives and lax.ppermute only.
A program may use at most 320 MiB of HBM per device.

```python
from functools import partial
import jax
import jax.numpy as jnp
from jax import lax

D_IN = 2048
MID = 512
HEAD = 256
CLASSES = 21
TASKS = 3
CROPS_GRP = 2
W_UNIT = 12
COLS = 192
ROWS = 32
CROPS = 8
N_DP = 4


def draw_crop_group(key, part):
    key = jax.random.fold_in(key, 11)
    order = jax.random.permutation(key, CROPS)
    return (order // CROPS_GRP).astype(jnp.int32)


def draw_crop_scale(key, part):
    key = jax.random.fold_in(key, 12)
    first, second = jax.random.split(key)
    codes = jax.random.randint(first, (CROPS,), 2, 9)
    chosen = jax.random.randint(second, (), 0, CROPS)
    return jnp.where(jnp.arange(CROPS) == chosen, 8, codes).astype(jnp.int32)


def plant(drawn, key, low, high):
    extent = drawn.shape
    place = [jax.random.randint(jax.random.fold_in(key, axis), (), 0, extent[axis]) for axis in range(len(extent))]
    drawn = drawn.at[tuple(place)].set(low)
    longest = extent.index(max(extent))
    place[longest] = (place[longest] + 1) % extent[longest]
    return drawn.at[tuple(place)].set(high)


def levels(stream_key, shape, cuts, smallest, high):
    level = 1.0
    for position, shards_of in cuts:
        steps = jax.random.uniform(jax.random.fold_in(jax.random.fold_in(stream_key, 6), position), (shards_of,), jnp.float32, smallest / len(cuts), high / len(cuts))
        level = level * jnp.repeat(jnp.exp(steps), shape[position] // shards_of).reshape((-1,) + (1,) * (len(shape) - 1 - position))
    return level


def bell_draw(stream_key, shape, spread, bound, cuts=(), held_as=jnp.bfloat16):
    level = levels(stream_key, shape, cuts, -0.22, 0.18) if cuts else 1.0
    values = jax.random.normal(stream_key, shape, jnp.float32) * spread * level
    return jnp.minimum(jnp.maximum(values, -bound), bound).astype(held_as)


def setup_inputs(seed: int = 0) -> dict:
    key_list = jax.random.split(jax.random.key(seed), 19)
    features = bell_draw(key_list[0], (N_DP, ROWS, COLS, D_IN), 1.0, 6.0, ((0, 4), (1, 8)))
    crop_scale = draw_crop_scale(jax.random.fold_in(key_list[18], 71), 0)
    crop_group = draw_crop_group(jax.random.fold_in(key_list[18], 71), 0)
    labels = plant(jax.random.randint(key_list[3], (TASKS, N_DP, ROWS, COLS), 0, CLASSES), jax.random.fold_in(key_list[3], 1), 0, CLASSES - 1).astype(jnp.int32)
    w_reduce = bell_draw(key_list[4], (D_IN, MID), D_IN ** -0.5, 0.125, ((0, 8),))
    gain_reduce = jnp.clip(1.0 + 0.1 * jax.random.normal(key_list[5], (MID,), jnp.float32), 0.5, 1.5)
    bias_reduce = bell_draw(key_list[6], (MID,), 0.3, 2.0, (), jnp.float32)
    w_middle = bell_draw(key_list[7], (MID, 9, MID), (9 * MID) ** -0.5, 0.09375, ((0, 8),))
    gain_middle = jnp.clip(1.0 + 0.1 * jax.random.normal(key_list[8], (MID,), jnp.float32), 0.5, 1.5)
    bias_middle = bell_draw(key_list[9], (MID,), 0.3, 2.0, (), jnp.float32)
    w_expand = bell_draw(key_list[10], (MID, D_IN), MID ** -0.5, 0.25, ((0, 8),))
    gain_expand = jnp.clip(1.0 + 0.1 * jax.random.normal(key_list[11], (D_IN,), jnp.float32), 0.5, 1.5)
    bias_expand = bell_draw(key_list[12], (D_IN,), 0.3, 2.0, (), jnp.float32)
    w_heads = bell_draw(key_list[13], (D_IN, TASKS, 9, HEAD), (9 * D_IN) ** -0.5, 0.046875, ((0, 8),))
    gain_heads = jnp.clip(1.0 + 0.1 * jax.random.normal(key_list[14], (TASKS, HEAD), jnp.float32), 0.5, 1.5)
    bias_heads = bell_draw(key_list[15], (TASKS, HEAD), 0.3, 2.0, (), jnp.float32)
    w_class = bell_draw(key_list[16], (TASKS, HEAD, CLASSES), (HEAD // 4) ** -0.5, 0.75)
    b_class = bell_draw(key_list[17], (TASKS, CLASSES), 0.5, 3.0, (), jnp.float32)
    return {"features": features, "crop_scale": crop_scale, "crop_group": crop_group, "labels": labels, "w_reduce": w_reduce, "gain_reduce": gain_reduce, "bias_reduce": bias_reduce, "w_middle": w_middle, "gain_middle": gain_middle, "bias_middle": bias_middle, "w_expand": w_expand, "gain_expand": gain_expand, "bias_expand": bias_expand, "w_heads": w_heads, "gain_heads": gain_heads, "bias_heads": bias_heads, "w_class": w_class, "b_class": b_class}


@jax.custom_vjp
def low(v):
    return lax.optimization_barrier(v.astype(jnp.bfloat16)).astype(jnp.float32)

@jax.custom_vjp
def low_back(v):
    return v

def low_keep(v):
    return (low(v), None)

def low_pass(kept, grad):
    return (grad,)

def back_keep(v):
    return (v, None)

def back_low(kept, grad):
    return (low(grad),)
low.defvjp(low_keep, low_pass)
low_back.defvjp(back_keep, back_low)
eps = 1e-05
mid_rate = 2
head_rates = (12, 24, 36)
precise = lax.Precision.HIGHEST

def along(value, offset, axis):
    size = value.shape[axis]
    if offset == 0:
        return value
    if abs(offset) >= size:
        return jnp.zeros_like(value)
    widths = [(0, 0)] * value.ndim
    if offset > 0:
        widths[axis] = (0, offset)
        return lax.slice_in_dim(jnp.pad(value, widths), offset, offset + size, axis=axis)
    widths[axis] = (-offset, 0)
    return lax.slice_in_dim(jnp.pad(value, widths), 0, size, axis=axis)

def tables(crop_scale, crop_group):

    def one_group(group):
        mine = (crop_group == group).astype(jnp.int32)
        widths = crop_scale * W_UNIT * mine
        ends = jnp.cumsum(widths)
        starts = ends - widths
        column = jnp.arange(COLS, dtype=jnp.int32)[:, None]
        return ((column >= starts[None, :]) & (column < ends[None, :])).astype(jnp.float32)
    return jax.vmap(one_group)(jnp.arange(N_DP, dtype=jnp.int32))

def same_crop(inside, offset):
    return lax.optimization_barrier(jnp.sum(inside * along(inside, offset, 1), axis=2))

def batch_norm(value, gain, bias, valid, count):
    mean = lax.optimization_barrier(jnp.sum(value * valid, axis=(0, 1, 2))) / count
    square = lax.optimization_barrier(jnp.sum(value * value * valid, axis=(0, 1, 2))) / count
    scale = lax.rsqrt(square - mean * mean + eps)
    return (value - mean) * scale * gain + bias

def middle_conv(hidden, weight, inside):
    total = jnp.zeros(hidden.shape[:3] + (weight.shape[2],), jnp.float32)
    for ir in range(3):
        for ic in range(3):
            dcol = (ic - 1) * mid_rate
            source = along(along(hidden, (ir - 1) * mid_rate, 1), dcol, 2) * same_crop(inside, dcol)[:, None, :, None]
            total = total + jnp.einsum('grci,io->grco', source, weight[:, 3 * ir + ic, :], precision=precise)
    return total

def block(features, w_reduce, gain_reduce, bias_reduce, w_middle, gain_middle, bias_middle, w_expand, gain_expand, bias_expand, inside, valid, count):
    source = features * valid
    reduced = low_back(jnp.einsum('grci,io->grco', source, w_reduce, precision=precise))
    hidden1 = low(jax.nn.silu(batch_norm(reduced, gain_reduce, bias_reduce, valid, count)) * valid)
    middled = low_back(middle_conv(hidden1, w_middle, inside))
    hidden2 = low(jax.nn.silu(batch_norm(middled, gain_middle, bias_middle, valid, count)) * valid)
    expanded = low_back(jnp.einsum('grci,io->grco', hidden2, w_expand, precision=precise))
    return jax.nn.silu(batch_norm(expanded, gain_expand, bias_expand, valid, count) + source) * valid

def row_term(grid, weight, masks, rate):
    total = jnp.zeros(grid.shape[:3] + (weight.shape[2],), jnp.float32)
    for ic in range(3):
        source = along(grid, (ic - 1) * rate, 2) * masks[ic][:, None, :, None]
        total = total + jnp.einsum('grci,io->grco', source, weight[:, ic, :], precision=precise)
    return total

def head_loss(grid, weight, gain, bias, w_cls, b_cls, labels, inside, valid, count, rate):
    masks = tuple((same_crop(inside, (ic - 1) * rate) for ic in range(3)))
    term_fn = jax.checkpoint(partial(row_term, rate=rate))
    mixed = jnp.zeros(grid.shape[:3] + (weight.shape[2],), jnp.float32)
    for ir in range(3):
        term = term_fn(grid, weight[:, 3 * ir:3 * ir + 3, :], masks)
        if ir != 1:
            term = low(term)
        mixed = mixed + along(term, (ir - 1) * rate, 1)
    mixed = low_back(mixed)
    activ = low(jax.nn.silu(batch_norm(mixed, gain, bias, valid, count)) * valid)
    logits = low_back(jnp.einsum('grch,hk->grck', activ, w_cls, precision=precise) + b_cls)
    logp = jax.nn.log_softmax(logits, axis=-1)
    picked = jnp.take_along_axis(logp, labels[..., None], axis=-1)[..., 0]
    return -jnp.sum(picked * valid[..., 0]) / CROPS

def task_scales(gram):
    norms = jnp.sqrt(jnp.stack([gram[0, 0], gram[1, 1], gram[2, 2]]) + 1e-12)
    corr = gram / (norms[:, None] * norms[None, :]) + 0.1 * jnp.eye(3, dtype=jnp.float32)
    adjugate = jnp.stack([jnp.cross(corr[:, 1], corr[:, 2]), jnp.cross(corr[:, 2], corr[:, 0]), jnp.cross(corr[:, 0], corr[:, 1])])
    weights = lax.optimization_barrier(jnp.sum(adjugate, axis=1))
    return 3.0 * weights * jnp.mean(norms) / (norms * jnp.sum(weights))

def reference(features, crop_scale, crop_group, labels, w_reduce, gain_reduce, bias_reduce, w_middle, gain_middle, bias_middle, w_expand, gain_expand, bias_expand, w_heads, gain_heads, bias_heads, w_class, b_class):
    inside = tables(crop_scale, crop_group)
    valid = lax.optimization_barrier(jnp.sum(inside, axis=2))[:, None, :, None]
    count = jnp.sum(valid) * ROWS
    params = [value.astype(jnp.float32) for value in (features, w_reduce, gain_reduce, bias_reduce, w_middle, gain_middle, bias_middle, w_expand, gain_expand, bias_expand)]
    shared, block_back = jax.vjp(lambda *p: block(*p, inside, valid, count), *params)
    grid = low(shared)
    heads_f = w_heads.astype(jnp.float32)
    class_f = w_class.astype(jnp.float32)
    task_grads = []
    head_parts = []
    for task in range(TASKS):
        loss_fn = partial(head_loss, labels=labels[task], inside=inside, valid=valid, count=count, rate=head_rates[task])
        loss, head_back = jax.vjp(loss_fn, grid, heads_f[:, task], gain_heads[task].astype(jnp.float32), bias_heads[task].astype(jnp.float32), class_f[task], b_class[task].astype(jnp.float32))
        grads = head_back(jnp.ones((), jnp.float32))
        task_grads.append(grads[0])
        head_parts.append(grads[1:])
    gram = jnp.stack([jnp.stack([jnp.sum(first * second) for second in task_grads]) for first in task_grads])
    task_weights = task_scales(gram)
    combined = task_weights[0] * task_grads[0]
    for task in range(1, TASKS):
        combined = combined + task_weights[task] * task_grads[task]
    block_grads = block_back(combined)
    grad_heads = jnp.stack([part[0] for part in head_parts], axis=1)
    grad_gain_heads = jnp.stack([part[1] for part in head_parts])
    grad_bias_heads = jnp.stack([part[2] for part in head_parts])
    grad_class = jnp.stack([part[3] for part in head_parts])
    grad_class_bias = jnp.stack([part[4] for part in head_parts])
    return (block_grads[0], block_grads[1], block_grads[4], block_grads[7], grad_heads, block_grads[2], block_grads[3], block_grads[5], block_grads[6], block_grads[8], block_grads[9], grad_gain_heads, grad_bias_heads, grad_class, grad_class_bias, task_weights)
```

```python
import itertools

import jax
import jax.numpy as jnp
import numpy as np
from jax import lax
from jax.sharding import Mesh
from jax.sharding import PartitionSpec as P

W_UNIT = 12


eps = 1e-05
mid_rate = 2
head_rates = (12, 24, 36)
AXES = ("z", "y", "x", "c")
LINE = ("z", "y")
low = jnp.bfloat16
full = jnp.float32


def coords(names):
    return list(itertools.product(*[range(lax.axis_size(name)) for name in names]))


def flip(value, moves):
    moves = sorted(moves, key=lambda move: AXES.index(move[0]))
    names = tuple(name for name, _ in moves)
    places = coords(names)
    index = {place: i for i, place in enumerate(places)}
    pairs = [
        (i, index[tuple(at ^ bit for at, (_, bit) in zip(place, moves))])
        for i, place in enumerate(places)
    ]
    return lax.ppermute(value, names, pairs)


def all_sum(value):
    moves = []
    for name in ("y", "x", "z"):
        bit = 1
        while bit < lax.axis_size(name):
            moves.append((name, bit))
            bit *= 2
    value = value + flip(value, [("c", 1)])
    while moves:
        if len(moves) == 1:
            value = value + flip(value, moves)
            break
        first, second = moves[:2]
        moves = moves[2:]
        both = [(first[0], first[1] | second[1])] if first[0] == second[0] else [first, second]
        one, two, three = flip(value, [first]), flip(value, [second]), flip(value, both)
        value = (value + one) + (two + three)
    return value


def rows_to(value, pairs):
    if not pairs:
        return jnp.zeros_like(value)
    return lax.ppermute(value, LINE, pairs)


def line_size():
    return lax.axis_size("z") * lax.axis_size("y")


def half_of(value, axis, core):
    size = value.shape[axis] // 2
    return lax.dynamic_slice_in_dim(value, core * size, size, axis=axis)


def both_halves(mine, other, core, axis):
    first = jnp.where(core == 0, mine, other)
    second = jnp.where(core == 0, other, mine)
    return jnp.stack([first, second], axis=axis)


def gather_rows(shard, axis):
    core = lax.axis_index("c")
    mine = lax.all_gather(half_of(shard, axis, core), LINE, axis=0, tiled=False)
    other = flip(mine, [("c", 1)])
    return both_halves(mine, other, core, axis + 1)


def scatter_rows(partial, axis):
    core = lax.axis_index("c")
    mine = half_of(partial, axis + 1, core)
    other = flip(half_of(partial, axis + 1, 1 - core), [("c", 1)])
    summed = (mine.astype(full) + other.astype(full)).astype(low)
    own = lax.psum_scatter(summed, LINE, scatter_dimension=0, tiled=False)
    bit = 1
    while bit < lax.axis_size("x"):
        own = (own.astype(full) + flip(own, [("x", bit)]).astype(full)).astype(low)
        bit *= 2
    other = flip(own, [("c", 1)])
    whole = both_halves(own, other, core, axis)
    return whole.reshape(own.shape[:axis] + (-1,) + own.shape[axis + 1 :]).astype(full)


def along(value, offset, axis):
    size = value.shape[axis]
    if offset == 0:
        return value
    widths = [(0, 0)] * value.ndim
    if offset > 0:
        widths[axis] = (0, offset)
        return lax.slice_in_dim(jnp.pad(value, widths), offset, offset + size, axis=axis)
    widths[axis] = (-offset, 0)
    return lax.slice_in_dim(jnp.pad(value, widths), 0, size, axis=axis)


def crop_table(crop_scale, crop_group, group, unit, cols):
    mine = (crop_group == group).astype(jnp.int32)
    widths = crop_scale * unit * mine
    ends = jnp.cumsum(widths)
    starts = ends - widths
    column = jnp.arange(cols, dtype=jnp.int32)[:, None]
    return ((column >= starts[None, :]) & (column < ends[None, :])).astype(full)


def silu_slope(value):
    sigma = jax.nn.sigmoid(value)
    return sigma * (1.0 + value * (1.0 - sigma))


def norm_scale(value, count):
    sums = all_sum(jnp.stack([jnp.sum(value, axis=0), jnp.sum(value * value, axis=0)]))
    mean = sums[0] / count
    return mean, lax.rsqrt(sums[1] / count - mean * mean + eps)


def head_plan(rows):
    line = line_size()
    terms = []
    for task, rate in enumerate(head_rates):
        hop = rate // rows
        for side in (-1, 1):
            if hop < line:
                terms.append((task, side, hop))
    last = lax.axis_size("y")
    planes = []
    for z in range(lax.axis_size("z")):
        need = []
        for e, (task, side, hop) in enumerate(terms):
            if any(0 <= z * last + y - side * hop < line for y in range(last)):
                need.append(e)
        planes.append(need)
    slots = max(len(need) for need in planes)
    table = np.zeros((slots, line), np.int32)
    for z, need in enumerate(planes):
        rest = [e for e in range(len(terms)) if e not in need]
        for s, e in enumerate((need + rest)[:slots]):
            table[s, z * last : (z + 1) * last] = e
    return terms, table


def task_scales(gram):
    norms = jnp.sqrt(jnp.stack([gram[0, 0], gram[1, 1], gram[2, 2]]) + 1e-12)
    corr = gram / (norms[:, None] * norms[None, :]) + 0.1 * jnp.eye(3, dtype=full)
    adjugate = jnp.stack(
        [
            jnp.cross(corr[:, 1], corr[:, 2]),
            jnp.cross(corr[:, 2], corr[:, 0]),
            jnp.cross(corr[:, 0], corr[:, 1]),
        ]
    )
    weights = jnp.sum(adjugate, axis=1)
    return 3.0 * weights * jnp.mean(norms) / (norms * jnp.sum(weights))


def dot(a, b):
    return jnp.dot(a, b, preferred_element_type=full)


def dot_nt(a, b):
    return lax.dot_general(a, b, (((1,), (1,)), ((), ())), preferred_element_type=full)


def dot_tn(a, b):
    return lax.dot_general(a, b, (((0,), (0,)), ((), ())), preferred_element_type=full)


def on_device(
    features,
    crop_scale,
    crop_group,
    labels,
    w_reduce,
    gain_reduce,
    bias_reduce,
    w_middle,
    gain_middle,
    bias_middle,
    w_expand,
    gain_expand,
    bias_expand,
    w_heads,
    gain_heads,
    bias_heads,
    w_class,
    b_class,
):
    rows = features.shape[1]
    cols = features.shape[2]
    depth = features.shape[3]
    width = w_reduce.shape[1]
    tasks = w_heads.shape[1]
    head = w_heads.shape[3]
    own = w_heads.shape[0]
    classes = w_class.shape[2]
    pixels = rows * cols
    line = line_size()
    place = lax.axis_index(LINE)
    group = lax.axis_index(("x", "c"))
    inside = crop_table(crop_scale, crop_group, group, W_UNIT, cols)

    def same(offset):
        return jnp.tile(jnp.sum(inside * along(inside, offset, 0), axis=1), rows)[:, None]

    valid = same(0)
    count = jnp.sum(crop_scale).astype(full) * float(W_UNIT * rows * line)
    crops = float(crop_scale.shape[0])

    red_all = gather_rows(w_reduce, 0).reshape(depth, width)
    mid_own = w_middle.reshape(-1, 3, 3, width).transpose(1, 0, 2, 3).reshape(3, -1, 3 * width)
    mid_all = gather_rows(mid_own, 1)
    mid_all = mid_all.transpose(1, 0, 2, 3, 4).reshape(3 * width, 3 * width)
    exp_all = gather_rows(w_expand, 0).reshape(width, depth)
    terms, table = head_plan(rows)
    slots = table.shape[0]
    by_term = w_heads.reshape(own, tasks, 3, 3, head).transpose(1, 2, 0, 3, 4)
    by_term = by_term.reshape(tasks, 3, own, 3 * head)
    parts = [by_term[t, 1] for t in range(tasks)] + [by_term[t, s + 1] for t, s, _ in terms]
    heads_all = gather_rows(jnp.stack(parts), 1)
    heads_all = heads_all.transpose(1, 0, 2, 3, 4).reshape(len(parts), depth, 3 * head)
    picked_term = [jnp.asarray(table[s])[place] for s in range(slots)]

    def slot_weight(s):
        if (table[s] == table[s][0]).all():
            return heads_all[tasks + int(table[s][0])]
        return lax.dynamic_index_in_dim(heads_all, tasks + picked_term[s], 0, keepdims=False)

    source = features.reshape(pixels, depth) * valid.astype(low)
    reduced = dot(source, red_all)
    mean1, scale1 = norm_scale(reduced, count)
    normed1 = (reduced - mean1) * scale1
    out1 = normed1 * gain_reduce + bias_reduce
    hidden1 = (jax.nn.silu(out1) * valid).astype(low)
    edge = mid_rate * cols
    down = [(i, i + 1) for i in range(line - 1)]
    up = [(i + 1, i) for i in range(line - 1)]
    before1 = rows_to(hidden1[pixels - edge :], down)
    after1 = rows_to(hidden1[:edge], up)
    tall = jnp.concatenate([before1, hidden1, after1], axis=0)
    wide1 = jnp.concatenate([tall[i * edge : i * edge + pixels] for i in range(3)], axis=1)
    spread = dot(wide1, mid_all)
    mid_masks = [same((k - 1) * mid_rate) for k in range(3)]
    middled = sum(
        along(spread[:, k * width : (k + 1) * width], (k - 1) * mid_rate, 0) * mid_masks[k]
        for k in range(3)
    )
    mean2, scale2 = norm_scale(middled, count)
    normed2 = (middled - mean2) * scale2
    out2 = normed2 * gain_middle + bias_middle
    hidden2 = (jax.nn.silu(out2) * valid).astype(low)
    expanded = dot(hidden2, exp_all)
    mean3, scale3 = norm_scale(expanded, count)
    normed3 = (expanded - mean3) * scale3
    before = normed3 * gain_expand + bias_expand + source.astype(full)
    grid = (jax.nn.silu(before) * valid).astype(low)

    masks = [[same((k - 1) * rate) for k in range(3)] for rate in head_rates]

    def gathered(spread, task):
        rate = head_rates[task]
        return sum(
            along(spread[:, k * head : (k + 1) * head], (k - 1) * rate, 0) * masks[task][k]
            for k in range(3)
        )

    def choose(s, by_task):
        tasks_of = [terms[e][0] for e in table[s]]
        chosen = by_task(tasks_of[0])
        for task in sorted(set(tasks_of) - {tasks_of[0]}):
            here = jnp.asarray(np.array([t == task for t in tasks_of]))[place]
            chosen = jnp.where(here, by_task(task), chosen)
        return chosen

    side_terms = []
    for s in range(slots):
        spread = dot(grid, slot_weight(s))
        side_terms.append(choose(s, lambda task: gathered(spread, task)).astype(low))
    moved = [None] * tasks
    for e, (task, side, hop) in enumerate(terms):
        pairs = [(f, f - side * hop) for f in range(line) if 0 <= f - side * hop < line]
        using = [s for s in range(slots) if any(table[s, f] == e for f, _ in pairs)]
        sent = side_terms[using[0]]
        for s in using[1:]:
            sent = jnp.where(picked_term[s] == e, side_terms[s], sent)
        got = rows_to(sent, pairs).astype(full)
        moved[task] = got if moved[task] is None else moved[task] + got
    mixed = []
    for task in range(tasks):
        center = gathered(dot(grid, heads_all[task]), task)
        mixed.append(center if moved[task] is None else center + moved[task])
    mixed = jnp.concatenate(mixed, axis=1)
    gain_h, bias_h = gain_heads.reshape(-1), bias_heads.reshape(-1)
    mean_h, scale_h = norm_scale(mixed, count)
    normed_h = (mixed - mean_h) * scale_h
    out_h = normed_h * gain_h + bias_h
    activ = (jax.nn.silu(out_h) * valid).astype(low)
    marks = labels.reshape(tasks, pixels)
    class_part, class_bias_part, dactiv = [], [], []
    for task in range(tasks):
        act = activ[:, task * head : (task + 1) * head]
        logits = dot(act, w_class[task]) + b_class[task]
        onehot = (marks[task][:, None] == jnp.arange(classes, dtype=jnp.int32)[None, :]).astype(full)
        dlogits = ((jax.nn.softmax(logits, axis=-1) - onehot) * valid / crops).astype(low)
        class_part.append(dot_tn(act, dlogits))
        class_bias_part.append(jnp.sum(dlogits.astype(full), axis=0))
        dactiv.append(dot_nt(dlogits, w_class[task]))
    dout_h = jnp.concatenate(dactiv, axis=1) * valid * silu_slope(out_h)
    sums_h = all_sum(jnp.stack([jnp.sum(dout_h * normed_h, axis=0), jnp.sum(dout_h, axis=0)]))
    dgain_h, dbias_h = sums_h[0], sums_h[1]
    dmixed = valid * (gain_h * scale_h) * (dout_h - dbias_h / count - normed_h * (dgain_h / count))
    dmixed = dmixed.astype(low)

    def spread_back(grad, task):
        rate = head_rates[task]
        return jnp.concatenate(
            [along(grad * masks[task][k].astype(low), -(k - 1) * rate, 0) for k in range(3)], axis=1
        )

    back = []
    for task, side, hop in terms:
        pairs = [(f, f + side * hop) for f in range(line) if 0 <= f + side * hop < line]
        back.append(rows_to(dmixed[:, task * head : (task + 1) * head], pairs))
    shared_grads, head_parts = [], [None] * len(parts)
    for task in range(tasks):
        dspread = spread_back(dmixed[:, task * head : (task + 1) * head], task)
        shared_grads.append(dot_nt(dspread, heads_all[task]))
        head_parts[task] = dot_tn(grid, dspread).astype(low)
    for s in range(slots):
        dside = back[table[s][0]]
        for e in sorted(set(table[s].tolist()) - {int(table[s][0])}):
            dside = jnp.where(picked_term[s] == e, back[e], dside)
        dspread = choose(s, lambda task: spread_back(dside, task))
        dshared = dot_nt(dspread, slot_weight(s))
        dweight = dot_tn(grid, dspread).astype(low)
        tasks_of = np.array([terms[e][0] for e in table[s]])
        for task in sorted(set(tasks_of.tolist())):
            here = jnp.asarray((tasks_of == task).astype(np.float32))[place]
            shared_grads[task] = shared_grads[task] + here * dshared
        for e in sorted(set(table[s].tolist())):
            here = jnp.asarray((table[s] == e).astype(np.float32))[place].astype(low)
            part = here * dweight
            held = head_parts[tasks + e]
            head_parts[tasks + e] = part if held is None else held + part
    slope3 = valid * silu_slope(before)
    sums = []
    for task in range(tasks):
        part = shared_grads[task] * slope3
        sums += [jnp.sum(part * normed3, axis=0), jnp.sum(part, axis=0)]
    gram_part = jnp.stack(
        [jnp.sum(shared_grads[t] * shared_grads[u]) for t in range(tasks) for u in range(tasks)]
    )
    class_part = jnp.stack(class_part).reshape(-1)
    class_bias_part = jnp.stack(class_bias_part).reshape(-1)
    small = jnp.concatenate([class_part, class_bias_part, gram_part])
    short = -small.shape[0] % depth
    small = jnp.pad(small, (0, short)).reshape(-1, depth)
    summed = all_sum(jnp.concatenate([jnp.stack(sums), small], axis=0))
    sums3 = summed[: 2 * tasks].reshape(tasks, 2, depth)
    small = summed[2 * tasks :].reshape(-1)
    size = tasks * head * classes
    grad_class = small[:size].reshape(tasks, head, classes)
    grad_class_bias = small[size : size + tasks * classes].reshape(tasks, classes)
    gram = small[size + tasks * classes :][: tasks * tasks].reshape(tasks, tasks)
    task_weights = task_scales(gram)
    head_full = jnp.stack(head_parts).reshape(len(parts), line, own, 3 * head).transpose(1, 0, 2, 3)
    head_own = scatter_rows(head_full, 1)

    combined = sum(task_weights[t] * shared_grads[t] for t in range(tasks))
    dgain3, dbias3 = (
        sum(task_weights[t] * sums3[t, j] for t in range(tasks)) for j in range(2)
    )
    dbefore = combined * slope3
    dexpanded = valid * (gain_expand * scale3) * (
        dbefore - dbias3 / count - normed3 * (dgain3 / count)
    )
    dexpanded = dexpanded.astype(low)
    dhidden2 = dot_nt(dexpanded, exp_all)
    dout2 = dhidden2 * valid * silu_slope(out2)
    sums2 = all_sum(jnp.stack([jnp.sum(dout2 * normed2, axis=0), jnp.sum(dout2, axis=0)]))
    dgain2, dbias2 = sums2[0], sums2[1]
    exp_own = scatter_rows(dot_tn(hidden2, dexpanded).astype(low).reshape(line, -1, depth), 0)
    dmiddled = valid * (gain_middle * scale2) * (
        dout2 - dbias2 / count - normed2 * (dgain2 / count)
    )
    dmiddled = dmiddled.astype(low)
    dspread = jnp.concatenate(
        [along(dmiddled * mid_masks[k].astype(low), -(k - 1) * mid_rate, 0) for k in range(3)],
        axis=1,
    )
    dwide = dot_nt(dspread, mid_all)
    from_below = rows_to(dwide[:edge, :width].astype(low), up).astype(full)
    from_above = rows_to(dwide[pixels - edge :, 2 * width :].astype(low), down).astype(full)
    dhidden1 = (
        dwide[:, width : 2 * width]
        + jnp.concatenate([dwide[edge:, :width], from_below], axis=0)
        + jnp.concatenate([from_above, dwide[: pixels - edge, 2 * width :]], axis=0)
    )
    dout1 = dhidden1 * valid * silu_slope(out1)
    sums1 = all_sum(jnp.stack([jnp.sum(dout1 * normed1, axis=0), jnp.sum(dout1, axis=0)]))
    dgain1, dbias1 = sums1[0], sums1[1]
    mid_part = dot_tn(wide1, dspread).astype(low).reshape(3, line, -1, 3 * width)
    mid_sum = scatter_rows(mid_part.transpose(1, 0, 2, 3), 1)
    mid_sum = mid_sum.reshape(3, -1, 3, width).transpose(1, 0, 2, 3).reshape(w_middle.shape)
    dreduced = valid * (gain_reduce * scale1) * (
        dout1 - dbias1 / count - normed1 * (dgain1 / count)
    )
    dreduced = dreduced.astype(low)
    red_own = scatter_rows(dot_tn(source, dreduced).astype(low).reshape(line, -1, width), 0)
    dfeatures = dbefore + dot_nt(dreduced, red_all)

    zero = jnp.zeros((own, 3 * head), full)
    ordered = [[zero, head_own[t], zero] for t in range(tasks)]
    for e, (task, side, _) in enumerate(terms):
        ordered[task][side + 1] = head_own[tasks + e]
    heads_out = jnp.stack([part for row in ordered for part in row])
    heads_out = heads_out.reshape(tasks, 3, own, 3, head).transpose(2, 0, 1, 3, 4)
    return (
        dfeatures.reshape(1, rows, cols, depth),
        red_own,
        mid_sum,
        exp_own,
        heads_out.reshape(w_heads.shape),
        dgain1,
        dbias1,
        dgain2,
        dbias2,
        dgain3,
        dbias3,
        dgain_h.reshape(tasks, head),
        dbias_h.reshape(tasks, head),
        grad_class,
        grad_class_bias,
        task_weights,
    )


def solution(mesh):
    line, groups = mesh.shape["fsdp"], mesh.shape["dp"]
    fine = Mesh(mesh.devices.reshape(line // 2, 2, groups // 2, 2), AXES)
    dp = ("x", "c")
    rows = P(LINE)
    in_specs = (
        P(dp, LINE, None, None),
        P(),
        P(),
        P(None, dp, LINE, None),
        rows,
        P(),
        P(),
        rows,
        P(),
        P(),
        rows,
        P(),
        P(),
        rows,
        P(),
        P(),
        P(),
        P(),
    )
    out_specs = (P(dp, LINE, None, None),) + (rows,) * 4 + (P(),) * 11
    return jax.shard_map(
        on_device, mesh=fine, in_specs=in_specs, out_specs=out_specs, check_vma=False
    )
```

```python
import itertools

import jax
import jax.numpy as jnp
import numpy as np
from jax import lax
from jax.experimental import pallas as pl
from jax.experimental.pallas import tpu as pltpu
from jax.sharding import Mesh
from jax.sharding import PartitionSpec as P

W_UNIT = 12


eps = 1e-05
mid_rate = 2
head_rates = (12, 24, 36)
AXES = ("z", "y", "x", "c")
LINE = ("z", "y")
low = jnp.bfloat16
full = jnp.float32


def coords(names):
    return list(itertools.product(*[range(lax.axis_size(name)) for name in names]))


def flip(value, moves):
    moves = sorted(moves, key=lambda move: AXES.index(move[0]))
    names = tuple(name for name, _ in moves)
    places = coords(names)
    index = {place: i for i, place in enumerate(places)}
    pairs = [
        (i, index[tuple(at ^ bit for at, (_, bit) in zip(place, moves))])
        for i, place in enumerate(places)
    ]
    return lax.ppermute(value, names, pairs)


def all_sum(value):
    moves = []
    for name in ("y", "x", "z"):
        bit = 1
        while bit < lax.axis_size(name):
            moves.append((name, bit))
            bit *= 2
    value = value + flip(value, [("c", 1)])
    while moves:
        if len(moves) == 1:
            value = value + flip(value, moves)
            break
        first, second = moves[:2]
        moves = moves[2:]
        both = [(first[0], first[1] | second[1])] if first[0] == second[0] else [first, second]
        one, two, three = flip(value, [first]), flip(value, [second]), flip(value, both)
        value = (value + one) + (two + three)
    return value


def rows_to(value, pairs):
    if not pairs:
        return jnp.zeros_like(value)
    return lax.ppermute(value, LINE, pairs)


def line_size():
    return lax.axis_size("z") * lax.axis_size("y")


def half_of(value, axis, core):
    size = value.shape[axis] // 2
    return lax.dynamic_slice_in_dim(value, core * size, size, axis=axis)


def both_halves(mine, other, core, axis):
    first = jnp.where(core == 0, mine, other)
    second = jnp.where(core == 0, other, mine)
    return jnp.stack([first, second], axis=axis)


def between_cores(partial):
    core = lax.axis_index("c")
    mine = half_of(partial, 1, core)
    other = flip(half_of(partial, 1, 1 - core), [("c", 1)])
    return (mine.astype(full) + other.astype(full)).astype(low)


def over_groups(own):
    bit = 1
    while bit < lax.axis_size("x"):
        own = (own.astype(full) + flip(own, [("x", bit)]).astype(full)).astype(low)
        bit *= 2
    return own, flip(own, [("c", 1)])


def scatter_halves(summed):
    return over_groups(lax.psum_scatter(summed, LINE, scatter_dimension=0, tiled=False))


def scatter_few(summed):
    arrived = lax.all_to_all(summed, LINE, 0, 0, tiled=True)
    return over_groups(jnp.sum(arrived.astype(full), axis=0).astype(low))


def along(value, offset, axis):
    size = value.shape[axis]
    if offset == 0:
        return value
    widths = [(0, 0)] * value.ndim
    if offset > 0:
        widths[axis] = (0, offset)
        return lax.slice_in_dim(jnp.pad(value, widths), offset, offset + size, axis=axis)
    widths[axis] = (-offset, 0)
    return lax.slice_in_dim(jnp.pad(value, widths), 0, size, axis=axis)


def crop_table(crop_scale, crop_group, group, unit, cols):
    mine = (crop_group == group).astype(jnp.int32)
    widths = crop_scale * unit * mine
    ends = jnp.cumsum(widths)
    starts = ends - widths
    column = jnp.arange(cols, dtype=jnp.int32)[:, None]
    return ((column >= starts[None, :]) & (column < ends[None, :])).astype(full)


def silu_slope(value):
    sigma = jax.nn.sigmoid(value)
    return sigma * (1.0 + value * (1.0 - sigma))


def norm_scale(value, count):
    sums = all_sum(jnp.stack([jnp.sum(value, axis=0), jnp.sum(value * value, axis=0)]))
    mean = sums[0] / count
    return mean, lax.rsqrt(sums[1] / count - mean * mean + eps)


def head_plan(rows):
    line = line_size()
    terms = []
    for task, rate in enumerate(head_rates):
        hop = rate // rows
        for side in (-1, 1):
            if hop < line:
                terms.append((task, side, hop))
    last = lax.axis_size("y")
    planes = []
    for z in range(lax.axis_size("z")):
        need = []
        for e, (task, side, hop) in enumerate(terms):
            if any(0 <= z * last + y - side * hop < line for y in range(last)):
                need.append(e)
        planes.append(need)
    slots = max(len(need) for need in planes)
    table = np.zeros((slots, line), np.int32)
    for z, need in enumerate(planes):
        rest = [e for e in range(len(terms)) if e not in need]
        for s, e in enumerate((need + rest)[:slots]):
            table[s, z * last : (z + 1) * last] = e
    return terms, table


def task_scales(products):
    g00, g01, g02, g11, g12, g22 = products
    n0, n1, n2 = (jnp.sqrt(g + 1e-12) for g in (g00, g11, g22))
    c00, c11, c22 = (g / (n * n) + 0.1 for g, n in ((g00, n0), (g11, n1), (g22, n2)))
    c01, c02, c12 = g01 / (n0 * n1), g02 / (n0 * n2), g12 / (n1 * n2)
    w0 = (c11 * c22 - c12 * c12) + (c12 * c02 - c01 * c22) + (c01 * c12 - c11 * c02)
    w1 = (c12 * c02 - c22 * c01) + (c22 * c00 - c02 * c02) + (c02 * c01 - c12 * c00)
    w2 = (c01 * c12 - c02 * c11) + (c02 * c01 - c00 * c12) + (c00 * c11 - c01 * c01)
    top = n0 + n1 + n2
    total = w0 + w1 + w2
    return [w * top / (n * total) for w, n in ((w0, n0), (w1, n1), (w2, n2))]


def dot(a, b):
    return jnp.dot(a, b, preferred_element_type=full)


def dot_nt(a, b):
    return lax.dot_general(a, b, (((1,), (1,)), ((), ())), preferred_element_type=full)


def dot_tn(a, b):
    return lax.dot_general(a, b, (((0,), (0,)), ((), ())), preferred_element_type=full)


def spec(shape, index):
    return pl.BlockSpec(shape, index)


def params(mib=56):
    return pltpu.CompilerParams(vmem_limit_bytes=mib * 2**20)


def cost(flops, moved):
    return pl.CostEstimate(flops=flops, bytes_accessed=moved, transcendentals=0)


def terms_kernel(picked_ref, task_ref, x_ref, w_ref, mask_ref, out_ref):
    at = pl.program_id(0)
    spread = jnp.dot(x_ref[...], w_ref[...], preferred_element_type=full)
    pixels, head = out_ref.shape
    for task, rate in enumerate(head_rates):

        @pl.when(task_ref[at] == task)
        def _():
            total = spread[:, head : 2 * head]
            for k, shift in ((0, rate), (2, pixels - rate)):
                piece = pltpu.roll(spread[:, k * head : (k + 1) * head], shift, 0)
                total = total + piece * mask_ref[:, 3 * task + k : 3 * task + k + 1]
            out_ref[...] = total.astype(out_ref.dtype)


def head_terms(grid, heads_all, masks, picked, task_of, head, dtype):
    pixels, depth = grid.shape
    items = picked.shape[0]
    return pl.pallas_call(
        terms_kernel,
        out_shape=jax.ShapeDtypeStruct((pixels, items * head), dtype),
        grid_spec=pltpu.PrefetchScalarGridSpec(
            num_scalar_prefetch=2,
            grid=(items,),
            in_specs=[
                spec((pixels, depth), lambda i, p, t: (0, 0)),
                spec((depth, 3 * head), lambda i, p, t: (0, p[i])),
                spec(masks.shape, lambda i, p, t: (0, 0)),
            ],
            out_specs=spec((pixels, head), lambda i, p, t: (0, i)),
        ),
        compiler_params=params(),
        cost_estimate=cost(
            2 * pixels * depth * 3 * head * items, 2 * items * depth * 3 * head + 2 * pixels * depth
        ),
    )(picked, task_of, grid, heads_all, masks)


def spread_kernel(task_ref, d_ref, mask_ref, out_ref):
    at = pl.program_id(0)
    pixels, head = d_ref.shape
    for task, rate in enumerate(head_rates):

        @pl.when(task_ref[at] == task)
        def _():
            grad = d_ref[...].astype(full)
            out_ref[:, head : 2 * head] = d_ref[...]
            for k, shift in ((0, pixels - rate), (2, rate)):
                piece = grad * mask_ref[:, 3 * task + k : 3 * task + k + 1]
                out_ref[:, k * head : (k + 1) * head] = pltpu.roll(piece, shift, 0).astype(low)


def spread_back(grads, masks, task_of, head):
    pixels = grads.shape[0]
    items = grads.shape[1] // head
    return pl.pallas_call(
        spread_kernel,
        out_shape=jax.ShapeDtypeStruct((pixels, 3 * head * items), low),
        grid_spec=pltpu.PrefetchScalarGridSpec(
            num_scalar_prefetch=1,
            grid=(items,),
            in_specs=[
                spec((pixels, head), lambda i, t: (0, i)),
                spec(masks.shape, lambda i, t: (0, 0)),
            ],
            out_specs=spec((pixels, 3 * head), lambda i, t: (0, i)),
        ),
        compiler_params=params(),
        cost_estimate=cost(10 * pixels * head * items * 3, 8 * pixels * head * items),
    )(task_of, grads, masks)


def shared_back_kernel(tasks, side_tasks, *refs):
    slots = len(side_tasks)
    picked_ref, here_ref = refs[:2]
    dy_ref = refs[2]
    w_refs = refs[3 : 3 + tasks + slots]
    wide_ref, source_ref, vec_ref, mask_ref = refs[3 + tasks + slots : 7 + tasks + slots]
    out_refs = refs[7 + tasks + slots : -1]
    sums_ref = refs[-1]
    three = w_refs[0].shape[1]

    def back(i):
        return lax.dot_general(
            dy_ref[:, i * three : (i + 1) * three],
            w_refs[i][...],
            (((1,), (1,)), ((), ())),
            preferred_element_type=full,
        )

    grads = [back(t) for t in range(tasks)]
    for s, choices in enumerate(side_tasks):
        side = back(tasks + s)
        for t in choices:
            grads[t] = grads[t] + (side if len(choices) == 1 else side * here_ref[s * tasks + t])
    normed = (wide_ref[...].astype(full) - vec_ref[0:1]) * vec_ref[1:2]
    value = normed * vec_ref[2:3] + vec_ref[3:4] + source_ref[...].astype(full)
    slope = silu_slope(value) * mask_ref[:, 1:2]
    rows = []
    for t in range(tasks):
        out_refs[t][...] = grads[t].astype(low)
        part = grads[t] * slope
        rows += [jnp.sum(part * normed, axis=0), jnp.sum(part, axis=0)]
    for t in range(tasks):
        for u in range(t, tasks):
            rows.append(jnp.sum(grads[t] * grads[u], axis=0))
    sums_ref[...] = jnp.zeros_like(sums_ref)
    for i, row in enumerate(rows):
        sums_ref[i, :] = row


def shared_back(dys, heads_all, picked, here, side_tasks, tasks, wide, source, vecs, masks, block):
    pixels, depth = wide.shape
    items = tasks + len(side_tasks)
    three = dys.shape[1] // items
    weights = [
        spec((block, three), (lambda j, p, h, i=i: (j, i)) if i < tasks else (lambda j, p, h, i=i: (j, p[i])))
        for i in range(items)
    ]
    column = lambda j, p, h: (0, j)
    return pl.pallas_call(
        lambda *refs: shared_back_kernel(tasks, side_tasks, *refs),
        out_shape=[jax.ShapeDtypeStruct((pixels, depth), low)] * tasks
        + [jax.ShapeDtypeStruct((16, depth), full)],
        grid_spec=pltpu.PrefetchScalarGridSpec(
            num_scalar_prefetch=2,
            grid=(depth // block,),
            in_specs=[spec(dys.shape, lambda j, p, h: (0, 0))]
            + weights
            + [
                spec((pixels, block), column),
                spec((pixels, block), column),
                spec((8, block), column),
                spec(masks.shape, lambda j, p, h: (0, 0)),
            ],
            out_specs=[spec((pixels, block), column)] * tasks + [spec((16, block), column)],
        ),
        compiler_params=params(),
        cost_estimate=cost(
            2 * pixels * depth * three * items, 2 * items * depth * three + 12 * pixels * depth
        ),
    )(picked, here, dys, *([heads_all] * items), wide, source, vecs, masks)


def expand_back_kernel(tasks, blocks, *refs):
    weight_ref = refs[0]
    grad_refs = refs[1 : 1 + tasks]
    wide_ref, source_ref, vec_ref, mask_ref, hidden_ref, w_ref, mid_ref, mid_vec_ref = refs[
        1 + tasks : 9 + tasks
    ]
    dbefore_ref, dweight_ref, dout_ref, sums_ref, total_ref = refs[9 + tasks :]
    at = pl.program_id(0)
    combined = grad_refs[0][...].astype(full) * weight_ref[0]
    for t in range(1, tasks):
        combined = combined + grad_refs[t][...].astype(full) * weight_ref[t]
    normed = (wide_ref[...].astype(full) - vec_ref[0:1]) * vec_ref[1:2]
    value = normed * vec_ref[2:3] + vec_ref[3:4] + source_ref[...].astype(full)
    valid = mask_ref[:, 1:2]
    dbefore = combined * (silu_slope(value) * valid)
    dbefore_ref[...] = dbefore.astype(low)
    dwide = (dbefore - vec_ref[5:6] - normed * vec_ref[4:5]) * vec_ref[6:7] * valid
    dwide = dwide.astype(low)
    dweight_ref[...] = lax.dot_general(
        hidden_ref[...], dwide, (((0,), (0,)), ((), ())), preferred_element_type=full
    ).astype(low)
    part = lax.dot_general(
        dwide, w_ref[...], (((1,), (1,)), ((), ())), preferred_element_type=full
    )

    @pl.when(at == 0)
    def _():
        total_ref[...] = part

    @pl.when(at > 0)
    def _():
        total_ref[...] += part

    @pl.when(at == blocks - 1)
    def _():
        mid = (mid_ref[...] - mid_vec_ref[0:1]) * mid_vec_ref[1:2]
        dout = total_ref[...] * silu_slope(mid * mid_vec_ref[2:3] + mid_vec_ref[3:4]) * valid
        dout_ref[...] = dout
        sums_ref[...] = jnp.zeros_like(sums_ref)
        sums_ref[0, :] = jnp.sum(dout * mid, axis=0)
        sums_ref[1, :] = jnp.sum(dout, axis=0)


def expand_back(task_weights, grads, wide, source, vecs, masks, hidden, weight, mid, mid_vecs, block):
    pixels, depth = wide.shape
    width = hidden.shape[1]
    tasks = len(grads)
    column = lambda j, w: (0, j)
    fixed = lambda j, w: (0, 0)
    blocks = depth // block
    return pl.pallas_call(
        lambda *refs: expand_back_kernel(tasks, blocks, *refs),
        out_shape=[
            jax.ShapeDtypeStruct((pixels, depth), low),
            jax.ShapeDtypeStruct((width, depth), low),
            jax.ShapeDtypeStruct((pixels, width), full),
            jax.ShapeDtypeStruct((8, width), full),
        ],
        grid_spec=pltpu.PrefetchScalarGridSpec(
            num_scalar_prefetch=1,
            grid=(blocks,),
            in_specs=[spec((pixels, block), column)] * (tasks + 2)
            + [
                spec((8, block), column),
                spec(masks.shape, fixed),
                spec((pixels, width), fixed),
                spec((width, block), column),
                spec((pixels, width), fixed),
                spec((8, width), fixed),
            ],
            out_specs=[
                spec((pixels, block), column),
                spec((width, block), column),
                spec((pixels, width), fixed),
                spec((8, width), fixed),
            ],
            scratch_shapes=[pltpu.VMEM((pixels, width), full)],
        ),
        compiler_params=params(),
        cost_estimate=cost(4 * pixels * depth * width, 14 * pixels * depth),
    )(task_weights, *grads, wide, source, vecs, masks, hidden, weight, mid, mid_vecs)


def weight_grad_kernel(slot_ref, x_ref, other_ref, dy_ref, dy_other_ref, out_ref, turned_ref):
    at = pl.program_id(0)
    pixels = x_ref.shape[0]

    @pl.when(at == 0)
    def _():
        turned_ref[:, :pixels] = x_ref[...].T
        turned_ref[:, pixels:] = other_ref[...].T

    @pl.when(slot_ref[at] >= 0)
    def _():
        total = jnp.dot(turned_ref[:, :pixels], dy_ref[...], preferred_element_type=full)
        total += jnp.dot(turned_ref[:, pixels:], dy_other_ref[...], preferred_element_type=full)
        out_ref[...] = total.astype(low)

    @pl.when(slot_ref[at] < 0)
    def _():
        out_ref[...] = jnp.zeros_like(out_ref)


def weight_grad(x, other, dys, dys_other, slot_of, three):
    pixels, depth = x.shape
    parts = slot_of.shape[0]
    fixed = lambda g, s: (0, 0)
    picked = lambda g, s: (0, jnp.maximum(s[g], 0))
    return pl.pallas_call(
        weight_grad_kernel,
        out_shape=jax.ShapeDtypeStruct((depth, parts * three), low),
        grid_spec=pltpu.PrefetchScalarGridSpec(
            num_scalar_prefetch=1,
            grid=(parts,),
            in_specs=[
                spec(x.shape, fixed),
                spec(other.shape, fixed),
                spec((pixels, three), picked),
                spec((pixels, three), picked),
            ],
            out_specs=spec((depth, three), lambda g, s: (0, g)),
            scratch_shapes=[pltpu.VMEM((depth, 2 * pixels), low)],
        ),
        compiler_params=params(),
        cost_estimate=cost(
            4 * pixels * depth * dys.shape[1], 2 * depth * parts * three + 4 * pixels * dys.shape[1]
        ),
    )(slot_of, x, other, dys, dys_other)


def place_kernel(part_ref, core_ref, mine_ref, other_ref, out_ref):
    at = pl.program_id(0)
    half = mine_ref.shape[0]

    @pl.when(part_ref[at] >= 0)
    def _():
        core = core_ref[0]
        out_ref[0, pl.ds(pl.multiple_of(core * half, half), half), :] = mine_ref[...].astype(full)
        out_ref[0, pl.ds(pl.multiple_of((1 - core) * half, half), half), :] = other_ref[
            ...
        ].astype(full)

    @pl.when(part_ref[at] < 0)
    def _():
        out_ref[...] = jnp.zeros_like(out_ref)


def place_rows(mine, other, part_of, core, head):
    half = mine.shape[0]
    taps = part_of.shape[0]
    picked = lambda i, p, c: (0, jnp.maximum(p[i], 0))
    return pl.pallas_call(
        place_kernel,
        out_shape=jax.ShapeDtypeStruct((taps, 2 * half, head), full),
        grid_spec=pltpu.PrefetchScalarGridSpec(
            num_scalar_prefetch=2,
            grid=(taps,),
            in_specs=[spec((half, head), picked), spec((half, head), picked)],
            out_specs=spec((1, 2 * half, head), lambda i, p, c: (i, 0, 0)),
        ),
        compiler_params=params(),
        cost_estimate=cost(0, 12 * taps * half * head),
    )(part_of, core, mine, other)


def on_device(
    features,
    crop_scale,
    crop_group,
    labels,
    w_reduce,
    gain_reduce,
    bias_reduce,
    w_middle,
    gain_middle,
    bias_middle,
    w_expand,
    gain_expand,
    bias_expand,
    w_heads,
    gain_heads,
    bias_heads,
    w_class,
    b_class,
):
    rows = features.shape[1]
    cols = features.shape[2]
    depth = features.shape[3]
    width = w_reduce.shape[1]
    tasks = w_heads.shape[1]
    head = w_heads.shape[3]
    own = w_heads.shape[0]
    classes = w_class.shape[2]
    pixels = rows * cols
    line = line_size()
    place = lax.axis_index(LINE)
    group = lax.axis_index(("x", "c"))
    inside = crop_table(crop_scale, crop_group, group, W_UNIT, cols)

    def same(offset):
        return jnp.tile(jnp.sum(inside * along(inside, offset, 0), axis=1), rows)[:, None]

    valid = same(0)
    count = jnp.sum(crop_scale).astype(full) * float(W_UNIT * rows * line)
    crops = float(crop_scale.shape[0])

    core = lax.axis_index("c")
    ratio = depth // width
    red_rows, mid_rows, exp_rows = (w.shape[0] // 2 for w in (w_reduce, w_middle, w_expand))
    mid_own = half_of(w_middle.transpose(1, 0, 2), 1, core).reshape(9 * mid_rows, width)
    exp_own = half_of(w_expand, 0, core).reshape(exp_rows, ratio, width).transpose(1, 0, 2)
    block_own = jnp.concatenate(
        [half_of(w_reduce, 0, core), mid_own, exp_own.reshape(ratio * exp_rows, width)], axis=0
    )
    block_mine = lax.all_gather(block_own, LINE, axis=0, tiled=False)
    block_all = both_halves(block_mine, flip(block_mine, [("c", 1)]), core, 1)
    cuts = np.cumsum([0, red_rows, 9 * mid_rows, ratio * exp_rows])
    red_all, mid_all, exp_all = (block_all[:, :, cuts[i] : cuts[i + 1]] for i in range(3))
    red_all = red_all.reshape(depth, width)
    mid_all = mid_all.reshape(line, 2, 3, 3, mid_rows, width).transpose(2, 0, 1, 4, 3, 5)
    mid_all = mid_all.reshape(3 * width, 3 * width)
    exp_all = exp_all.reshape(line, 2, ratio, exp_rows, width).transpose(0, 1, 3, 2, 4)
    exp_all = exp_all.reshape(width, depth)
    terms, table = head_plan(rows)
    slots = table.shape[0]
    three = 3 * head
    by_term = w_heads.reshape(own, tasks, 3, 3, head).transpose(1, 2, 0, 3, 4)
    by_term = by_term.reshape(tasks, 3, own, three)
    parts = [by_term[t, 1] for t in range(tasks)] + [by_term[t, s + 1] for t, s, _ in terms]
    quarter = own // lax.axis_size(("x", "c"))
    heads_own = jnp.concatenate(
        [lax.dynamic_slice_in_dim(part, group * quarter, quarter, axis=0) for part in parts], axis=1
    )
    heads_own, block_mine = lax.optimization_barrier((heads_own, block_mine))
    heads_all = lax.all_gather(heads_own, AXES, axis=0, tiled=True)
    term_tasks = np.array([task for task, _, _ in terms], np.int32)
    picked_term = jnp.asarray(table)[:, place]
    slot_tasks = [sorted({int(term_tasks[e]) for e in table[s]}) for s in range(slots)]
    side_task = jnp.asarray(term_tasks)[picked_term]
    centers = jnp.arange(tasks, dtype=jnp.int32)
    all_tasks = jnp.concatenate([centers, side_task])
    all_picked = jnp.concatenate([centers, tasks + picked_term])

    source = features.reshape(pixels, depth) * valid.astype(low)
    reduced = dot(source, red_all)
    mean1, scale1 = norm_scale(reduced, count)
    normed1 = (reduced - mean1) * scale1
    out1 = normed1 * gain_reduce + bias_reduce
    hidden1 = (jax.nn.silu(out1) * valid).astype(low)
    edge = mid_rate * cols
    down = [(i, i + 1) for i in range(line - 1)]
    up = [(i + 1, i) for i in range(line - 1)]
    before1 = rows_to(hidden1[pixels - edge :], down)
    after1 = rows_to(hidden1[:edge], up)
    tall = jnp.concatenate([before1, hidden1, after1], axis=0)
    wide1 = jnp.concatenate([tall[i * edge : i * edge + pixels] for i in range(3)], axis=1)
    spread = dot(wide1, mid_all)
    mid_masks = [same((k - 1) * mid_rate) for k in range(3)]
    middled = sum(
        along(spread[:, k * width : (k + 1) * width], (k - 1) * mid_rate, 0) * mid_masks[k]
        for k in range(3)
    )
    mean2, scale2 = norm_scale(middled, count)
    normed2 = (middled - mean2) * scale2
    out2 = normed2 * gain_middle + bias_middle
    hidden2 = (jax.nn.silu(out2) * valid).astype(low)
    expanded = dot(hidden2, exp_all)
    mean3, scale3 = norm_scale(expanded, count)
    normed3 = (expanded - mean3) * scale3
    before = normed3 * gain_expand + bias_expand + source.astype(full)
    grid = (jax.nn.silu(before) * valid).astype(low)

    def mask_table(group):
        inside = crop_table(crop_scale, crop_group, group, W_UNIT, cols)
        columns = [
            jnp.sum(inside * along(inside, (k - 1) * rate, 0), axis=1)
            for rate in head_rates
            for k in range(3)
        ]
        table = jnp.pad(jnp.stack(columns, axis=1), ((0, 0), (0, 128 - 3 * tasks)))
        return jnp.tile(table, (rows, 1))

    masks = mask_table(group)
    side_terms = head_terms(grid, heads_all, masks, tasks + picked_term, side_task, head, low)
    moved = [None] * tasks
    for e, (task, side, hop) in enumerate(terms):
        pairs = [(f, f - side * hop) for f in range(line) if 0 <= f - side * hop < line]
        using = [s for s in range(slots) if any(table[s, f] == e for f, _ in pairs)]
        sent = side_terms[:, using[0] * head : (using[0] + 1) * head]
        for s in using[1:]:
            sent = jnp.where(picked_term[s] == e, side_terms[:, s * head : (s + 1) * head], sent)
        got = rows_to(sent, pairs).astype(full)
        moved[task] = got if moved[task] is None else moved[task] + got
    middle_terms = head_terms(grid, heads_all, masks, centers, centers, head, full)
    mixed = []
    for task in range(tasks):
        center = middle_terms[:, task * head : (task + 1) * head]
        mixed.append(center if moved[task] is None else center + moved[task])
    mixed = jnp.concatenate(mixed, axis=1)
    gain_h, bias_h = gain_heads.reshape(-1), bias_heads.reshape(-1)
    mean_h, scale_h = norm_scale(mixed, count)
    normed_h = (mixed - mean_h) * scale_h
    out_h = normed_h * gain_h + bias_h
    activ = (jax.nn.silu(out_h) * valid).astype(low)
    marks = labels.reshape(tasks, pixels)
    class_part, class_bias_part, dactiv = [], [], []
    for task in range(tasks):
        act = activ[:, task * head : (task + 1) * head]
        logits = dot(act, w_class[task]) + b_class[task]
        onehot = (marks[task][:, None] == jnp.arange(classes, dtype=jnp.int32)[None, :]).astype(full)
        dlogits = ((jax.nn.softmax(logits, axis=-1) - onehot) * valid / crops).astype(low)
        class_part.append(dot_tn(dlogits, act))
        class_bias_part.append(jnp.sum(dlogits.astype(full), axis=0))
        dactiv.append(dot_nt(dlogits, w_class[task]))
    dout_h = jnp.concatenate(dactiv, axis=1) * valid * silu_slope(out_h)
    sums_h = all_sum(jnp.stack([jnp.sum(dout_h * normed_h, axis=0), jnp.sum(dout_h, axis=0)]))
    dgain_h, dbias_h = sums_h[0], sums_h[1]
    dmixed = valid * (gain_h * scale_h) * (dout_h - dbias_h / count - normed_h * (dgain_h / count))
    dmixed = dmixed.astype(low)

    back = []
    for task, side, hop in terms:
        pairs = [(f, f + side * hop) for f in range(line) if 0 <= f + side * hop < line]
        back.append(rows_to(dmixed[:, task * head : (task + 1) * head], pairs))
    dsides = []
    for s in range(slots):
        dside = back[table[s][0]]
        for e in sorted(set(table[s].tolist()) - {int(table[s][0])}):
            dside = jnp.where(picked_term[s] == e, back[e], dside)
        dsides.append(dside)
    dterms = jnp.concatenate([dmixed] + dsides, axis=1)
    dys = spread_back(dterms, masks, all_tasks, head)
    half = own // 2

    def half_columns(which):
        cuts = [f * own + which * half for f in range(line)]
        return jnp.concatenate(
            [lax.dynamic_slice_in_dim(grid, cut, half, axis=1) for cut in cuts], axis=1
        )

    grid_other = flip(half_columns(1 - core), [("c", 1)])
    dterms_other = flip(dterms, [("c", 1)])
    dys_other = spread_back(dterms_other, mask_table(group ^ 1), all_tasks, head)
    slot_of = jnp.full((len(terms),), -1, jnp.int32)
    for s in range(slots):
        slot_of = jnp.where(jnp.arange(len(terms)) == picked_term[s], tasks + s, slot_of)
    slot_of = jnp.concatenate([centers, slot_of])
    core_at = core.reshape(1).astype(jnp.int32)
    head_half = weight_grad(half_columns(core), grid_other, dys, dys_other, slot_of, three)
    dys, head_half = lax.optimization_barrier((dys, head_half))
    head_own, head_other = scatter_halves(head_half.reshape(line, half, len(parts) * three))

    here = (side_task[:, None] == centers[None, :]).astype(full).reshape(-1)
    vec_rows = [mean3, scale3, gain_expand, bias_expand]
    vecs = jnp.pad(jnp.stack(vec_rows), ((0, 4), (0, 0)))
    *shared_grads, sums = shared_back(
        dys, heads_all, all_picked, here, slot_tasks, tasks, expanded, source, vecs, masks, 256
    )
    gram_part = jnp.sum(sums[2 * tasks : 4 * tasks], axis=1)
    gram_row = jnp.pad(gram_part, (0, depth - gram_part.shape[0]))[None, :]
    summed = all_sum(jnp.concatenate([sums[: 2 * tasks], gram_row], axis=0))
    sums3 = summed[: 2 * tasks].reshape(tasks, 2, depth)
    weight_list = task_scales([summed[2 * tasks, i] for i in range(6)])
    task_weights = jnp.stack(weight_list)

    dgain3, dbias3 = (
        sum(weight_list[t] * sums3[t, j] for t in range(tasks)) for j in range(2)
    )
    vec_rows += [dgain3 / count, dbias3 / count, gain_expand * scale3]
    vecs = jnp.pad(jnp.stack(vec_rows), ((0, 1), (0, 0)))
    mid_vecs = jnp.pad(jnp.stack([mean2, scale2, gain_middle, bias_middle]), ((0, 4), (0, 0)))
    dbefore, exp_part, dout2, sums2 = expand_back(
        task_weights, shared_grads, expanded, source, vecs, masks, hidden2, exp_all, middled,
        mid_vecs, 256,
    )
    sums2 = all_sum(sums2[:2])
    dgain2, dbias2 = sums2[0], sums2[1]
    dmiddled = valid * (gain_middle * scale2) * (
        dout2 - dbias2 / count - normed2 * (dgain2 / count)
    )
    dmiddled = dmiddled.astype(low)
    dspread = jnp.concatenate(
        [along(dmiddled * mid_masks[k].astype(low), -(k - 1) * mid_rate, 0) for k in range(3)],
        axis=1,
    )
    dwide = dot_nt(dspread, mid_all)
    from_below = rows_to(dwide[:edge, :width].astype(low), up).astype(full)
    from_above = rows_to(dwide[pixels - edge :, 2 * width :].astype(low), down).astype(full)
    dhidden1 = (
        dwide[:, width : 2 * width]
        + jnp.concatenate([dwide[edge:, :width], from_below], axis=0)
        + jnp.concatenate([from_above, dwide[: pixels - edge, 2 * width :]], axis=0)
    )
    dout1 = dhidden1 * valid * silu_slope(out1)
    sums1 = all_sum(jnp.stack([jnp.sum(dout1 * normed1, axis=0), jnp.sum(dout1, axis=0)]))
    dgain1, dbias1 = sums1[0], sums1[1]
    class_sums = jnp.concatenate(
        [jnp.concatenate(class_part, axis=0), jnp.pad(jnp.stack(class_bias_part), ((0, 0), (0, head - classes)))],
        axis=0,
    )
    class_sums, sums1 = lax.optimization_barrier((class_sums, sums1))
    class_sums = all_sum(class_sums)
    grad_class = class_sums[: tasks * classes].reshape(tasks, classes, head).transpose(0, 2, 1)
    grad_class_bias = class_sums[tasks * classes :, :classes]
    dreduced = valid * (gain_reduce * scale1) * (
        dout1 - dbias1 / count - normed1 * (dgain1 / count)
    )
    dreduced = dreduced.astype(low)
    dfeatures = dbefore.astype(full) + dot_nt(dreduced, red_all)

    mid_part = dot_tn(wide1, dspread).astype(low).reshape(3, line, -1, 3, width)
    mid_part = mid_part.transpose(1, 2, 0, 3, 4).reshape(line, 2 * mid_rows, 9, width)
    exp_part = exp_part.reshape(line, 2 * exp_rows, ratio, width)
    later = jnp.concatenate([mid_part.reshape(line, 2 * mid_rows, -1, width), exp_part], axis=2)
    later = between_cores(later)
    wide_rows = 9 + ratio
    later_own, later_other = scatter_halves(later.reshape(line, mid_rows * wide_rows, width))
    later_sum = both_halves(later_own, later_other, core, 0).astype(full)
    later_sum = later_sum.reshape(2 * mid_rows, wide_rows, width)
    mid_sum = later_sum[:, :9]
    exp_sum = later_sum[:, 9:].reshape(2 * exp_rows, depth)
    red_part = dot_tn(source, dreduced).astype(low).reshape(line, -1, width)
    red_sum = both_halves(*scatter_few(between_cores(red_part)), core, 0).astype(full)
    part_of = np.full((tasks, 3, 3), -1, np.int32)
    for task in range(tasks):
        part_of[task, 1] = 3 * task + np.arange(3)
    for e, (task, side, _) in enumerate(terms):
        part_of[task, side + 1] = 3 * (tasks + e) + np.arange(3)
    heads_out = place_rows(
        head_own, head_other, jnp.asarray(part_of.reshape(-1)), core_at, head
    )
    heads_out = heads_out.reshape(tasks, 9, own, head).transpose(2, 0, 1, 3)
    return (
        dfeatures.reshape(1, rows, cols, depth),
        red_sum.reshape(w_reduce.shape),
        mid_sum,
        exp_sum,
        heads_out,
        dgain1,
        dbias1,
        dgain2,
        dbias2,
        dgain3,
        dbias3,
        dgain_h.reshape(tasks, head),
        dbias_h.reshape(tasks, head),
        grad_class,
        grad_class_bias,
        task_weights,
    )


def solution(mesh):
    line, groups = mesh.shape["fsdp"], mesh.shape["dp"]
    fine = Mesh(mesh.devices.reshape(line // 2, 2, groups // 2, 2), AXES)
    dp = ("x", "c")
    rows = P(LINE)
    in_specs = (
        P(dp, LINE, None, None),
        P(),
        P(),
        P(None, dp, LINE, None),
        rows,
        P(),
        P(),
        rows,
        P(),
        P(),
        rows,
        P(),
        P(),
        rows,
        P(),
        P(),
        P(),
        P(),
    )
    out_specs = (P(dp, LINE, None, None),) + (rows,) * 4 + (P(),) * 11
    return jax.shard_map(
        on_device, mesh=fine, in_specs=in_specs, out_specs=out_specs, check_vma=False
    )
```

```python
import itertools

import jax
import jax.numpy as jnp
import numpy as np
from jax import lax
from jax.experimental import pallas as pl
from jax.experimental.pallas import tpu as pltpu
from jax.sharding import Mesh
from jax.sharding import PartitionSpec as P

W_UNIT = 12


eps = 1e-05
mid_rate = 2
head_rates = (12, 24, 36)
AXES = ("z", "y", "x", "c")
LINE = ("z", "y")
low = jnp.bfloat16
full = jnp.float32


def coords(names):
    return list(itertools.product(*[range(lax.axis_size(name)) for name in names]))


def flip(value, moves):
    moves = sorted([m for m in moves if m[1]], key=lambda move: AXES.index(move[0]))
    names = tuple(name for name, _ in moves)
    places = coords(names)
    index = {place: i for i, place in enumerate(places)}
    pairs = [
        (i, index[tuple(at ^ bit for at, (_, bit) in zip(place, moves))])
        for i, place in enumerate(places)
    ]
    return lax.ppermute(value, names, pairs)


def all_sum(value):
    moves = []
    for name in ("y", "x", "z"):
        bit = 1
        while bit < lax.axis_size(name):
            moves.append((name, bit))
            bit *= 2
    value = value + flip(value, [("c", 1)])
    while moves:
        if len(moves) == 1:
            value = value + flip(value, moves)
            break
        first, second = moves[:2]
        moves = moves[2:]
        both = [(first[0], first[1] | second[1])] if first[0] == second[0] else [first, second]
        one, two, three = flip(value, [first]), flip(value, [second]), flip(value, both)
        value = (value + one) + (two + three)
    return value


def sum_along(value, name):
    bit = 1
    while bit < lax.axis_size(name):
        value = value + flip(value, [(name, bit)])
        bit *= 2
    return value


def rows_to(value, pairs):
    if not pairs:
        return jnp.zeros_like(value)
    return lax.ppermute(value, LINE, pairs)


def line_size():
    return lax.axis_size("z") * lax.axis_size("y")


def half_of(value, axis, core):
    size = value.shape[axis] // 2
    return lax.dynamic_slice_in_dim(value, core * size, size, axis=axis)


def both_halves(mine, other, core, axis):
    first = jnp.where(core == 0, mine, other)
    second = jnp.where(core == 0, other, mine)
    return jnp.stack([first, second], axis=axis)


def between_cores(partial):
    core = lax.axis_index("c")
    mine = half_of(partial, 1, core)
    other = flip(half_of(partial, 1, 1 - core), [("c", 1)])
    return (mine.astype(full) + other.astype(full)).astype(low)


def over_groups(own):
    bit = 1
    while bit < lax.axis_size("x"):
        own = (own.astype(full) + flip(own, [("x", bit)]).astype(full)).astype(low)
        bit *= 2
    return own, flip(own, [("c", 1)])


def scatter_y(partial):
    parts = partial.reshape(-1, 2, *partial.shape[1:])
    here = lax.axis_index("y")
    mine = lax.dynamic_index_in_dim(parts, here, 1, keepdims=False)
    other = lax.dynamic_index_in_dim(parts, 1 - here, 1, keepdims=False)
    return (mine.astype(full) + flip(other, [("y", 1)]).astype(full)).astype(low)


def scatter_z(parts):
    here = lax.axis_index("z")
    total = lax.dynamic_index_in_dim(parts, here, 0, keepdims=False).astype(full)
    for m in range(1, lax.axis_size("z")):
        part = lax.dynamic_index_in_dim(parts, here ^ m, 0, keepdims=False)
        total = total + flip(part, [("z", m)]).astype(full)
    return total.astype(low)


def along(value, offset, axis):
    size = value.shape[axis]
    if offset == 0:
        return value
    widths = [(0, 0)] * value.ndim
    if offset > 0:
        widths[axis] = (0, offset)
        return lax.slice_in_dim(jnp.pad(value, widths), offset, offset + size, axis=axis)
    widths[axis] = (-offset, 0)
    return lax.slice_in_dim(jnp.pad(value, widths), 0, size, axis=axis)


def crop_table(crop_scale, crop_group, group, unit, cols):
    mine = (crop_group == group).astype(jnp.int32)
    widths = crop_scale * unit * mine
    ends = jnp.cumsum(widths)
    starts = ends - widths
    column = jnp.arange(cols, dtype=jnp.int32)[:, None]
    return ((column >= starts[None, :]) & (column < ends[None, :])).astype(full)


def silu(value):
    return value * (0.5 + 0.5 * jnp.tanh(0.5 * value))


def silu_slope(value):
    turn = jnp.tanh(0.5 * value)
    return 0.5 + 0.5 * turn + 0.25 * value * (1.0 - turn * turn)


def norm_scale(value, count):
    sums = all_sum(jnp.stack([jnp.sum(value, axis=0), jnp.sum(value * value, axis=0)]))
    mean = sums[0] / count
    return mean, lax.rsqrt(sums[1] / count - mean * mean + eps)


def head_plan(rows):
    line = line_size()
    terms = []
    for task, rate in enumerate(head_rates):
        hop = rate // rows
        for side in (-1, 1):
            if hop < line:
                terms.append((task, side, hop))
    last = lax.axis_size("y")
    planes = []
    for z in range(lax.axis_size("z")):
        need = []
        for e, (task, side, hop) in enumerate(terms):
            if any(0 <= z * last + y - side * hop < line for y in range(last)):
                need.append(e)
        planes.append(need)
    slots = max(len(need) for need in planes)
    table = np.zeros((slots, line), np.int32)
    for z, need in enumerate(planes):
        rest = [e for e in range(len(terms)) if e not in need]
        for s, e in enumerate((need + rest)[:slots]):
            table[s, z * last : (z + 1) * last] = e
    return terms, table


def row_moves(terms, line):
    moves = []
    for e, (task, side, hop) in enumerate(terms):
        pairs = [(f, f - side * hop) for f in range(line) if 0 <= f - side * hop < line]
        last = moves[-1] if moves else None
        if last and last[0] == task and not {t for _, t in last[1]} & {t for _, t in pairs}:
            if not {f for f, _ in last[1]} & {f for f, _ in pairs}:
                last[1].extend(pairs)
                last[2].append((e, [f for f, _ in pairs]))
                continue
        moves.append((task, pairs, [(e, [f for f, _ in pairs])]))
    return moves


def task_scales(products):
    g00, g01, g02, g11, g12, g22 = products
    n0, n1, n2 = (jnp.sqrt(g + 1e-12) for g in (g00, g11, g22))
    c00, c11, c22 = (g / (n * n) + 0.1 for g, n in ((g00, n0), (g11, n1), (g22, n2)))
    c01, c02, c12 = g01 / (n0 * n1), g02 / (n0 * n2), g12 / (n1 * n2)
    w0 = (c11 * c22 - c12 * c12) + (c12 * c02 - c01 * c22) + (c01 * c12 - c11 * c02)
    w1 = (c12 * c02 - c22 * c01) + (c22 * c00 - c02 * c02) + (c02 * c01 - c12 * c00)
    w2 = (c01 * c12 - c02 * c11) + (c02 * c01 - c00 * c12) + (c00 * c11 - c01 * c01)
    top = n0 + n1 + n2
    total = w0 + w1 + w2
    return [w * top / (n * total) for w, n in ((w0, n0), (w1, n1), (w2, n2))]


def dot(a, b):
    return jnp.dot(a, b, preferred_element_type=full)


def dot_nt(a, b):
    return lax.dot_general(a, b, (((1,), (1,)), ((), ())), preferred_element_type=full)


def dot_tn(a, b):
    return lax.dot_general(a, b, (((0,), (0,)), ((), ())), preferred_element_type=full)


def spec(shape, index):
    return pl.BlockSpec(shape, index)


def params(mib=56):
    return pltpu.CompilerParams(vmem_limit_bytes=mib * 2**20)


def cost(flops, moved):
    return pl.CostEstimate(flops=flops, bytes_accessed=moved, transcendentals=0)


def terms_kernel(picked_ref, task_ref, x_ref, w_ref, mask_ref, out_ref):
    at = pl.program_id(0)
    pixels, head = out_ref.shape

    def product(k):
        return jnp.dot(
            x_ref[...], w_ref[:, k * head : (k + 1) * head], preferred_element_type=full
        )

    for task, rate in enumerate(head_rates):

        @pl.when(task_ref[at] == task)
        def _():
            left = pltpu.roll(product(0), rate, 0) * mask_ref[:, 3 * task : 3 * task + 1]
            right = pltpu.roll(product(2), pixels - rate, 0)
            right = right * mask_ref[:, 3 * task + 2 : 3 * task + 3]
            out_ref[...] = (product(1) + left + right).astype(out_ref.dtype)


def head_terms(grid, heads_all, masks, picked, task_of, head, dtype):
    pixels, depth = grid.shape
    items = picked.shape[0]
    return pl.pallas_call(
        terms_kernel,
        out_shape=jax.ShapeDtypeStruct((pixels, items * head), dtype),
        grid_spec=pltpu.PrefetchScalarGridSpec(
            num_scalar_prefetch=2,
            grid=(items,),
            in_specs=[
                spec((pixels, depth), lambda i, p, t: (0, 0)),
                spec((depth, 3 * head), lambda i, p, t: (0, p[i])),
                spec(masks.shape, lambda i, p, t: (0, 0)),
            ],
            out_specs=spec((pixels, head), lambda i, p, t: (0, i)),
        ),
        compiler_params=params(),
        cost_estimate=cost(
            2 * pixels * depth * 3 * head * items, 2 * items * depth * 3 * head + 2 * pixels * depth
        ),
    )(picked, task_of, grid, heads_all, masks)


def spread_kernel(task_ref, d_ref, mask_ref, out_ref):
    at = pl.program_id(1)
    pixels, head = d_ref.shape
    for task, rate in enumerate(head_rates):

        @pl.when(task_ref[at] == task)
        def _():
            grad = d_ref[...].astype(full)
            out_ref[:, head : 2 * head] = d_ref[...]
            for k, shift in ((0, pixels - rate), (2, rate)):
                piece = grad * mask_ref[:, 3 * task + k : 3 * task + k + 1]
                out_ref[:, k * head : (k + 1) * head] = pltpu.roll(piece, shift, 0).astype(low)


def spread_back(grads, masks, task_of, head, pixels):
    rows = grads.shape[0]
    items = grads.shape[1] // head
    return pl.pallas_call(
        spread_kernel,
        out_shape=jax.ShapeDtypeStruct((rows, 3 * head * items), low),
        grid_spec=pltpu.PrefetchScalarGridSpec(
            num_scalar_prefetch=1,
            grid=(rows // pixels, items),
            in_specs=[
                spec((pixels, head), lambda j, i, t: (j, i)),
                spec((pixels, masks.shape[1]), lambda j, i, t: (j, 0)),
            ],
            out_specs=spec((pixels, 3 * head), lambda j, i, t: (j, i)),
        ),
        compiler_params=params(),
        cost_estimate=cost(30 * rows * head * items, 8 * rows * head * items),
    )(task_of, grads, masks)


def shared_back_kernel(tasks, side_tasks, *refs):
    slots = len(side_tasks)
    picked_ref, here_ref = refs[:2]
    dy_ref = refs[2]
    w_refs = refs[3 : 3 + tasks + slots]
    wide_ref, source_ref, vec_ref, mask_ref = refs[3 + tasks + slots : 7 + tasks + slots]
    out_refs = refs[7 + tasks + slots : -3]
    slope_ref, normed_ref, sums_ref = refs[-3:]
    three = w_refs[0].shape[1]

    def back(i):
        return lax.dot_general(
            dy_ref[:, i * three : (i + 1) * three],
            w_refs[i][...],
            (((1,), (1,)), ((), ())),
            preferred_element_type=full,
        )

    grads = [back(t) for t in range(tasks)]
    for s, choices in enumerate(side_tasks):
        side = back(tasks + s)
        for t in choices:
            grads[t] = grads[t] + (side if len(choices) == 1 else side * here_ref[s * tasks + t])
    normed = (wide_ref[...].astype(full) - vec_ref[0:1]) * vec_ref[1:2]
    value = normed * vec_ref[2:3] + vec_ref[3:4] + source_ref[...].astype(full)
    slope = silu_slope(value) * mask_ref[:, 1:2]
    slope_ref[...] = slope.astype(low)
    normed_ref[...] = normed.astype(low)
    rows = []
    for t in range(tasks):
        out_refs[t][...] = grads[t].astype(low)
        part = grads[t] * slope
        rows += [jnp.sum(part * normed, axis=0), jnp.sum(part, axis=0)]
    for t in range(tasks):
        for u in range(t, tasks):
            rows.append(jnp.sum(grads[t] * grads[u], axis=0))
    sums_ref[...] = jnp.zeros_like(sums_ref)
    for i, row in enumerate(rows):
        sums_ref[i, :] = row


def shared_back(dys, heads_all, picked, here, side_tasks, tasks, wide, source, vecs, masks, block):
    pixels, depth = wide.shape
    items = tasks + len(side_tasks)
    three = dys.shape[1] // items
    weights = [
        spec((block, three), (lambda j, p, h, i=i: (j, i)) if i < tasks else (lambda j, p, h, i=i: (j, p[i])))
        for i in range(items)
    ]
    column = lambda j, p, h: (0, j)
    return pl.pallas_call(
        lambda *refs: shared_back_kernel(tasks, side_tasks, *refs),
        out_shape=[jax.ShapeDtypeStruct((pixels, depth), low)] * (tasks + 2)
        + [jax.ShapeDtypeStruct((16, depth), full)],
        grid_spec=pltpu.PrefetchScalarGridSpec(
            num_scalar_prefetch=2,
            grid=(depth // block,),
            in_specs=[spec(dys.shape, lambda j, p, h: (0, 0))]
            + weights
            + [
                spec((pixels, block), column),
                spec((pixels, block), column),
                spec((8, block), column),
                spec(masks.shape, lambda j, p, h: (0, 0)),
            ],
            out_specs=[spec((pixels, block), column)] * (tasks + 2) + [spec((16, block), column)],
        ),
        compiler_params=params(),
        cost_estimate=cost(
            2 * pixels * depth * three * items, 2 * items * depth * three + 12 * pixels * depth
        ),
    )(picked, here, dys, *([heads_all] * items), wide, source, vecs, masks)


def expand_back_kernel(tasks, blocks, *refs):
    gram_ref, sum_ref = refs[0], refs[1 + tasks]
    grad_refs = refs[1 : 1 + tasks]
    slope_ref, normed_ref, vec_ref, mask_ref, hidden_ref, w_ref, mid_ref, mid_vec_ref = refs[
        2 + tasks : 10 + tasks
    ]
    dbefore_ref, dweight_ref, dout_ref, sums_ref, total_ref, turned_ref = refs[10 + tasks :]
    at = pl.program_id(0)

    @pl.when(at == 0)
    def _():
        turned_ref[...] = hidden_ref[...].T

    gram = 2 * tasks
    weights = task_scales([gram_ref[gram : gram + 1, i : i + 1] for i in range(6)])
    combined = grad_refs[0][...].astype(full) * weights[0]
    dgain = sum_ref[0:1] * weights[0]
    dbias = sum_ref[1:2] * weights[0]
    for t in range(1, tasks):
        combined = combined + grad_refs[t][...].astype(full) * weights[t]
        dgain = dgain + sum_ref[2 * t : 2 * t + 1] * weights[t]
        dbias = dbias + sum_ref[2 * t + 1 : 2 * t + 2] * weights[t]
    normed = normed_ref[...].astype(full)
    valid = mask_ref[:, 1:2]
    dbefore = combined * slope_ref[...].astype(full)
    dbefore_ref[...] = dbefore.astype(low)
    per = vec_ref[1:2]
    dwide = (dbefore - dbias * per - normed * (dgain * per)) * vec_ref[0:1] * valid
    dwide = dwide.astype(low)
    dweight_ref[...] = jnp.dot(turned_ref[...], dwide, preferred_element_type=full).astype(low)
    part = lax.dot_general(
        dwide, w_ref[...], (((1,), (1,)), ((), ())), preferred_element_type=full
    )

    @pl.when(at == 0)
    def _():
        total_ref[...] = part

    @pl.when(at > 0)
    def _():
        total_ref[...] += part

    @pl.when(at == blocks - 1)
    def _():
        mid = (mid_ref[...] - mid_vec_ref[0:1]) * mid_vec_ref[1:2]
        dout = total_ref[...] * silu_slope(mid * mid_vec_ref[2:3] + mid_vec_ref[3:4]) * valid
        dout_ref[...] = dout
        sums_ref[...] = jnp.zeros_like(sums_ref)
        sums_ref[0, :] = jnp.sum(dout * mid, axis=0)
        sums_ref[1, :] = jnp.sum(dout, axis=0)


def expand_back(summed, grads, slope, normed, vecs, masks, hidden, weight, mid, mid_vecs, block):
    pixels, depth = slope.shape
    width = hidden.shape[1]
    tasks = len(grads)
    column = lambda j: (0, j)
    fixed = lambda j: (0, 0)
    blocks = depth // block
    return pl.pallas_call(
        lambda *refs: expand_back_kernel(tasks, blocks, *refs),
        out_shape=[
            jax.ShapeDtypeStruct((pixels, depth), low),
            jax.ShapeDtypeStruct((width, depth), low),
            jax.ShapeDtypeStruct((pixels, width), full),
            jax.ShapeDtypeStruct((8, width), full),
        ],
        grid_spec=pltpu.PrefetchScalarGridSpec(
            num_scalar_prefetch=0,
            grid=(blocks,),
            in_specs=[spec((summed.shape[0], 128), fixed)]
            + [spec((pixels, block), column)] * tasks
            + [spec((summed.shape[0], block), column)]
            + [spec((pixels, block), column)] * 2
            + [
                spec((8, block), column),
                spec(masks.shape, fixed),
                spec((pixels, width), fixed),
                spec((width, block), column),
                spec((pixels, width), fixed),
                spec((8, width), fixed),
            ],
            out_specs=[
                spec((pixels, block), column),
                spec((width, block), column),
                spec((pixels, width), fixed),
                spec((8, width), fixed),
            ],
            scratch_shapes=[pltpu.VMEM((pixels, width), full), pltpu.VMEM((width, pixels), low)],
        ),
        compiler_params=params(),
        cost_estimate=cost(4 * pixels * width, 14 * pixels),
    )(summed, *grads, summed, slope, normed, vecs, masks, hidden, weight, mid, mid_vecs)


def turn_kernel(*refs):
    out_ref = refs[-1]
    pixels = refs[0].shape[0]
    for i, ref in enumerate(refs[:-1]):
        out_ref[:, i * pixels : (i + 1) * pixels] = ref[...].T


def turn(pieces):
    pixels, depth = pieces[0].shape
    block = min(depth, 512)
    return pl.pallas_call(
        turn_kernel,
        out_shape=jax.ShapeDtypeStruct((depth, len(pieces) * pixels), low),
        grid=(depth // block,),
        in_specs=[spec((pixels, block), lambda i: (0, i))] * len(pieces),
        out_specs=spec((block, len(pieces) * pixels), lambda i: (i, 0)),
        compiler_params=params(),
        cost_estimate=cost(0, 4 * len(pieces) * pixels * depth),
    )(*pieces)


def weight_grad_kernel(members, side_tasks, tasks, groups, *refs):
    slot_ref, task_ref, x_ref = refs[:3]
    chips = groups // 2
    center_refs, side_refs = refs[3 : 3 + chips], refs[3 + chips : 3 + groups]
    mask_refs = refs[3 + groups : 3 + 2 * groups]
    out_ref, dy_ref, total_ref = refs[3 + 2 * groups :]
    pixels = center_refs[0].shape[0]
    lane = center_refs[0].shape[1] // (2 * tasks)
    slots = len(side_tasks)
    three = 3 * lane

    def spread(j, i, grad_ref, at, task):
        rows = slice(j * pixels, (j + 1) * pixels)
        held = grad_ref[:, at * lane : (at + 1) * lane]
        dy_ref[rows, i * three + lane : i * three + 2 * lane] = held
        rate = head_rates[task]
        for k, shift in ((0, pixels - rate), (2, rate)):
            piece = held.astype(full) * mask_refs[j][:, 3 * task + k : 3 * task + k + 1]
            columns = slice(i * three + k * lane, i * three + (k + 1) * lane)
            dy_ref[rows, columns] = pltpu.roll(piece, shift, 0).astype(low)

    @pl.when(pl.program_id(0) == 0)
    def _():
        for j in range(groups):
            for i, item in enumerate(members):
                if item < tasks:
                    spread(j, i, center_refs[j // 2], j % 2 * tasks + item, item)
                    continue
                at = item - tasks
                for task in side_tasks[at]:
                    move = lambda j=j, i=i, at=at, task=task: spread(
                        j, i, side_refs[j // 2], j % 2 * slots + at, task
                    )
                    if len(side_tasks[at]) == 1:
                        move()
                    else:
                        pl.when(task_ref[at] == task)(move)

    total_ref[...] = jnp.dot(x_ref[...], dy_ref[...], preferred_element_type=full)
    for g in range(out_ref.shape[1] // three):
        columns = slice(g * three, (g + 1) * three)

        @pl.when(slot_ref[g] >= 0)
        def _():
            start = pl.multiple_of(slot_ref[g] * three, 128)
            out_ref[:, columns] = total_ref[:, pl.ds(start, three)].astype(low)

        @pl.when(slot_ref[g] < 0)
        def _():
            out_ref[:, columns] = jnp.zeros((out_ref.shape[0], three), low)


def weight_grad(turned, centers, sides, masks, slot_of, side_task, side_tasks, tasks):
    three = 3 * centers[0].shape[1] // (2 * tasks)
    items = tasks + len(side_tasks)
    few = max(1, 2**24 // (turned.shape[1] * three * 2))
    total = None
    for start in range(0, items, few):
        members = list(range(start, min(start + few, items)))
        here = (slot_of >= start) & (slot_of < start + few)
        slots = jnp.where(here, slot_of - start, -1)
        part = some_weight_grad(
            turned, centers, sides, masks, slots, side_task, side_tasks, tasks, members
        )
        total = part if total is None else total + part
    return total


def some_weight_grad(
    turned, centers, sides, masks, slot_of, side_task, side_tasks, tasks, members
):
    depth, pixels = turned.shape
    groups = len(masks)
    parts = slot_of.shape[0]
    three = 3 * centers[0].shape[1] // (2 * tasks)
    items = len(members)
    block = min(depth, 512)
    fixed = lambda g, s, t: (0, 0)
    return pl.pallas_call(
        lambda *refs: weight_grad_kernel(members, side_tasks, tasks, groups, *refs),
        out_shape=jax.ShapeDtypeStruct((depth, parts * three), low),
        grid_spec=pltpu.PrefetchScalarGridSpec(
            num_scalar_prefetch=2,
            grid=(depth // block,),
            in_specs=[spec((block, pixels), lambda g, s, t: (g, 0))]
            + [spec(array.shape, fixed) for array in (*centers, *sides, *masks)],
            out_specs=spec((block, parts * three), lambda g, s, t: (g, 0)),
            scratch_shapes=[
                pltpu.VMEM((pixels, items * three), low),
                pltpu.VMEM((block, items * three), full),
            ],
        ),
        compiler_params=params(),
        cost_estimate=cost(
            2 * pixels * depth * items * three, 2 * depth * (pixels + parts * three)
        ),
    )(slot_of, side_task, turned, *centers, *sides, *masks)


def place_halves_kernel(core_ref, mine_ref, other_ref, out_ref):
    parts, half, _ = mine_ref.shape
    for i in range(parts):
        for ref, which in ((mine_ref, core_ref[0]), (other_ref, 1 - core_ref[0])):
            row = pl.multiple_of((2 * i + which) * half, half)
            out_ref[pl.ds(row, half), :] = ref[i]


def place_halves(mine, other, core, half):
    parts, _, width = mine.shape
    fixed = lambda i, c: (0, 0, 0)
    return pl.pallas_call(
        place_halves_kernel,
        out_shape=jax.ShapeDtypeStruct((parts * 2 * half, width), low),
        grid_spec=pltpu.PrefetchScalarGridSpec(
            num_scalar_prefetch=1,
            grid=(1,),
            in_specs=[spec((parts, half, width), fixed)] * 2,
            out_specs=spec((parts * 2 * half, width), lambda i, c: (0, 0)),
        ),
        compiler_params=params(),
        cost_estimate=cost(0, 8 * parts * half * width),
    )(core, mine, other)


def place_block_kernel(
    red_rows, mid_rows, exp_rows, ratio, core_ref, mine_ref, other_ref, mid_ref, exp_ref
):
    width = mid_ref.shape[0] // 3
    for i in range(mine_ref.shape[0]):
        for ref, which in ((mine_ref, core_ref[0]), (other_ref, 1 - core_ref[0])):
            row = pl.multiple_of((2 * i + which) * mid_rows, mid_rows)
            for tap in range(9):
                ir, ic = divmod(tap, 3)
                at = red_rows + tap * mid_rows
                mid_ref[pl.ds(ir * width + row, mid_rows), ic * width : (ic + 1) * width] = ref[
                    i, at : at + mid_rows
                ]
            row = pl.multiple_of((2 * i + which) * exp_rows, exp_rows)
            for part in range(ratio):
                at = red_rows + 9 * mid_rows + part * exp_rows
                exp_ref[pl.ds(row, exp_rows), part * width : (part + 1) * width] = ref[
                    i, at : at + exp_rows
                ]


def place_block(mine, other, core, red_rows, mid_rows, exp_rows, ratio):
    width = mine.shape[2]
    fixed = lambda i, c: (0, 0, 0)
    flat = lambda i, c: (0, 0)
    shapes = [(3 * width, 3 * width), (width, ratio * width)]
    return pl.pallas_call(
        lambda *refs: place_block_kernel(red_rows, mid_rows, exp_rows, ratio, *refs),
        out_shape=[jax.ShapeDtypeStruct(shape, low) for shape in shapes],
        grid_spec=pltpu.PrefetchScalarGridSpec(
            num_scalar_prefetch=1,
            grid=(1,),
            in_specs=[spec(mine.shape, fixed)] * 2,
            out_specs=[spec(shape, flat) for shape in shapes],
        ),
        compiler_params=params(),
        cost_estimate=cost(0, 8 * mine.size),
    )(core, mine, other)


def place_kernel(chips, part_ref, at_ref, *refs):
    at = pl.program_id(0)
    out_ref = refs[-1]
    taps, _, head = out_ref.shape
    share, lane = refs[0].shape[0], head // 2

    @pl.when(part_ref[at] >= 0)
    def _():
        for m in range(chips):
            row = pl.multiple_of((at_ref[0] ^ m) * share, share)
            for ref, core in ((refs[m], at_ref[1]), (refs[chips + m], 1 - at_ref[1])):
                column = pl.multiple_of(core * lane, lane)
                for k in range(taps):
                    out_ref[k, pl.ds(row, share), pl.ds(column, lane)] = ref[
                        :, k * lane : (k + 1) * lane
                    ].astype(full)

    @pl.when(part_ref[at] < 0)
    def _():
        out_ref[...] = jnp.zeros_like(out_ref)


def place_shares(mine, other, part_of, at, head):
    chips = len(mine)
    share = mine[0].shape[0]
    steps = part_of.shape[0]
    picked = lambda i, p, c: (0, jnp.maximum(p[i], 0))
    return pl.pallas_call(
        lambda *refs: place_kernel(chips, *refs),
        out_shape=jax.ShapeDtypeStruct((3 * steps, chips * share, head), full),
        grid_spec=pltpu.PrefetchScalarGridSpec(
            num_scalar_prefetch=2,
            grid=(steps,),
            in_specs=[spec((share, 3 * head // 2), picked)] * (2 * chips),
            out_specs=spec((3, chips * share, head), lambda i, p, c: (i, 0, 0)),
        ),
        compiler_params=params(),
        cost_estimate=cost(0, 36 * steps * chips * share * head // 2),
    )(part_of, at, *mine, *other)


def on_device(
    features,
    crop_scale,
    crop_group,
    labels,
    w_reduce,
    gain_reduce,
    bias_reduce,
    w_middle,
    gain_middle,
    bias_middle,
    w_expand,
    gain_expand,
    bias_expand,
    w_heads,
    gain_heads,
    bias_heads,
    w_class,
    b_class,
):
    rows = features.shape[1]
    cols = features.shape[2]
    depth = features.shape[3]
    width = w_reduce.shape[1]
    tasks = w_heads.shape[1]
    head = w_heads.shape[3]
    own = w_heads.shape[0]
    classes = w_class.shape[2]
    pixels = rows * cols
    line = line_size()
    place = lax.axis_index(LINE)
    group = lax.axis_index(("x", "c"))
    inside = crop_table(crop_scale, crop_group, group, W_UNIT, cols)

    def same(offset):
        return jnp.tile(jnp.sum(inside * along(inside, offset, 0), axis=1), rows)[:, None]

    valid = same(0)
    count = jnp.sum(crop_scale).astype(full) * float(W_UNIT * rows * line)
    crops = float(crop_scale.shape[0])

    core = lax.axis_index("c")
    core_at = core.reshape(1).astype(jnp.int32)
    ratio = depth // width
    red_rows, mid_rows, exp_rows = (w.shape[0] // 2 for w in (w_reduce, w_middle, w_expand))
    red_own = half_of(w_reduce, 0, core)
    mid_own = half_of(w_middle.transpose(1, 0, 2), 1, core).reshape(9 * mid_rows, width)
    exp_own = half_of(w_expand, 0, core).reshape(exp_rows, ratio, width).transpose(1, 0, 2)
    rest_own = jnp.concatenate([mid_own, exp_own.reshape(ratio * exp_rows, width)], axis=0)
    block_own = jnp.concatenate([red_own, rest_own], axis=0)
    source = features.reshape(pixels, depth) * valid.astype(low)
    block_mine = lax.all_gather(block_own, LINE, axis=0, tiled=False)
    block_mine, source = lax.optimization_barrier((block_mine, source))
    block_other = flip(block_mine, [("c", 1)])
    if mid_rows % 16 == 0 and red_rows % 16 == 0:
        red_all = place_halves(block_mine, block_other, core_at, red_rows)
        mid_all, exp_all = place_block(
            block_mine, block_other, core_at, red_rows, mid_rows, exp_rows, ratio
        )
    else:
        block_all = both_halves(block_mine, block_other, core, 1)
        cuts = np.cumsum([0, red_rows, 9 * mid_rows, ratio * exp_rows])
        red_all, mid_all, exp_all = (block_all[:, :, cuts[i] : cuts[i + 1]] for i in range(3))
        red_all = red_all.reshape(depth, width)
        mid_all = mid_all.reshape(line, 2, 3, 3, mid_rows, width).transpose(2, 0, 1, 4, 3, 5)
        mid_all = mid_all.reshape(3 * width, 3 * width)
        exp_all = exp_all.reshape(line, 2, ratio, exp_rows, width).transpose(0, 1, 3, 2, 4)
        exp_all = exp_all.reshape(width, depth)
    terms, table = head_plan(rows)
    slots = table.shape[0]
    three = 3 * head
    by_term = w_heads.reshape(own, tasks, 3, 3, head).transpose(1, 2, 0, 3, 4)
    by_term = by_term.reshape(tasks, 3, own, three)
    parts = [by_term[t, 1] for t in range(tasks)] + [by_term[t, s + 1] for t, s, _ in terms]
    quarter = own // lax.axis_size(("x", "c"))
    heads_own = jnp.concatenate(
        [lax.dynamic_slice_in_dim(part, group * quarter, quarter, axis=0) for part in parts], axis=1
    )
    heads_own, block_mine = lax.optimization_barrier((heads_own, block_mine))
    heads_all = lax.all_gather(heads_own, AXES, axis=0, tiled=True)
    term_tasks = np.array([task for task, _, _ in terms], np.int32)
    picked_term = jnp.asarray(table)[:, place]
    slot_tasks = [sorted({int(term_tasks[e]) for e in table[s]}) for s in range(slots)]
    side_task = jnp.asarray(term_tasks)[picked_term]
    centers = jnp.arange(tasks, dtype=jnp.int32)
    all_tasks = jnp.concatenate([centers, side_task])
    all_picked = jnp.concatenate([centers, tasks + picked_term])

    reduced = dot(source, red_all)
    mean1, scale1 = norm_scale(reduced, count)
    normed1 = (reduced - mean1) * scale1
    out1 = normed1 * gain_reduce + bias_reduce
    hidden1 = (silu(out1) * valid).astype(low)
    edge = mid_rate * cols
    down = [(i, i + 1) for i in range(line - 1)]
    up = [(i + 1, i) for i in range(line - 1)]
    before1 = rows_to(hidden1[pixels - edge :], down)
    after1 = rows_to(hidden1[:edge], up)
    tall = jnp.concatenate([before1, hidden1, after1], axis=0)
    wide1 = jnp.concatenate([tall[i * edge : i * edge + pixels] for i in range(3)], axis=1)
    spread = dot(wide1, mid_all)
    mid_masks = [same((k - 1) * mid_rate) for k in range(3)]
    middled = sum(
        along(spread[:, k * width : (k + 1) * width], (k - 1) * mid_rate, 0) * mid_masks[k]
        for k in range(3)
    )
    mean2, scale2 = norm_scale(middled, count)
    normed2 = (middled - mean2) * scale2
    out2 = normed2 * gain_middle + bias_middle
    hidden2 = (silu(out2) * valid).astype(low)
    expanded = dot(hidden2, exp_all)
    mean3, scale3 = norm_scale(expanded, count)
    normed3 = (expanded - mean3) * scale3
    before = normed3 * gain_expand + bias_expand + source.astype(full)
    grid = (silu(before) * valid).astype(low)

    chips = lax.axis_size("x")
    chip = lax.axis_index("x")
    share = own // chips

    def share_columns(which):
        cuts = [f * own + which * share for f in range(line)]
        return jnp.concatenate(
            [lax.dynamic_slice_in_dim(grid, cut, share, axis=1) for cut in cuts], axis=1
        )

    grid_pieces = []
    for m in range(chips):
        piece = share_columns(chip ^ m)
        piece = flip(piece, [("x", m)]) if m else piece
        grid_pieces += [piece, flip(piece, [("c", 1)])]

    def mask_table(group):
        inside = crop_table(crop_scale, crop_group, group, W_UNIT, cols)
        columns = [
            jnp.sum(inside * along(inside, (k - 1) * rate, 0), axis=1)
            for rate in head_rates
            for k in range(3)
        ]
        table = jnp.pad(jnp.stack(columns, axis=1), ((0, 0), (0, 128 - 3 * tasks)))
        return jnp.tile(table, (rows, 1))

    masks = mask_table(group)
    moves = row_moves(terms, line)
    side_terms = head_terms(grid, heads_all, masks, tasks + picked_term, side_task, head, low)
    moved = [None] * tasks
    for task, pairs, members in moves:
        sends = {f: s for e, froms in members for f in froms for s in range(slots) if table[s, f] == e}
        sent = None
        for s in sorted(set(sends.values())):
            part = side_terms[:, s * head : (s + 1) * head]
            here = jnp.asarray(np.array([sends.get(f) == s for f in range(line)]))[place]
            sent = part if sent is None else jnp.where(here, part, sent)
        got = rows_to(sent, pairs).astype(full)
        moved[task] = got if moved[task] is None else moved[task] + got
    middle_terms = head_terms(grid, heads_all, masks, centers, centers, head, full)
    middle_terms, grid_pieces = lax.optimization_barrier((middle_terms, grid_pieces))
    mixed = []
    for task in range(tasks):
        center = middle_terms[:, task * head : (task + 1) * head]
        mixed.append(center if moved[task] is None else center + moved[task])
    mixed = jnp.concatenate(mixed, axis=1)
    gain_h, bias_h = gain_heads.reshape(-1), bias_heads.reshape(-1)
    mean_h, scale_h = norm_scale(mixed, count)
    normed_h = (mixed - mean_h) * scale_h
    out_h = normed_h * gain_h + bias_h
    activ = (silu(out_h) * valid).astype(low)
    marks = labels.reshape(tasks, pixels)
    class_part, class_bias_part, dactiv = [], [], []
    for task in range(tasks):
        act = activ[:, task * head : (task + 1) * head]
        logits = dot(act, w_class[task]) + b_class[task]
        onehot = (marks[task][:, None] == jnp.arange(classes, dtype=jnp.int32)[None, :]).astype(full)
        dlogits = ((jax.nn.softmax(logits, axis=-1) - onehot) * valid / crops).astype(low)
        class_part.append(dot_tn(dlogits, act))
        class_bias_part.append(jnp.sum(dlogits.astype(full), axis=0))
        dactiv.append(dot_nt(dlogits, w_class[task]))
    dout_h = jnp.concatenate(dactiv, axis=1) * valid * silu_slope(out_h)
    sums_h = all_sum(jnp.stack([jnp.sum(dout_h * normed_h, axis=0), jnp.sum(dout_h, axis=0)]))
    dgain_h, dbias_h = sums_h[0], sums_h[1]
    dmixed = valid * (gain_h * scale_h) * (dout_h - dbias_h / count - normed_h * (dgain_h / count))
    dmixed = dmixed.astype(low)

    class_sums = jnp.concatenate(
        [jnp.concatenate(class_part, axis=0), jnp.pad(jnp.stack(class_bias_part), ((0, 0), (0, head - classes)))],
        axis=0,
    )
    class_sums = class_sums + flip(class_sums, [("c", 1)])
    class_sums = sum_along(class_sums, "y")
    lane = head // 2
    tap_half = 3 * lane

    def half_taps(grads, which):
        cuts = [i * head + which * lane for i in range(grads.shape[1] // head)]
        return jnp.concatenate(
            [lax.dynamic_slice_in_dim(grads, cut, lane, axis=1) for cut in cuts], axis=1
        )

    def from_groups(grads):
        halves = [half_taps(grads, core), flip(half_taps(grads, 1 - core), [("c", 1)])]
        halves = jnp.concatenate(halves, axis=1)
        return [halves] + [flip(halves, [("x", m)]) for m in range(1, chips)]

    center_halves = from_groups(dmixed)
    all_masks = [masks, mask_table(group ^ 1)]
    for m in range(1, chips):
        all_masks += [mask_table((chip ^ m) * 2 + core), mask_table((chip ^ m) * 2 + 1 - core)]
    back = [None] * len(terms)
    for task, pairs, members in moves:
        got = rows_to(dmixed[:, task * head : (task + 1) * head], [(t, f) for f, t in pairs])
        for e, froms in members:
            here = jnp.asarray(np.array([f in froms for f in range(line)]))[place]
            back[e] = got if len(members) == 1 else jnp.where(here, got, jnp.zeros_like(got))
    dsides = []
    for s in range(slots):
        dside = back[table[s][0]]
        for e in sorted(set(table[s].tolist()) - {int(table[s][0])}):
            dside = jnp.where(picked_term[s] == e, back[e], dside)
        dsides.append(dside)
    turned, dsides, center_halves, class_sums = lax.optimization_barrier(
        (turn(grid_pieces), jnp.concatenate(dsides, axis=1), center_halves, class_sums)
    )
    class_sums = sum_along(class_sums, "z")
    side_halves = from_groups(dsides)
    dterms = jnp.concatenate([dmixed, dsides], axis=1)
    dys = spread_back(dterms, masks, all_tasks, head, pixels)
    here = (side_task[:, None] == centers[None, :]).astype(full).reshape(-1)
    vec_rows = [mean3, scale3, gain_expand, bias_expand]
    vecs = jnp.pad(jnp.stack(vec_rows), ((0, 4), (0, 0)))
    *shared_grads, slope3, normed3, sums = shared_back(
        dys, heads_all, all_picked, here, slot_tasks, tasks, expanded, source, vecs, masks, 256
    )
    sums, center_halves, side_halves, class_sums = lax.optimization_barrier(
        (sums, center_halves, side_halves, class_sums)
    )
    class_sums = sum_along(class_sums, "x")
    gram_part = jnp.sum(sums[2 * tasks : 4 * tasks], axis=1)
    gram_row = jnp.pad(gram_part, (0, depth - gram_part.shape[0]))[None, :]
    summed = all_sum(jnp.concatenate([sums[: 2 * tasks], gram_row], axis=0))
    sums3 = summed[: 2 * tasks].reshape(tasks, 2, depth)
    weight_list = task_scales([summed[2 * tasks, i] for i in range(6)])
    task_weights = jnp.stack(weight_list)

    slot_of = jnp.full((len(terms),), -1, jnp.int32)
    for s in range(slots):
        slot_of = jnp.where(jnp.arange(len(terms)) == picked_term[s], tasks + s, slot_of)
    slot_of = jnp.concatenate([centers, slot_of])
    head_part = weight_grad(
        turned, center_halves, side_halves, all_masks, slot_of, side_task, slot_tasks, tasks
    )
    shared_grads, head_part = lax.optimization_barrier((shared_grads, head_part))
    head_part = head_part.reshape(line, share, len(parts) * tap_half)
    head_own = lax.psum_scatter(head_part, LINE, scatter_dimension=0, tiled=False)

    dgain3, dbias3 = (
        sum(weight_list[t] * sums3[t, j] for t in range(tasks)) for j in range(2)
    )
    vec_rows = [gain_expand * scale3, jnp.broadcast_to(1.0 / count, (depth,))]
    vecs = jnp.pad(jnp.stack(vec_rows), ((0, 6), (0, 0)))
    mid_vecs = jnp.pad(jnp.stack([mean2, scale2, gain_middle, bias_middle]), ((0, 4), (0, 0)))
    dbefore, exp_part, dout2, sums2 = expand_back(
        summed, shared_grads, slope3, normed3, vecs, masks, hidden2, exp_all, middled,
        mid_vecs, 256,
    )
    sums2 = all_sum(sums2[:2])
    dgain2, dbias2 = sums2[0], sums2[1]
    dmiddled = valid * (gain_middle * scale2) * (
        dout2 - dbias2 / count - normed2 * (dgain2 / count)
    )
    dmiddled = dmiddled.astype(low)
    dspread = jnp.concatenate(
        [along(dmiddled * mid_masks[k].astype(low), -(k - 1) * mid_rate, 0) for k in range(3)],
        axis=1,
    )
    dwide = dot_nt(dspread, mid_all)
    from_below = rows_to(dwide[:edge, :width].astype(low), up).astype(full)
    from_above = rows_to(dwide[pixels - edge :, 2 * width :].astype(low), down).astype(full)
    dspread, exp_part, dwide = lax.optimization_barrier((dspread, exp_part, dwide))
    mid_part = dot_tn(wide1, dspread).astype(low).reshape(3, line, 2, mid_rows, 3 * width)
    exp_part = exp_part.reshape(line, 2, exp_rows, depth)

    def later_half(which):
        mid_half = lax.dynamic_index_in_dim(mid_part, which, 2, keepdims=False)
        exp_half = lax.dynamic_index_in_dim(exp_part, which, 1, keepdims=False)
        pieces = [
            mid_half[i, :, :, k * width : (k + 1) * width] for i in range(3) for k in range(3)
        ]
        pieces += [exp_half[:, :, k * width : (k + 1) * width] for k in range(ratio)]
        return jnp.concatenate(pieces, axis=1)

    later_other = flip(later_half(1 - core), [("c", 1)])
    later = (later_half(core).astype(full) + later_other.astype(full)).astype(low)
    dhidden1 = (
        dwide[:, width : 2 * width]
        + jnp.concatenate([dwide[edge:, :width], from_below], axis=0)
        + jnp.concatenate([from_above, dwide[: pixels - edge, 2 * width :]], axis=0)
    )
    dout1 = dhidden1 * valid * silu_slope(out1)
    sums1 = all_sum(jnp.stack([jnp.sum(dout1 * normed1, axis=0), jnp.sum(dout1, axis=0)]))
    sums1, later = lax.optimization_barrier((sums1, later))
    cut = later.shape[1] // 2
    later_own = jnp.concatenate(
        [scatter_z(scatter_y(piece)) for piece in (later[:, :cut], later[:, cut:])], axis=0
    )
    dgain1, dbias1 = sums1[0], sums1[1]
    dreduced = valid * (gain_reduce * scale1) * (
        dout1 - dbias1 / count - normed1 * (dgain1 / count)
    )
    dreduced = dreduced.astype(low)
    dfeatures = dbefore.astype(full) + dot_nt(dreduced, red_all)

    red_part = dot_tn(source, dreduced).astype(low).reshape(line, -1, width)
    red_sum = over_groups(scatter_z(scatter_y(between_cores(red_part))))
    red_sum = both_halves(*red_sum, core, 0).astype(full)
    part_of = np.full((tasks, 3), -1, np.int32)
    part_of[:, 1] = np.arange(tasks)
    for e, (task, side, _) in enumerate(terms):
        part_of[task, side + 1] = tasks + e
    head_shares = [head_own] + [flip(head_own, [("x", m)]) for m in range(1, chips)]
    head_others = [flip(part, [("c", 1)]) for part in head_shares]
    at = jnp.stack([chip, core]).astype(jnp.int32)
    heads_out = place_shares(head_shares, head_others, jnp.asarray(part_of.reshape(-1)), at, head)
    heads_out = heads_out.reshape(tasks, 9, own, head).transpose(2, 0, 1, 3)
    later_own, later_other = over_groups(later_own)
    later_sum = both_halves(
        later_own.reshape(9 + ratio, mid_rows, width),
        later_other.reshape(9 + ratio, mid_rows, width),
        core,
        1,
    ).reshape(9 + ratio, 2 * mid_rows, width)
    mid_sum = later_sum[:9].transpose(1, 0, 2).astype(full)
    exp_sum = later_sum[9:].transpose(1, 0, 2).reshape(2 * exp_rows, depth).astype(full)
    grad_class = class_sums[: tasks * classes].reshape(tasks, classes, head).transpose(0, 2, 1)
    grad_class_bias = class_sums[tasks * classes :, :classes]
    return (
        dfeatures.reshape(1, rows, cols, depth),
        red_sum.reshape(w_reduce.shape),
        mid_sum,
        exp_sum,
        heads_out,
        dgain1,
        dbias1,
        dgain2,
        dbias2,
        dgain3,
        dbias3,
        dgain_h.reshape(tasks, head),
        dbias_h.reshape(tasks, head),
        grad_class,
        grad_class_bias,
        task_weights,
    )


def solution(mesh):
    line, groups = mesh.shape["fsdp"], mesh.shape["dp"]
    fine = Mesh(mesh.devices.reshape(line // 2, 2, groups // 2, 2), AXES)
    dp = ("x", "c")
    rows = P(LINE)
    in_specs = (
        P(dp, LINE, None, None),
        P(),
        P(),
        P(None, dp, LINE, None),
        rows,
        P(),
        P(),
        rows,
        P(),
        P(),
        rows,
        P(),
        P(),
        rows,
        P(),
        P(),
        P(),
        P(),
    )
    out_specs = (P(dp, LINE, None, None),) + (rows,) * 4 + (P(),) * 11
    return jax.shard_map(
        on_device, mesh=fine, in_specs=in_specs, out_specs=out_specs, check_vma=False
    )
```

```python
import itertools

import jax
import jax.numpy as jnp
import numpy as np
from jax import lax
from jax.experimental import pallas as pl
from jax.experimental.pallas import tpu as pltpu
from jax.sharding import Mesh
from jax.sharding import PartitionSpec as P

W_UNIT = 12


eps = 1e-05
mid_rate = 2
head_rates = (12, 24, 36)
AXES = ("z", "y", "x", "c")
LINE = ("z", "y")
low = jnp.bfloat16
full = jnp.float32


def coords(names):
    return list(itertools.product(*[range(lax.axis_size(name)) for name in names]))


def flip(value, moves):
    moves = sorted([m for m in moves if m[1]], key=lambda move: AXES.index(move[0]))
    names = tuple(name for name, _ in moves)
    places = coords(names)
    index = {place: i for i, place in enumerate(places)}
    pairs = [
        (i, index[tuple(at ^ bit for at, (_, bit) in zip(place, moves))])
        for i, place in enumerate(places)
    ]
    return lax.ppermute(value, names, pairs)


def all_sum(value):
    moves = []
    for name in ("y", "x", "z"):
        bit = 1
        while bit < lax.axis_size(name):
            moves.append((name, bit))
            bit *= 2
    value = value + flip(value, [("c", 1)])
    while moves:
        if len(moves) == 1:
            value = value + flip(value, moves)
            break
        first, second = moves[:2]
        moves = moves[2:]
        both = [(first[0], first[1] | second[1])] if first[0] == second[0] else [first, second]
        one, two, three = flip(value, [first]), flip(value, [second]), flip(value, both)
        value = (value + one) + (two + three)
    return value


def sum_along(value, name):
    bit = 1
    while bit < lax.axis_size(name):
        value = value + flip(value, [(name, bit)])
        bit *= 2
    return value


def rows_to(value, pairs):
    if not pairs:
        return jnp.zeros_like(value)
    return lax.ppermute(value, LINE, pairs)


def line_size():
    return lax.axis_size("z") * lax.axis_size("y")


def half_of(value, axis, core):
    size = value.shape[axis] // 2
    return lax.dynamic_slice_in_dim(value, core * size, size, axis=axis)


def both_halves(mine, other, core, axis):
    first = jnp.where(core == 0, mine, other)
    second = jnp.where(core == 0, other, mine)
    return jnp.stack([first, second], axis=axis)


def between_cores(partial):
    core = lax.axis_index("c")
    mine = half_of(partial, 1, core)
    other = flip(half_of(partial, 1, 1 - core), [("c", 1)])
    return (mine.astype(full) + other.astype(full)).astype(low)


def over_groups(own):
    bit = 1
    while bit < lax.axis_size("x"):
        own = (own.astype(full) + flip(own, [("x", bit)]).astype(full)).astype(low)
        bit *= 2
    return own, flip(own, [("c", 1)])


def scatter_y(partial):
    parts = partial.reshape(-1, 2, *partial.shape[1:])
    here = lax.axis_index("y")
    mine = lax.dynamic_index_in_dim(parts, here, 1, keepdims=False)
    other = lax.dynamic_index_in_dim(parts, 1 - here, 1, keepdims=False)
    return (mine.astype(full) + flip(other, [("y", 1)]).astype(full)).astype(low)


def scatter_x(partial, axis):
    chips, here = lax.axis_size("x"), lax.axis_index("x")
    size = partial.shape[axis] // chips
    total = lax.dynamic_slice_in_dim(partial, here * size, size, axis).astype(full)
    for m in range(1, chips):
        part = lax.dynamic_slice_in_dim(partial, (here ^ m) * size, size, axis)
        total = total + flip(part, [("x", m)]).astype(full)
    return total.astype(low)


def gather_x(own):
    chips, here = lax.axis_size("x"), lax.axis_index("x")
    parts = jnp.stack([own] + [flip(own, [("x", m)]) for m in range(1, chips)])
    ordered = [lax.dynamic_index_in_dim(parts, here ^ m, 0, keepdims=False) for m in range(chips)]
    return jnp.concatenate(ordered, axis=0)


def scatter_z(parts):
    here = lax.axis_index("z")
    total = lax.dynamic_index_in_dim(parts, here, 0, keepdims=False).astype(full)
    for m in range(1, lax.axis_size("z")):
        part = lax.dynamic_index_in_dim(parts, here ^ m, 0, keepdims=False)
        total = total + flip(part, [("z", m)]).astype(full)
    return total.astype(low)


def along(value, offset, axis):
    size = value.shape[axis]
    if offset == 0:
        return value
    widths = [(0, 0)] * value.ndim
    if offset > 0:
        widths[axis] = (0, offset)
        return lax.slice_in_dim(jnp.pad(value, widths), offset, offset + size, axis=axis)
    widths[axis] = (-offset, 0)
    return lax.slice_in_dim(jnp.pad(value, widths), 0, size, axis=axis)


def crop_table(crop_scale, crop_group, group, unit, cols):
    mine = (crop_group == group).astype(jnp.int32)
    widths = crop_scale * unit * mine
    ends = jnp.cumsum(widths)
    starts = ends - widths
    column = jnp.arange(cols, dtype=jnp.int32)[:, None]
    return ((column >= starts[None, :]) & (column < ends[None, :])).astype(full)


def silu(value):
    return value * (0.5 + 0.5 * jnp.tanh(0.5 * value))


def silu_slope(value):
    turn = jnp.tanh(0.5 * value)
    return 0.5 + 0.5 * turn + 0.25 * value * (1.0 - turn * turn)


def norm_scale(value, count):
    sums = all_sum(jnp.stack([jnp.sum(value, axis=0), jnp.sum(value * value, axis=0)]))
    mean = sums[0] / count
    return mean, lax.rsqrt(sums[1] / count - mean * mean + eps)


def head_plan(rows):
    line = line_size()
    terms = []
    for task, rate in enumerate(head_rates):
        hop = rate // rows
        for side in (-1, 1):
            if hop < line:
                terms.append((task, side, hop))
    last = lax.axis_size("y")
    planes = []
    for z in range(lax.axis_size("z")):
        need = []
        for e, (task, side, hop) in enumerate(terms):
            if any(0 <= z * last + y - side * hop < line for y in range(last)):
                need.append(e)
        planes.append(need)
    slots = max(len(need) for need in planes)
    table = np.zeros((slots, line), np.int32)
    for z, need in enumerate(planes):
        rest = [e for e in range(len(terms)) if e not in need]
        for s, e in enumerate((need + rest)[:slots]):
            table[s, z * last : (z + 1) * last] = e
    return terms, table


def row_moves(terms, line):
    moves = []
    for e, (task, side, hop) in enumerate(terms):
        pairs = [(f, f - side * hop) for f in range(line) if 0 <= f - side * hop < line]
        last = moves[-1] if moves else None
        if last and last[0] == task and not {t for _, t in last[1]} & {t for _, t in pairs}:
            if not {f for f, _ in last[1]} & {f for f, _ in pairs}:
                last[1].extend(pairs)
                last[2].append((e, [f for f, _ in pairs]))
                continue
        moves.append((task, pairs, [(e, [f for f, _ in pairs])]))
    return moves


def task_scales(products):
    g00, g01, g02, g11, g12, g22 = products
    n0, n1, n2 = (jnp.sqrt(g + 1e-12) for g in (g00, g11, g22))
    c00, c11, c22 = (g / (n * n) + 0.1 for g, n in ((g00, n0), (g11, n1), (g22, n2)))
    c01, c02, c12 = g01 / (n0 * n1), g02 / (n0 * n2), g12 / (n1 * n2)
    w0 = (c11 * c22 - c12 * c12) + (c12 * c02 - c01 * c22) + (c01 * c12 - c11 * c02)
    w1 = (c12 * c02 - c22 * c01) + (c22 * c00 - c02 * c02) + (c02 * c01 - c12 * c00)
    w2 = (c01 * c12 - c02 * c11) + (c02 * c01 - c00 * c12) + (c00 * c11 - c01 * c01)
    top = n0 + n1 + n2
    total = w0 + w1 + w2
    return [w * top / (n * total) for w, n in ((w0, n0), (w1, n1), (w2, n2))]


def dot(a, b):
    return jnp.dot(a, b, preferred_element_type=full)


def dot_nt(a, b):
    return lax.dot_general(a, b, (((1,), (1,)), ((), ())), preferred_element_type=full)


def dot_tn(a, b):
    return lax.dot_general(a, b, (((0,), (0,)), ((), ())), preferred_element_type=full)


def spec(shape, index):
    return pl.BlockSpec(shape, index)


def params(mib=56):
    return pltpu.CompilerParams(vmem_limit_bytes=mib * 2**20)


def cost(flops, moved):
    return pl.CostEstimate(flops=flops, bytes_accessed=moved, transcendentals=0)


def terms_kernel(picked_ref, task_ref, x_ref, w_ref, mask_ref, out_ref):
    at = pl.program_id(0)
    pixels, head = out_ref.shape

    def product(k):
        return jnp.dot(
            x_ref[...], w_ref[:, k * head : (k + 1) * head], preferred_element_type=full
        )

    for task, rate in enumerate(head_rates):

        @pl.when(task_ref[at] == task)
        def _():
            left = pltpu.roll(product(0), rate, 0) * mask_ref[:, 3 * task : 3 * task + 1]
            right = pltpu.roll(product(2), pixels - rate, 0)
            right = right * mask_ref[:, 3 * task + 2 : 3 * task + 3]
            out_ref[...] = (product(1) + left + right).astype(out_ref.dtype)


def head_terms(grid, heads_all, masks, picked, task_of, head, dtype):
    pixels, depth = grid.shape
    items = picked.shape[0]
    return pl.pallas_call(
        terms_kernel,
        out_shape=jax.ShapeDtypeStruct((pixels, items * head), dtype),
        grid_spec=pltpu.PrefetchScalarGridSpec(
            num_scalar_prefetch=2,
            grid=(items,),
            in_specs=[
                spec((pixels, depth), lambda i, p, t: (0, 0)),
                spec((depth, 3 * head), lambda i, p, t: (0, p[i])),
                spec(masks.shape, lambda i, p, t: (0, 0)),
            ],
            out_specs=spec((pixels, head), lambda i, p, t: (0, i)),
        ),
        compiler_params=params(),
        cost_estimate=cost(
            2 * pixels * depth * 3 * head * items, 2 * items * depth * 3 * head + 2 * pixels * depth
        ),
    )(picked, task_of, grid, heads_all, masks)


def spread_kernel(task_ref, d_ref, mask_ref, out_ref):
    at = pl.program_id(1)
    pixels, head = d_ref.shape
    for task, rate in enumerate(head_rates):

        @pl.when(task_ref[at] == task)
        def _():
            grad = d_ref[...].astype(full)
            out_ref[:, head : 2 * head] = d_ref[...]
            for k, shift in ((0, pixels - rate), (2, rate)):
                piece = grad * mask_ref[:, 3 * task + k : 3 * task + k + 1]
                out_ref[:, k * head : (k + 1) * head] = pltpu.roll(piece, shift, 0).astype(low)


def spread_back(grads, masks, task_of, head, pixels):
    rows = grads.shape[0]
    items = grads.shape[1] // head
    return pl.pallas_call(
        spread_kernel,
        out_shape=jax.ShapeDtypeStruct((rows, 3 * head * items), low),
        grid_spec=pltpu.PrefetchScalarGridSpec(
            num_scalar_prefetch=1,
            grid=(rows // pixels, items),
            in_specs=[
                spec((pixels, head), lambda j, i, t: (j, i)),
                spec((pixels, masks.shape[1]), lambda j, i, t: (j, 0)),
            ],
            out_specs=spec((pixels, 3 * head), lambda j, i, t: (j, i)),
        ),
        compiler_params=params(),
        cost_estimate=cost(30 * rows * head * items, 8 * rows * head * items),
    )(task_of, grads, masks)


def center_back_kernel(tasks, *refs):
    dy_ref = refs[0]
    w_refs = refs[1 : 1 + tasks]
    wide_ref, source_ref, vec_ref, mask_ref = refs[1 + tasks : 5 + tasks]
    out_refs = refs[5 + tasks : -2]
    slope_ref, normed_ref = refs[-2:]
    three = w_refs[0].shape[1]
    pixels = dy_ref.shape[0]
    for at in range(0, pixels, pixels // 3):
        rows = slice(at, at + pixels // 3)
        for t in range(tasks):
            out_refs[t][rows, :] = lax.dot_general(
                dy_ref[rows, t * three : (t + 1) * three],
                w_refs[t][...],
                (((1,), (1,)), ((), ())),
                preferred_element_type=full,
            ).astype(low)
        normed = (wide_ref[rows, :].astype(full) - vec_ref[0:1]) * vec_ref[1:2]
        value = normed * vec_ref[2:3] + vec_ref[3:4] + source_ref[rows, :].astype(full)
        slope_ref[rows, :] = (silu_slope(value) * mask_ref[rows, 1:2]).astype(low)
        normed_ref[rows, :] = normed.astype(low)


def center_back(dys, heads_all, tasks, wide, source, vecs, masks, block):
    pixels, depth = wide.shape
    three = dys.shape[1] // tasks
    column = lambda j: (0, j)
    fixed = lambda j: (0, 0)
    return pl.pallas_call(
        lambda *refs: center_back_kernel(tasks, *refs),
        out_shape=[jax.ShapeDtypeStruct((pixels, depth), low)] * (tasks + 2),
        grid=(depth // block,),
        in_specs=[spec(dys.shape, fixed)]
        + [spec((block, three), lambda j, i=i: (j, i)) for i in range(tasks)]
        + [spec((pixels, block), column)] * 2
        + [spec((8, block), column), spec(masks.shape, fixed)],
        out_specs=[spec((pixels, block), column)] * (tasks + 2),
        compiler_params=params(),
        cost_estimate=cost(2 * pixels * depth * three * tasks, 16 * pixels * depth),
    )(dys, *([heads_all] * tasks), wide, source, vecs, masks)


def side_back_kernel(tasks, side_tasks, touched, *refs):
    slots = len(side_tasks)
    here_ref, dy_ref = refs[1:3]
    w_refs = refs[3 : 3 + slots]
    held_refs = refs[3 + slots : 3 + slots + tasks]
    slope_ref, normed_ref = refs[3 + slots + tasks : 5 + slots + tasks]
    out_refs = refs[5 + slots + tasks : -1]
    sums_ref = refs[-1]
    pixels = dy_ref.shape[0]
    totals = None
    for at in range(0, pixels, pixels // 3):
        rows = slice(at, at + pixels // 3)
        grads = [ref[rows, :].astype(full) for ref in held_refs]
        for s, choices in enumerate(side_tasks):
            three = w_refs[s].shape[1]
            side = lax.dot_general(
                dy_ref[rows, s * three : (s + 1) * three],
                w_refs[s][...],
                (((1,), (1,)), ((), ())),
                preferred_element_type=full,
            )
            for t in choices:
                more = side if len(choices) == 1 else side * here_ref[s * tasks + t]
                grads[t] = grads[t] + more
        slope, normed = slope_ref[rows, :].astype(full), normed_ref[rows, :].astype(full)
        parts = []
        for t in range(tasks):
            part = grads[t] * slope
            parts += [jnp.sum(part * normed, axis=0), jnp.sum(part, axis=0)]
        for t in range(tasks):
            for u in range(t, tasks):
                parts.append(jnp.sum(grads[t] * grads[u], axis=0))
        for i, t in enumerate(touched):
            out_refs[i][rows, :] = grads[t].astype(low)
        totals = parts if totals is None else [a + b for a, b in zip(totals, parts)]
    sums_ref[...] = jnp.zeros_like(sums_ref)
    for i, row in enumerate(totals):
        sums_ref[i, :] = row


def side_back(dys, heads_all, picked, here, side_tasks, tasks, held, slope, normed, block):
    pixels, depth = slope.shape
    slots = len(side_tasks)
    three = dys.shape[1] // slots
    touched = sorted({t for choices in side_tasks for t in choices})
    column = lambda j, p, h: (0, j)
    *outs, sums = pl.pallas_call(
        lambda *refs: side_back_kernel(tasks, side_tasks, touched, *refs),
        out_shape=[jax.ShapeDtypeStruct((pixels, depth), low)] * len(touched)
        + [jax.ShapeDtypeStruct((16, depth), full)],
        grid_spec=pltpu.PrefetchScalarGridSpec(
            num_scalar_prefetch=2,
            grid=(depth // block,),
            in_specs=[spec(dys.shape, lambda j, p, h: (0, 0))]
            + [spec((block, three), lambda j, p, h, i=i: (j, p[i])) for i in range(slots)]
            + [spec((pixels, block), column)] * (tasks + 2),
            out_specs=[spec((pixels, block), column)] * len(touched) + [spec((16, block), column)],
        ),
        compiler_params=params(),
        cost_estimate=cost(2 * pixels * depth * three * slots, 14 * pixels * depth),
    )(picked, here, dys, *([heads_all] * slots), *held, slope, normed)
    return [outs[touched.index(t)] if t in touched else held[t] for t in range(tasks)], sums


def expand_back_kernel(tasks, blocks, *refs):
    gram_ref, sum_ref = refs[0], refs[1 + tasks]
    grad_refs = refs[1 : 1 + tasks]
    slope_ref, normed_ref, vec_ref, mask_ref, hidden_ref, w_ref, mid_ref, mid_vec_ref = refs[
        2 + tasks : 10 + tasks
    ]
    dbefore_ref, dweight_ref, dout_ref, sums_ref, total_ref, turned_ref, scale_ref = refs[
        10 + tasks :
    ]
    at = pl.program_id(0)

    @pl.when(at == 0)
    def _():
        turned_ref[...] = hidden_ref[...].T
        gram = 2 * tasks
        scales = task_scales([gram_ref[gram : gram + 1, i : i + 1] for i in range(6)])
        for t in range(tasks):
            scale_ref[t : t + 1, :] = jnp.broadcast_to(scales[t], (1, scale_ref.shape[1]))

    weights = [scale_ref[t : t + 1, :] for t in range(tasks)]
    combined = grad_refs[0][...].astype(full) * weights[0]
    dgain = sum_ref[0:1] * weights[0]
    dbias = sum_ref[1:2] * weights[0]
    for t in range(1, tasks):
        combined = combined + grad_refs[t][...].astype(full) * weights[t]
        dgain = dgain + sum_ref[2 * t : 2 * t + 1] * weights[t]
        dbias = dbias + sum_ref[2 * t + 1 : 2 * t + 2] * weights[t]
    normed = normed_ref[...].astype(full)
    valid = mask_ref[:, 1:2]
    dbefore = combined * slope_ref[...].astype(full)
    dbefore_ref[...] = dbefore.astype(low)
    per = vec_ref[1:2]
    dwide = (dbefore - dbias * per - normed * (dgain * per)) * vec_ref[0:1] * valid
    dwide = dwide.astype(low)
    dweight_ref[...] = jnp.dot(turned_ref[...], dwide, preferred_element_type=full).astype(low)
    part = lax.dot_general(
        dwide, w_ref[...], (((1,), (1,)), ((), ())), preferred_element_type=full
    )

    @pl.when(at == 0)
    def _():
        total_ref[...] = part

    @pl.when(at > 0)
    def _():
        total_ref[...] += part

    @pl.when(at == blocks - 1)
    def _():
        mid = (mid_ref[...] - mid_vec_ref[0:1]) * mid_vec_ref[1:2]
        dout = total_ref[...] * silu_slope(mid * mid_vec_ref[2:3] + mid_vec_ref[3:4]) * valid
        dout_ref[...] = dout
        sums_ref[...] = jnp.zeros_like(sums_ref)
        sums_ref[0, :] = jnp.sum(dout * mid, axis=0)
        sums_ref[1, :] = jnp.sum(dout, axis=0)


def expand_back(summed, grads, slope, normed, vecs, masks, hidden, weight, mid, mid_vecs, block):
    pixels, depth = slope.shape
    width = hidden.shape[1]
    tasks = len(grads)
    column = lambda j: (0, j)
    fixed = lambda j: (0, 0)
    blocks = depth // block
    return pl.pallas_call(
        lambda *refs: expand_back_kernel(tasks, blocks, *refs),
        out_shape=[
            jax.ShapeDtypeStruct((pixels, depth), low),
            jax.ShapeDtypeStruct((width, depth), low),
            jax.ShapeDtypeStruct((pixels, width), full),
            jax.ShapeDtypeStruct((8, width), full),
        ],
        grid_spec=pltpu.PrefetchScalarGridSpec(
            num_scalar_prefetch=0,
            grid=(blocks,),
            in_specs=[spec((summed.shape[0], 128), fixed)]
            + [spec((pixels, block), column)] * tasks
            + [spec((summed.shape[0], block), column)]
            + [spec((pixels, block), column)] * 2
            + [
                spec((8, block), column),
                spec(masks.shape, fixed),
                spec((pixels, width), fixed),
                spec((width, block), column),
                spec((pixels, width), fixed),
                spec((8, width), fixed),
            ],
            out_specs=[
                spec((pixels, block), column),
                spec((width, block), column),
                spec((pixels, width), fixed),
                spec((8, width), fixed),
            ],
            scratch_shapes=[
                pltpu.VMEM((pixels, width), full),
                pltpu.VMEM((width, pixels), low),
                pltpu.VMEM((8, block), full),
            ],
        ),
        compiler_params=params(),
        cost_estimate=cost(4 * pixels * width, 14 * pixels),
    )(summed, *grads, summed, slope, normed, vecs, masks, hidden, weight, mid, mid_vecs)


def turn_kernel(*refs):
    out_ref = refs[-1]
    pixels = refs[0].shape[0]
    for i, ref in enumerate(refs[:-1]):
        out_ref[:, i * pixels : (i + 1) * pixels] = ref[...].T


def turn(pieces):
    pixels, depth = pieces[0].shape
    block = min(depth, 512)
    return pl.pallas_call(
        turn_kernel,
        out_shape=jax.ShapeDtypeStruct((depth, len(pieces) * pixels), low),
        grid=(depth // block,),
        in_specs=[spec((pixels, block), lambda i: (0, i))] * len(pieces),
        out_specs=spec((block, len(pieces) * pixels), lambda i: (i, 0)),
        compiler_params=params(),
        cost_estimate=cost(0, 4 * len(pieces) * pixels * depth),
    )(*pieces)


def weight_grad_kernel(members, side_tasks, tasks, groups, *refs):
    slot_ref, task_ref, x_ref = refs[:3]
    chips = groups // 2
    center_refs, side_refs = refs[3 : 3 + chips], refs[3 + chips : 3 + groups]
    mask_refs = refs[3 + groups : 3 + 2 * groups]
    out_ref, dy_ref, total_ref = refs[3 + 2 * groups :]
    pixels = center_refs[0].shape[0]
    lane = center_refs[0].shape[1] // (2 * tasks)
    slots = len(side_tasks)
    three = 3 * lane

    def spread(j, i, grad_ref, at, task):
        rows = slice(j * pixels, (j + 1) * pixels)
        held = grad_ref[:, at * lane : (at + 1) * lane]
        dy_ref[rows, i * three + lane : i * three + 2 * lane] = held
        rate = head_rates[task]
        for k, shift in ((0, pixels - rate), (2, rate)):
            piece = held.astype(full) * mask_refs[j][:, 3 * task + k : 3 * task + k + 1]
            columns = slice(i * three + k * lane, i * three + (k + 1) * lane)
            dy_ref[rows, columns] = pltpu.roll(piece, shift, 0).astype(low)

    @pl.when(pl.program_id(0) == 0)
    def _():
        for j in range(groups):
            for i, item in enumerate(members):
                if item < tasks:
                    spread(j, i, center_refs[j // 2], j % 2 * tasks + item, item)
                    continue
                at = item - tasks
                for task in side_tasks[at]:
                    move = lambda j=j, i=i, at=at, task=task: spread(
                        j, i, side_refs[j // 2], j % 2 * slots + at, task
                    )
                    if len(side_tasks[at]) == 1:
                        move()
                    else:
                        pl.when(task_ref[at] == task)(move)

    total_ref[...] = jnp.dot(x_ref[...], dy_ref[...], preferred_element_type=full)
    for g in range(out_ref.shape[1] // three):
        columns = slice(g * three, (g + 1) * three)

        @pl.when(slot_ref[g] >= 0)
        def _():
            start = pl.multiple_of(slot_ref[g] * three, 128)
            out_ref[:, columns] = total_ref[:, pl.ds(start, three)].astype(low)

        @pl.when(slot_ref[g] < 0)
        def _():
            out_ref[:, columns] = jnp.zeros((out_ref.shape[0], three), low)


def weight_grad(turned, centers, sides, masks, slot_of, side_task, side_tasks, tasks):
    three = 3 * centers[0].shape[1] // (2 * tasks)
    items = tasks + len(side_tasks)
    few = max(1, 2**24 // (turned.shape[1] * three * 2))
    total = None
    for start in range(0, items, few):
        members = list(range(start, min(start + few, items)))
        here = (slot_of >= start) & (slot_of < start + few)
        slots = jnp.where(here, slot_of - start, -1)
        part = some_weight_grad(
            turned, centers, sides, masks, slots, side_task, side_tasks, tasks, members
        )
        total = part if total is None else total + part
    return total


def some_weight_grad(
    turned, centers, sides, masks, slot_of, side_task, side_tasks, tasks, members
):
    depth, pixels = turned.shape
    groups = len(masks)
    parts = slot_of.shape[0]
    three = 3 * centers[0].shape[1] // (2 * tasks)
    items = len(members)
    block = min(depth, 512)
    fixed = lambda g, s, t: (0, 0)
    return pl.pallas_call(
        lambda *refs: weight_grad_kernel(members, side_tasks, tasks, groups, *refs),
        out_shape=jax.ShapeDtypeStruct((depth, parts * three), low),
        grid_spec=pltpu.PrefetchScalarGridSpec(
            num_scalar_prefetch=2,
            grid=(depth // block,),
            in_specs=[spec((block, pixels), lambda g, s, t: (g, 0))]
            + [spec(array.shape, fixed) for array in (*centers, *sides, *masks)],
            out_specs=spec((block, parts * three), lambda g, s, t: (g, 0)),
            scratch_shapes=[
                pltpu.VMEM((pixels, items * three), low),
                pltpu.VMEM((block, items * three), full),
            ],
        ),
        compiler_params=params(),
        cost_estimate=cost(
            2 * pixels * depth * items * three, 2 * depth * (pixels + parts * three)
        ),
    )(slot_of, side_task, turned, *centers, *sides, *masks)


def place_halves_kernel(core_ref, mine_ref, other_ref, out_ref):
    parts, half, _ = mine_ref.shape
    for i in range(parts):
        for ref, which in ((mine_ref, core_ref[0]), (other_ref, 1 - core_ref[0])):
            row = pl.multiple_of((2 * i + which) * half, half)
            out_ref[pl.ds(row, half), :] = ref[i]


def place_halves(mine, other, core, half):
    parts, _, width = mine.shape
    fixed = lambda i, c: (0, 0, 0)
    return pl.pallas_call(
        place_halves_kernel,
        out_shape=jax.ShapeDtypeStruct((parts * 2 * half, width), low),
        grid_spec=pltpu.PrefetchScalarGridSpec(
            num_scalar_prefetch=1,
            grid=(1,),
            in_specs=[spec((parts, half, width), fixed)] * 2,
            out_specs=spec((parts * 2 * half, width), lambda i, c: (0, 0)),
        ),
        compiler_params=params(),
        cost_estimate=cost(0, 8 * parts * half * width),
    )(core, mine, other)


def place_block_kernel(
    red_rows, mid_rows, exp_rows, ratio, core_ref, mine_ref, other_ref, mid_ref, exp_ref
):
    width = mid_ref.shape[0] // 3
    for i in range(mine_ref.shape[0]):
        for ref, which in ((mine_ref, core_ref[0]), (other_ref, 1 - core_ref[0])):
            row = pl.multiple_of((2 * i + which) * mid_rows, mid_rows)
            for tap in range(9):
                ir, ic = divmod(tap, 3)
                at = red_rows + tap * mid_rows
                mid_ref[pl.ds(ir * width + row, mid_rows), ic * width : (ic + 1) * width] = ref[
                    i, at : at + mid_rows
                ]
            row = pl.multiple_of((2 * i + which) * exp_rows, exp_rows)
            for part in range(ratio):
                at = red_rows + 9 * mid_rows + part * exp_rows
                exp_ref[pl.ds(row, exp_rows), part * width : (part + 1) * width] = ref[
                    i, at : at + exp_rows
                ]


def place_block(mine, other, core, red_rows, mid_rows, exp_rows, ratio):
    width = mine.shape[2]
    fixed = lambda i, c: (0, 0, 0)
    flat = lambda i, c: (0, 0)
    shapes = [(3 * width, 3 * width), (width, ratio * width)]
    return pl.pallas_call(
        lambda *refs: place_block_kernel(red_rows, mid_rows, exp_rows, ratio, *refs),
        out_shape=[jax.ShapeDtypeStruct(shape, low) for shape in shapes],
        grid_spec=pltpu.PrefetchScalarGridSpec(
            num_scalar_prefetch=1,
            grid=(1,),
            in_specs=[spec(mine.shape, fixed)] * 2,
            out_specs=[spec(shape, flat) for shape in shapes],
        ),
        compiler_params=params(),
        cost_estimate=cost(0, 8 * mine.size),
    )(core, mine, other)


def place_kernel(chips, part_ref, at_ref, *refs):
    at = pl.program_id(0)
    out_ref = refs[-1]
    taps, _, head = out_ref.shape
    share, lane = refs[0].shape[0], head // 2

    @pl.when(part_ref[at] >= 0)
    def _():
        for m in range(chips):
            row = pl.multiple_of((at_ref[0] ^ m) * share, share)
            for ref, core in ((refs[m], at_ref[1]), (refs[chips + m], 1 - at_ref[1])):
                column = pl.multiple_of(core * lane, lane)
                for k in range(taps):
                    out_ref[k, pl.ds(row, share), pl.ds(column, lane)] = ref[
                        :, k * lane : (k + 1) * lane
                    ].astype(full)

    @pl.when(part_ref[at] < 0)
    def _():
        out_ref[...] = jnp.zeros_like(out_ref)


def place_shares(mine, other, part_of, at, head):
    chips = len(mine)
    share = mine[0].shape[0]
    steps = part_of.shape[0]
    picked = lambda i, p, c: (0, jnp.maximum(p[i], 0))
    return pl.pallas_call(
        lambda *refs: place_kernel(chips, *refs),
        out_shape=jax.ShapeDtypeStruct((3 * steps, chips * share, head), full),
        grid_spec=pltpu.PrefetchScalarGridSpec(
            num_scalar_prefetch=2,
            grid=(steps,),
            in_specs=[spec((share, 3 * head // 2), picked)] * (2 * chips),
            out_specs=spec((3, chips * share, head), lambda i, p, c: (i, 0, 0)),
        ),
        compiler_params=params(),
        cost_estimate=cost(0, 36 * steps * chips * share * head // 2),
    )(part_of, at, *mine, *other)


def on_device(
    features,
    crop_scale,
    crop_group,
    labels,
    w_reduce,
    gain_reduce,
    bias_reduce,
    w_middle,
    gain_middle,
    bias_middle,
    w_expand,
    gain_expand,
    bias_expand,
    w_heads,
    gain_heads,
    bias_heads,
    w_class,
    b_class,
):
    rows = features.shape[1]
    cols = features.shape[2]
    depth = features.shape[3]
    width = w_reduce.shape[1]
    tasks = w_heads.shape[1]
    head = w_heads.shape[3]
    own = w_heads.shape[0]
    classes = w_class.shape[2]
    pixels = rows * cols
    line = line_size()
    place = lax.axis_index(LINE)
    group = lax.axis_index(("x", "c"))
    inside = crop_table(crop_scale, crop_group, group, W_UNIT, cols)

    def same(offset):
        return jnp.tile(jnp.sum(inside * along(inside, offset, 0), axis=1), rows)[:, None]

    valid = same(0)
    count = jnp.sum(crop_scale).astype(full) * float(W_UNIT * rows * line)
    crops = float(crop_scale.shape[0])

    core = lax.axis_index("c")
    core_at = core.reshape(1).astype(jnp.int32)
    ratio = depth // width
    red_rows, mid_rows, exp_rows = (w.shape[0] // 2 for w in (w_reduce, w_middle, w_expand))
    red_own = half_of(w_reduce, 0, core)
    mid_own = half_of(w_middle.transpose(1, 0, 2), 1, core).reshape(9 * mid_rows, width)
    exp_own = half_of(w_expand, 0, core).reshape(exp_rows, ratio, width).transpose(1, 0, 2)
    rest_own = jnp.concatenate([mid_own, exp_own.reshape(ratio * exp_rows, width)], axis=0)
    block_own = jnp.concatenate([red_own, rest_own], axis=0)
    source = features.reshape(pixels, depth) * valid.astype(low)
    block_mine = lax.all_gather(block_own, LINE, axis=0, tiled=False)
    block_mine, source = lax.optimization_barrier((block_mine, source))
    block_other = flip(block_mine, [("c", 1)])
    if mid_rows % 16 == 0 and red_rows % 16 == 0:
        red_all = place_halves(block_mine, block_other, core_at, red_rows)
        mid_all, exp_all = place_block(
            block_mine, block_other, core_at, red_rows, mid_rows, exp_rows, ratio
        )
    else:
        block_all = both_halves(block_mine, block_other, core, 1)
        cuts = np.cumsum([0, red_rows, 9 * mid_rows, ratio * exp_rows])
        red_all, mid_all, exp_all = (block_all[:, :, cuts[i] : cuts[i + 1]] for i in range(3))
        red_all = red_all.reshape(depth, width)
        mid_all = mid_all.reshape(line, 2, 3, 3, mid_rows, width).transpose(2, 0, 1, 4, 3, 5)
        mid_all = mid_all.reshape(3 * width, 3 * width)
        exp_all = exp_all.reshape(line, 2, ratio, exp_rows, width).transpose(0, 1, 3, 2, 4)
        exp_all = exp_all.reshape(width, depth)
    terms, table = head_plan(rows)
    slots = table.shape[0]
    three = 3 * head
    by_term = w_heads.reshape(own, tasks, 3, 3, head).transpose(1, 2, 0, 3, 4)
    by_term = by_term.reshape(tasks, 3, own, three)
    parts = [by_term[t, 1] for t in range(tasks)] + [by_term[t, s + 1] for t, s, _ in terms]
    quarter = own // lax.axis_size(("x", "c"))
    heads_own = jnp.concatenate(
        [lax.dynamic_slice_in_dim(part, group * quarter, quarter, axis=0) for part in parts], axis=1
    )
    heads_own, block_mine = lax.optimization_barrier((heads_own, block_mine))
    heads_all = lax.all_gather(heads_own, AXES, axis=0, tiled=True)
    term_tasks = np.array([task for task, _, _ in terms], np.int32)
    picked_term = jnp.asarray(table)[:, place]
    slot_tasks = [sorted({int(term_tasks[e]) for e in table[s]}) for s in range(slots)]
    side_task = jnp.asarray(term_tasks)[picked_term]
    centers = jnp.arange(tasks, dtype=jnp.int32)
    all_tasks = jnp.concatenate([centers, side_task])
    all_picked = jnp.concatenate([centers, tasks + picked_term])

    reduced = dot(source, red_all)
    mean1, scale1 = norm_scale(reduced, count)
    normed1 = (reduced - mean1) * scale1
    out1 = normed1 * gain_reduce + bias_reduce
    hidden1 = (silu(out1) * valid).astype(low)
    edge = mid_rate * cols
    down = [(i, i + 1) for i in range(line - 1)]
    up = [(i + 1, i) for i in range(line - 1)]
    before1 = rows_to(hidden1[pixels - edge :], down)
    after1 = rows_to(hidden1[:edge], up)
    tall = jnp.concatenate([before1, hidden1, after1], axis=0)
    wide1 = jnp.concatenate([tall[i * edge : i * edge + pixels] for i in range(3)], axis=1)
    spread = dot(wide1, mid_all)
    mid_masks = [same((k - 1) * mid_rate) for k in range(3)]
    middled = sum(
        along(spread[:, k * width : (k + 1) * width], (k - 1) * mid_rate, 0) * mid_masks[k]
        for k in range(3)
    )
    mean2, scale2 = norm_scale(middled, count)
    normed2 = (middled - mean2) * scale2
    out2 = normed2 * gain_middle + bias_middle
    hidden2 = (silu(out2) * valid).astype(low)
    expanded = dot(hidden2, exp_all)
    mean3, scale3 = norm_scale(expanded, count)
    normed3 = (expanded - mean3) * scale3
    before = normed3 * gain_expand + bias_expand + source.astype(full)
    grid = (silu(before) * valid).astype(low)

    chips = lax.axis_size("x")
    chip = lax.axis_index("x")
    share = own // chips

    def share_columns(which):
        cuts = [f * own + which * share for f in range(line)]
        return jnp.concatenate(
            [lax.dynamic_slice_in_dim(grid, cut, share, axis=1) for cut in cuts], axis=1
        )

    grid_pieces = []
    for m in range(chips):
        piece = share_columns(chip ^ m)
        piece = flip(piece, [("x", m)]) if m else piece
        grid_pieces += [piece, flip(piece, [("c", 1)])]

    def mask_table(group):
        inside = crop_table(crop_scale, crop_group, group, W_UNIT, cols)
        columns = [
            jnp.sum(inside * along(inside, (k - 1) * rate, 0), axis=1)
            for rate in head_rates
            for k in range(3)
        ]
        table = jnp.pad(jnp.stack(columns, axis=1), ((0, 0), (0, 128 - 3 * tasks)))
        return jnp.tile(table, (rows, 1))

    masks = mask_table(group)
    moves = row_moves(terms, line)
    side_terms = head_terms(grid, heads_all, masks, tasks + picked_term, side_task, head, low)
    moved = [None] * tasks
    for task, pairs, members in moves:
        sends = {f: s for e, froms in members for f in froms for s in range(slots) if table[s, f] == e}
        sent = None
        for s in sorted(set(sends.values())):
            part = side_terms[:, s * head : (s + 1) * head]
            here = jnp.asarray(np.array([sends.get(f) == s for f in range(line)]))[place]
            sent = part if sent is None else jnp.where(here, part, sent)
        got = rows_to(sent, pairs).astype(full)
        moved[task] = got if moved[task] is None else moved[task] + got
    middle_terms = head_terms(grid, heads_all, masks, centers, centers, head, full)
    middle_terms, grid_pieces = lax.optimization_barrier((middle_terms, grid_pieces))
    mixed = []
    for task in range(tasks):
        center = middle_terms[:, task * head : (task + 1) * head]
        mixed.append(center if moved[task] is None else center + moved[task])
    mixed = jnp.concatenate(mixed, axis=1)
    gain_h, bias_h = gain_heads.reshape(-1), bias_heads.reshape(-1)
    mean_h, scale_h = norm_scale(mixed, count)
    normed_h = (mixed - mean_h) * scale_h
    out_h = normed_h * gain_h + bias_h
    activ = (silu(out_h) * valid).astype(low)
    marks = labels.reshape(tasks, pixels)
    class_part, class_bias_part, dactiv = [], [], []
    for task in range(tasks):
        act = activ[:, task * head : (task + 1) * head]
        logits = dot(act, w_class[task]) + b_class[task]
        onehot = (marks[task][:, None] == jnp.arange(classes, dtype=jnp.int32)[None, :]).astype(full)
        dlogits = ((jax.nn.softmax(logits, axis=-1) - onehot) * valid / crops).astype(low)
        class_part.append(dot_tn(dlogits, act))
        class_bias_part.append(jnp.sum(dlogits.astype(full), axis=0))
        dactiv.append(dot_nt(dlogits, w_class[task]))
    dout_h = jnp.concatenate(dactiv, axis=1) * valid * silu_slope(out_h)
    sums_h = all_sum(jnp.stack([jnp.sum(dout_h * normed_h, axis=0), jnp.sum(dout_h, axis=0)]))
    dgain_h, dbias_h = sums_h[0], sums_h[1]
    dmixed = valid * (gain_h * scale_h) * (dout_h - dbias_h / count - normed_h * (dgain_h / count))
    dmixed = dmixed.astype(low)

    class_sums = jnp.concatenate(
        [jnp.concatenate(class_part, axis=0), jnp.pad(jnp.stack(class_bias_part), ((0, 0), (0, head - classes)))],
        axis=0,
    )
    class_sums = class_sums + flip(class_sums, [("c", 1)])
    class_sums = sum_along(class_sums, "y")
    lane = head // 2
    tap_half = 3 * lane

    def half_taps(grads, which):
        cuts = [i * head + which * lane for i in range(grads.shape[1] // head)]
        return jnp.concatenate(
            [lax.dynamic_slice_in_dim(grads, cut, lane, axis=1) for cut in cuts], axis=1
        )

    def from_groups(grads):
        halves = [half_taps(grads, core), flip(half_taps(grads, 1 - core), [("c", 1)])]
        halves = jnp.concatenate(halves, axis=1)
        return [halves] + [flip(halves, [("x", m)]) for m in range(1, chips)]

    center_halves = from_groups(dmixed)
    all_masks = [masks, mask_table(group ^ 1)]
    for m in range(1, chips):
        all_masks += [mask_table((chip ^ m) * 2 + core), mask_table((chip ^ m) * 2 + 1 - core)]
    back = [None] * len(terms)
    for task, pairs, members in moves:
        got = rows_to(dmixed[:, task * head : (task + 1) * head], [(t, f) for f, t in pairs])
        for e, froms in members:
            here = jnp.asarray(np.array([f in froms for f in range(line)]))[place]
            back[e] = got if len(members) == 1 else jnp.where(here, got, jnp.zeros_like(got))
    dsides = []
    for s in range(slots):
        dside = back[table[s][0]]
        for e in sorted(set(table[s].tolist()) - {int(table[s][0])}):
            dside = jnp.where(picked_term[s] == e, back[e], dside)
        dsides.append(dside)
    vecs = jnp.pad(jnp.stack([mean3, scale3, gain_expand, bias_expand]), ((0, 4), (0, 0)))
    dys = spread_back(dmixed, masks, centers, head, pixels)
    *center_grads, slope3, normed3 = center_back(
        dys, heads_all, tasks, expanded, source, vecs, masks, 256
    )
    center_grads, slope3, normed3, turned, dsides, center_halves, class_sums = (
        lax.optimization_barrier(
            (
                center_grads,
                slope3,
                normed3,
                turn(grid_pieces),
                jnp.concatenate(dsides, axis=1),
                center_halves,
                class_sums,
            )
        )
    )
    class_sums = sum_along(class_sums, "z")
    side_halves = from_groups(dsides)
    dys = spread_back(dsides, masks, side_task, head, pixels)
    here = (side_task[:, None] == centers[None, :]).astype(full).reshape(-1)
    shared_grads, sums = side_back(
        dys, heads_all, tasks + picked_term, here, slot_tasks, tasks, center_grads, slope3, normed3, 256
    )
    sums, center_halves, side_halves, class_sums = lax.optimization_barrier(
        (sums, center_halves, side_halves, class_sums)
    )
    class_sums = sum_along(class_sums, "x")
    gram_part = jnp.sum(sums[2 * tasks : 4 * tasks], axis=1)
    gram_row = jnp.pad(gram_part, (0, depth - gram_part.shape[0]))[None, :]
    summed = all_sum(jnp.concatenate([sums[: 2 * tasks], gram_row], axis=0))
    sums3 = summed[: 2 * tasks].reshape(tasks, 2, depth)
    weight_list = task_scales([summed[2 * tasks, i] for i in range(6)])
    task_weights = jnp.stack(weight_list)

    slot_of = jnp.full((len(terms),), -1, jnp.int32)
    for s in range(slots):
        slot_of = jnp.where(jnp.arange(len(terms)) == picked_term[s], tasks + s, slot_of)
    slot_of = jnp.concatenate([centers, slot_of])
    head_part = weight_grad(
        turned, center_halves, side_halves, all_masks, slot_of, side_task, slot_tasks, tasks
    )
    shared_grads, head_part = lax.optimization_barrier((shared_grads, head_part))
    head_part = head_part.reshape(line, share, len(parts) * tap_half)
    head_own = lax.psum_scatter(head_part, LINE, scatter_dimension=0, tiled=False)

    dgain3, dbias3 = (
        sum(weight_list[t] * sums3[t, j] for t in range(tasks)) for j in range(2)
    )
    vec_rows = [gain_expand * scale3, jnp.broadcast_to(1.0 / count, (depth,))]
    vecs = jnp.pad(jnp.stack(vec_rows), ((0, 6), (0, 0)))
    mid_vecs = jnp.pad(jnp.stack([mean2, scale2, gain_middle, bias_middle]), ((0, 4), (0, 0)))
    dbefore, exp_part, dout2, sums2 = expand_back(
        summed, shared_grads, slope3, normed3, vecs, masks, hidden2, exp_all, middled,
        mid_vecs, 256,
    )
    sums2 = all_sum(sums2[:2])
    dgain2, dbias2 = sums2[0], sums2[1]
    dmiddled = valid * (gain_middle * scale2) * (
        dout2 - dbias2 / count - normed2 * (dgain2 / count)
    )
    dmiddled = dmiddled.astype(low)
    dspread = jnp.concatenate(
        [along(dmiddled * mid_masks[k].astype(low), -(k - 1) * mid_rate, 0) for k in range(3)],
        axis=1,
    )
    dwide = dot_nt(dspread, mid_all)
    from_below = rows_to(dwide[:edge, :width].astype(low), up).astype(full)
    from_above = rows_to(dwide[pixels - edge :, 2 * width :].astype(low), down).astype(full)
    dspread, exp_part, dwide = lax.optimization_barrier((dspread, exp_part, dwide))
    mid_part = dot_tn(wide1, dspread).astype(low).reshape(3, line, 2, mid_rows, 3 * width)
    exp_part = exp_part.reshape(line, 2, exp_rows, depth)

    def later_half(which):
        mid_half = lax.dynamic_index_in_dim(mid_part, which, 2, keepdims=False)
        exp_half = lax.dynamic_index_in_dim(exp_part, which, 1, keepdims=False)
        pieces = [
            mid_half[i, :, :, k * width : (k + 1) * width] for i in range(3) for k in range(3)
        ]
        pieces += [exp_half[:, :, k * width : (k + 1) * width] for k in range(ratio)]
        return jnp.concatenate(pieces, axis=1)

    later_other = flip(later_half(1 - core), [("c", 1)])
    later = (later_half(core).astype(full) + later_other.astype(full)).astype(low)
    dhidden1 = (
        dwide[:, width : 2 * width]
        + jnp.concatenate([dwide[edge:, :width], from_below], axis=0)
        + jnp.concatenate([from_above, dwide[: pixels - edge, 2 * width :]], axis=0)
    )
    dout1 = dhidden1 * valid * silu_slope(out1)
    sums1 = all_sum(jnp.stack([jnp.sum(dout1 * normed1, axis=0), jnp.sum(dout1, axis=0)]))
    sums1, later = lax.optimization_barrier((sums1, later))
    cut = later.shape[1] // 64 * 32
    first, second = scatter_x(later[:, :cut], 1), scatter_x(later[:, cut:], 1)
    second, head_own = lax.optimization_barrier((second, head_own))
    head_shares = [head_own] + [flip(head_own, [("x", m)]) for m in range(1, chips)]
    head_others = [flip(part, [("c", 1)]) for part in head_shares]
    later_own = [scatter_z(scatter_y(piece)) for piece in (first, second)]
    dgain1, dbias1 = sums1[0], sums1[1]
    dreduced = valid * (gain_reduce * scale1) * (
        dout1 - dbias1 / count - normed1 * (dgain1 / count)
    )
    dreduced = dreduced.astype(low)
    dfeatures = dbefore.astype(full) + dot_nt(dreduced, red_all)

    red_part = dot_tn(source, dreduced).astype(low).reshape(line, -1, width)
    red_sum = over_groups(scatter_z(scatter_y(between_cores(red_part))))
    red_sum = both_halves(*red_sum, core, 0).astype(full)
    part_of = np.full((tasks, 3), -1, np.int32)
    part_of[:, 1] = np.arange(tasks)
    for e, (task, side, _) in enumerate(terms):
        part_of[task, side + 1] = tasks + e
    head_shares, head_others, later_own = lax.optimization_barrier(
        (head_shares, head_others, later_own)
    )
    at = jnp.stack([chip, core]).astype(jnp.int32)
    heads_out = place_shares(head_shares, head_others, jnp.asarray(part_of.reshape(-1)), at, head)
    heads_out = heads_out.reshape(tasks, 9, own, head).transpose(2, 0, 1, 3)
    later_own = jnp.concatenate([gather_x(piece) for piece in later_own], axis=0)
    later_other = flip(later_own, [("c", 1)])
    later_sum = both_halves(
        later_own.reshape(9 + ratio, mid_rows, width),
        later_other.reshape(9 + ratio, mid_rows, width),
        core,
        1,
    ).reshape(9 + ratio, 2 * mid_rows, width)
    mid_sum = later_sum[:9].transpose(1, 0, 2).astype(full)
    exp_sum = later_sum[9:].transpose(1, 0, 2).reshape(2 * exp_rows, depth).astype(full)
    grad_class = class_sums[: tasks * classes].reshape(tasks, classes, head).transpose(0, 2, 1)
    grad_class_bias = class_sums[tasks * classes :, :classes]
    return (
        dfeatures.reshape(1, rows, cols, depth),
        red_sum.reshape(w_reduce.shape),
        mid_sum,
        exp_sum,
        heads_out,
        dgain1,
        dbias1,
        dgain2,
        dbias2,
        dgain3,
        dbias3,
        dgain_h.reshape(tasks, head),
        dbias_h.reshape(tasks, head),
        grad_class,
        grad_class_bias,
        task_weights,
    )


def solution(mesh):
    line, groups = mesh.shape["fsdp"], mesh.shape["dp"]
    fine = Mesh(mesh.devices.reshape(line // 2, 2, groups // 2, 2), AXES)
    dp = ("x", "c")
    rows = P(LINE)
    in_specs = (
        P(dp, LINE, None, None),
        P(),
        P(),
        P(None, dp, LINE, None),
        rows,
        P(),
        P(),
        rows,
        P(),
        P(),
        rows,
        P(),
        P(),
        rows,
        P(),
        P(),
        P(),
        P(),
    )
    out_specs = (P(dp, LINE, None, None),) + (rows,) * 4 + (P(),) * 11
    return jax.shard_map(
        on_device, mesh=fine, in_specs=in_specs, out_specs=out_specs, check_vma=False
    )
```

```python
import itertools

import jax
import jax.numpy as jnp
import numpy as np
from jax import lax
from jax.experimental import pallas as pl
from jax.experimental.pallas import tpu as pltpu
from jax.sharding import Mesh
from jax.sharding import PartitionSpec as P

W_UNIT = 12


eps = 1e-05
mid_rate = 2
head_rates = (12, 24, 36)
AXES = ("z", "y", "x", "c")
LINE = ("z", "y")
low = jnp.bfloat16
full = jnp.float32


def coords(names):
    return list(itertools.product(*[range(lax.axis_size(name)) for name in names]))


def flip(value, moves):
    moves = sorted([m for m in moves if m[1]], key=lambda move: AXES.index(move[0]))
    names = tuple(name for name, _ in moves)
    places = coords(names)
    index = {place: i for i, place in enumerate(places)}
    pairs = [
        (i, index[tuple(at ^ bit for at, (_, bit) in zip(place, moves))])
        for i, place in enumerate(places)
    ]
    return lax.ppermute(value, names, pairs)


def all_sum(value):
    moves = []
    for name in ("y", "x", "z"):
        bit = 1
        while bit < lax.axis_size(name):
            moves.append((name, bit))
            bit *= 2
    value = value + flip(value, [("c", 1)])
    while moves:
        if len(moves) == 1:
            value = value + flip(value, moves)
            break
        first, second = moves[:2]
        moves = moves[2:]
        both = [(first[0], first[1] | second[1])] if first[0] == second[0] else [first, second]
        one, two, three = flip(value, [first]), flip(value, [second]), flip(value, both)
        value = (value + one) + (two + three)
    return value


def sum_along(value, name):
    bit = 1
    while bit < lax.axis_size(name):
        value = value + flip(value, [(name, bit)])
        bit *= 2
    return value


def rows_to(value, pairs):
    if not pairs:
        return jnp.zeros_like(value)
    return lax.ppermute(value, LINE, pairs)


def line_size():
    return lax.axis_size("z") * lax.axis_size("y")


def half_of(value, axis, core):
    size = value.shape[axis] // 2
    return lax.dynamic_slice_in_dim(value, core * size, size, axis=axis)


def both_halves(mine, other, core, axis):
    first = jnp.where(core == 0, mine, other)
    second = jnp.where(core == 0, other, mine)
    return jnp.stack([first, second], axis=axis)


def between_cores(partial):
    core = lax.axis_index("c")
    mine = half_of(partial, 1, core)
    other = flip(half_of(partial, 1, 1 - core), [("c", 1)])
    return (mine.astype(full) + other.astype(full)).astype(low)


def over_groups(own):
    bit = 1
    while bit < lax.axis_size("x"):
        own = (own.astype(full) + flip(own, [("x", bit)]).astype(full)).astype(low)
        bit *= 2
    return own, flip(own, [("c", 1)])


def scatter_y(partial):
    parts = partial.reshape(-1, 2, *partial.shape[1:])
    here = lax.axis_index("y")
    mine = lax.dynamic_index_in_dim(parts, here, 1, keepdims=False)
    other = lax.dynamic_index_in_dim(parts, 1 - here, 1, keepdims=False)
    return (mine.astype(full) + flip(other, [("y", 1)]).astype(full)).astype(low)


def scatter_x(partial, axis):
    chips, here = lax.axis_size("x"), lax.axis_index("x")
    size = partial.shape[axis] // chips
    total = lax.dynamic_slice_in_dim(partial, here * size, size, axis).astype(full)
    for m in range(1, chips):
        part = lax.dynamic_slice_in_dim(partial, (here ^ m) * size, size, axis)
        total = total + flip(part, [("x", m)]).astype(full)
    return total.astype(low)


def gather_x(own):
    chips, here = lax.axis_size("x"), lax.axis_index("x")
    parts = jnp.stack([own] + [flip(own, [("x", m)]) for m in range(1, chips)])
    ordered = [lax.dynamic_index_in_dim(parts, here ^ m, 0, keepdims=False) for m in range(chips)]
    return jnp.concatenate(ordered, axis=0)


def scatter_z(parts):
    here = lax.axis_index("z")
    total = lax.dynamic_index_in_dim(parts, here, 0, keepdims=False).astype(full)
    for m in range(1, lax.axis_size("z")):
        part = lax.dynamic_index_in_dim(parts, here ^ m, 0, keepdims=False)
        total = total + flip(part, [("z", m)]).astype(full)
    return total.astype(low)


def along(value, offset, axis):
    size = value.shape[axis]
    if offset == 0:
        return value
    widths = [(0, 0)] * value.ndim
    if offset > 0:
        widths[axis] = (0, offset)
        return lax.slice_in_dim(jnp.pad(value, widths), offset, offset + size, axis=axis)
    widths[axis] = (-offset, 0)
    return lax.slice_in_dim(jnp.pad(value, widths), 0, size, axis=axis)


def crop_table(crop_scale, crop_group, group, unit, cols):
    mine = (crop_group == group).astype(jnp.int32)
    widths = crop_scale * unit * mine
    ends = jnp.cumsum(widths)
    starts = ends - widths
    column = jnp.arange(cols, dtype=jnp.int32)[:, None]
    return ((column >= starts[None, :]) & (column < ends[None, :])).astype(full)


def silu(value):
    return value * (0.5 + 0.5 * jnp.tanh(0.5 * value))


def silu_slope(value):
    turn = jnp.tanh(0.5 * value)
    return 0.5 + 0.5 * turn + 0.25 * value * (1.0 - turn * turn)


def norm_scale(value, count):
    sums = all_sum(jnp.stack([jnp.sum(value, axis=0), jnp.sum(value * value, axis=0)]))
    mean = sums[0] / count
    return mean, lax.rsqrt(sums[1] / count - mean * mean + eps)


def head_plan(rows):
    line = line_size()
    terms = []
    for task, rate in enumerate(head_rates):
        hop = rate // rows
        for side in (-1, 1):
            if hop < line:
                terms.append((task, side, hop))
    last = lax.axis_size("y")
    planes = []
    for z in range(lax.axis_size("z")):
        need = []
        for e, (task, side, hop) in enumerate(terms):
            if any(0 <= z * last + y - side * hop < line for y in range(last)):
                need.append(e)
        planes.append(need)
    slots = max(len(need) for need in planes)
    table = np.zeros((slots, line), np.int32)
    for z, need in enumerate(planes):
        rest = [e for e in range(len(terms)) if e not in need]
        for s, e in enumerate((need + rest)[:slots]):
            table[s, z * last : (z + 1) * last] = e
    return terms, table


def row_moves(terms, line):
    moves = []
    for e, (task, side, hop) in enumerate(terms):
        pairs = [(f, f - side * hop) for f in range(line) if 0 <= f - side * hop < line]
        last = moves[-1] if moves else None
        if last and last[0] == task and not {t for _, t in last[1]} & {t for _, t in pairs}:
            if not {f for f, _ in last[1]} & {f for f, _ in pairs}:
                last[1].extend(pairs)
                last[2].append((e, [f for f, _ in pairs]))
                continue
        moves.append((task, pairs, [(e, [f for f, _ in pairs])]))
    return moves


def task_scales(products):
    g00, g01, g02, g11, g12, g22 = products
    n0, n1, n2 = (jnp.sqrt(g + 1e-12) for g in (g00, g11, g22))
    c00, c11, c22 = (g / (n * n) + 0.1 for g, n in ((g00, n0), (g11, n1), (g22, n2)))
    c01, c02, c12 = g01 / (n0 * n1), g02 / (n0 * n2), g12 / (n1 * n2)
    w0 = (c11 * c22 - c12 * c12) + (c12 * c02 - c01 * c22) + (c01 * c12 - c11 * c02)
    w1 = (c12 * c02 - c22 * c01) + (c22 * c00 - c02 * c02) + (c02 * c01 - c12 * c00)
    w2 = (c01 * c12 - c02 * c11) + (c02 * c01 - c00 * c12) + (c00 * c11 - c01 * c01)
    top = n0 + n1 + n2
    total = w0 + w1 + w2
    return [w * top / (n * total) for w, n in ((w0, n0), (w1, n1), (w2, n2))]


def dot(a, b):
    return jnp.dot(a, b, preferred_element_type=full)


def dot_nt(a, b):
    return lax.dot_general(a, b, (((1,), (1,)), ((), ())), preferred_element_type=full)


def dot_tn(a, b):
    return lax.dot_general(a, b, (((0,), (0,)), ((), ())), preferred_element_type=full)


def spec(shape, index):
    return pl.BlockSpec(shape, index)


def params(mib=56):
    return pltpu.CompilerParams(vmem_limit_bytes=mib * 2**20)


def cost(flops, moved):
    return pl.CostEstimate(flops=flops, bytes_accessed=moved, transcendentals=0)


def terms_kernel(picked_ref, task_ref, x_ref, w_ref, mask_ref, out_ref):
    at = pl.program_id(0)
    pixels, head = out_ref.shape

    def product(k):
        return jnp.dot(
            x_ref[...], w_ref[:, k * head : (k + 1) * head], preferred_element_type=full
        )

    for task, rate in enumerate(head_rates):

        @pl.when(task_ref[at] == task)
        def _():
            left = pltpu.roll(product(0), rate, 0) * mask_ref[:, 3 * task : 3 * task + 1]
            right = pltpu.roll(product(2), pixels - rate, 0)
            right = right * mask_ref[:, 3 * task + 2 : 3 * task + 3]
            out_ref[...] = (product(1) + left + right).astype(out_ref.dtype)


def head_terms(grid, heads_all, masks, picked, task_of, head, dtype):
    pixels, depth = grid.shape
    items = picked.shape[0]
    return pl.pallas_call(
        terms_kernel,
        out_shape=jax.ShapeDtypeStruct((pixels, items * head), dtype),
        grid_spec=pltpu.PrefetchScalarGridSpec(
            num_scalar_prefetch=2,
            grid=(items,),
            in_specs=[
                spec((pixels, depth), lambda i, p, t: (0, 0)),
                spec((depth, 3 * head), lambda i, p, t: (0, p[i])),
                spec(masks.shape, lambda i, p, t: (0, 0)),
            ],
            out_specs=spec((pixels, head), lambda i, p, t: (0, i)),
        ),
        compiler_params=params(),
        cost_estimate=cost(
            2 * pixels * depth * 3 * head * items, 2 * items * depth * 3 * head + 2 * pixels * depth
        ),
    )(picked, task_of, grid, heads_all, masks)


def spread_kernel(task_ref, d_ref, mask_ref, out_ref):
    at = pl.program_id(1)
    pixels, head = d_ref.shape
    for task, rate in enumerate(head_rates):

        @pl.when(task_ref[at] == task)
        def _():
            grad = d_ref[...].astype(full)
            out_ref[:, head : 2 * head] = d_ref[...]
            for k, shift in ((0, pixels - rate), (2, rate)):
                piece = grad * mask_ref[:, 3 * task + k : 3 * task + k + 1]
                out_ref[:, k * head : (k + 1) * head] = pltpu.roll(piece, shift, 0).astype(low)


def spread_back(grads, masks, task_of, head, pixels):
    rows = grads.shape[0]
    items = grads.shape[1] // head
    return pl.pallas_call(
        spread_kernel,
        out_shape=jax.ShapeDtypeStruct((rows, 3 * head * items), low),
        grid_spec=pltpu.PrefetchScalarGridSpec(
            num_scalar_prefetch=1,
            grid=(rows // pixels, items),
            in_specs=[
                spec((pixels, head), lambda j, i, t: (j, i)),
                spec((pixels, masks.shape[1]), lambda j, i, t: (j, 0)),
            ],
            out_specs=spec((pixels, 3 * head), lambda j, i, t: (j, i)),
        ),
        compiler_params=params(),
        cost_estimate=cost(30 * rows * head * items, 8 * rows * head * items),
    )(task_of, grads, masks)


def center_back_kernel(tasks, *refs):
    dy_ref = refs[0]
    w_refs = refs[1 : 1 + tasks]
    wide_ref, source_ref, vec_ref, mask_ref = refs[1 + tasks : 5 + tasks]
    out_refs = refs[5 + tasks : -2]
    slope_ref, normed_ref = refs[-2:]
    three = w_refs[0].shape[1]
    pixels = dy_ref.shape[0]
    for at in range(0, pixels, pixels // 3):
        rows = slice(at, at + pixels // 3)
        for t in range(tasks):
            out_refs[t][rows, :] = lax.dot_general(
                dy_ref[rows, t * three : (t + 1) * three],
                w_refs[t][...],
                (((1,), (1,)), ((), ())),
                preferred_element_type=full,
            ).astype(low)
        normed = (wide_ref[rows, :].astype(full) - vec_ref[0:1]) * vec_ref[1:2]
        value = normed * vec_ref[2:3] + vec_ref[3:4] + source_ref[rows, :].astype(full)
        slope_ref[rows, :] = (silu_slope(value) * mask_ref[rows, 1:2]).astype(low)
        normed_ref[rows, :] = normed.astype(low)


def center_back(dys, heads_all, tasks, wide, source, vecs, masks, block):
    pixels, depth = wide.shape
    three = dys.shape[1] // tasks
    column = lambda j: (0, j)
    fixed = lambda j: (0, 0)
    return pl.pallas_call(
        lambda *refs: center_back_kernel(tasks, *refs),
        out_shape=[jax.ShapeDtypeStruct((pixels, depth), low)] * (tasks + 2),
        grid=(depth // block,),
        in_specs=[spec(dys.shape, fixed)]
        + [spec((block, three), lambda j, i=i: (j, i)) for i in range(tasks)]
        + [spec((pixels, block), column)] * 2
        + [spec((8, block), column), spec(masks.shape, fixed)],
        out_specs=[spec((pixels, block), column)] * (tasks + 2),
        compiler_params=params(),
        cost_estimate=cost(2 * pixels * depth * three * tasks, 16 * pixels * depth),
    )(dys, *([heads_all] * tasks), wide, source, vecs, masks)


def side_back_kernel(tasks, side_tasks, touched, *refs):
    slots = len(side_tasks)
    here_ref, dy_ref = refs[1:3]
    w_refs = refs[3 : 3 + slots]
    held_refs = refs[3 + slots : 3 + slots + tasks]
    slope_ref, normed_ref = refs[3 + slots + tasks : 5 + slots + tasks]
    out_refs = refs[5 + slots + tasks : -1]
    sums_ref = refs[-1]
    pixels = dy_ref.shape[0]
    totals = None
    for at in range(0, pixels, pixels // 3):
        rows = slice(at, at + pixels // 3)
        grads = [ref[rows, :].astype(full) for ref in held_refs]
        for s, choices in enumerate(side_tasks):
            three = w_refs[s].shape[1]
            side = lax.dot_general(
                dy_ref[rows, s * three : (s + 1) * three],
                w_refs[s][...],
                (((1,), (1,)), ((), ())),
                preferred_element_type=full,
            )
            for t in choices:
                more = side if len(choices) == 1 else side * here_ref[s * tasks + t]
                grads[t] = grads[t] + more
        slope, normed = slope_ref[rows, :].astype(full), normed_ref[rows, :].astype(full)
        parts = []
        for t in range(tasks):
            part = grads[t] * slope
            parts += [jnp.sum(part * normed, axis=0), jnp.sum(part, axis=0)]
        for t in range(tasks):
            for u in range(t, tasks):
                parts.append(jnp.sum(grads[t] * grads[u], axis=0))
        for i, t in enumerate(touched):
            out_refs[i][rows, :] = grads[t].astype(low)
        totals = parts if totals is None else [a + b for a, b in zip(totals, parts)]
    sums_ref[...] = jnp.zeros_like(sums_ref)
    for i, row in enumerate(totals):
        sums_ref[i, :] = row


def side_back(dys, heads_all, picked, here, side_tasks, tasks, held, slope, normed, block):
    pixels, depth = slope.shape
    slots = len(side_tasks)
    three = dys.shape[1] // slots
    touched = sorted({t for choices in side_tasks for t in choices})
    column = lambda j, p, h: (0, j)
    *outs, sums = pl.pallas_call(
        lambda *refs: side_back_kernel(tasks, side_tasks, touched, *refs),
        out_shape=[jax.ShapeDtypeStruct((pixels, depth), low)] * len(touched)
        + [jax.ShapeDtypeStruct((16, depth), full)],
        grid_spec=pltpu.PrefetchScalarGridSpec(
            num_scalar_prefetch=2,
            grid=(depth // block,),
            in_specs=[spec(dys.shape, lambda j, p, h: (0, 0))]
            + [spec((block, three), lambda j, p, h, i=i: (j, p[i])) for i in range(slots)]
            + [spec((pixels, block), column)] * (tasks + 2),
            out_specs=[spec((pixels, block), column)] * len(touched) + [spec((16, block), column)],
        ),
        compiler_params=params(),
        cost_estimate=cost(2 * pixels * depth * three * slots, 14 * pixels * depth),
    )(picked, here, dys, *([heads_all] * slots), *held, slope, normed)
    return [outs[touched.index(t)] if t in touched else held[t] for t in range(tasks)], sums


def expand_back_kernel(tasks, blocks, *refs):
    gram_ref, sum_ref = refs[0], refs[1 + tasks]
    grad_refs = refs[1 : 1 + tasks]
    slope_ref, normed_ref, vec_ref, mask_ref, hidden_ref, w_ref, mid_ref, mid_vec_ref = refs[
        2 + tasks : 10 + tasks
    ]
    dbefore_ref, dweight_ref, dout_ref, sums_ref, total_ref, turned_ref, scale_ref = refs[
        10 + tasks :
    ]
    at = pl.program_id(0)

    @pl.when(at == 0)
    def _():
        turned_ref[...] = hidden_ref[...].T
        gram = 2 * tasks
        scales = task_scales([gram_ref[gram : gram + 1, i : i + 1] for i in range(6)])
        for t in range(tasks):
            scale_ref[t : t + 1, :] = jnp.broadcast_to(scales[t], (1, scale_ref.shape[1]))

    weights = [scale_ref[t : t + 1, :] for t in range(tasks)]
    combined = grad_refs[0][...].astype(full) * weights[0]
    dgain = sum_ref[0:1] * weights[0]
    dbias = sum_ref[1:2] * weights[0]
    for t in range(1, tasks):
        combined = combined + grad_refs[t][...].astype(full) * weights[t]
        dgain = dgain + sum_ref[2 * t : 2 * t + 1] * weights[t]
        dbias = dbias + sum_ref[2 * t + 1 : 2 * t + 2] * weights[t]
    normed = normed_ref[...].astype(full)
    valid = mask_ref[:, 1:2]
    dbefore = combined * slope_ref[...].astype(full)
    dbefore_ref[...] = dbefore.astype(low)
    per = vec_ref[1:2]
    dwide = (dbefore - dbias * per - normed * (dgain * per)) * vec_ref[0:1] * valid
    dwide = dwide.astype(low)
    dweight_ref[...] = jnp.dot(turned_ref[...], dwide, preferred_element_type=full).astype(low)
    part = lax.dot_general(
        dwide, w_ref[...], (((1,), (1,)), ((), ())), preferred_element_type=full
    )

    @pl.when(at == 0)
    def _():
        total_ref[...] = part

    @pl.when(at > 0)
    def _():
        total_ref[...] += part

    @pl.when(at == blocks - 1)
    def _():
        mid = (mid_ref[...] - mid_vec_ref[0:1]) * mid_vec_ref[1:2]
        dout = total_ref[...] * silu_slope(mid * mid_vec_ref[2:3] + mid_vec_ref[3:4]) * valid
        dout_ref[...] = dout
        sums_ref[...] = jnp.zeros_like(sums_ref)
        sums_ref[0, :] = jnp.sum(dout * mid, axis=0)
        sums_ref[1, :] = jnp.sum(dout, axis=0)


def expand_back(summed, grads, slope, normed, vecs, masks, hidden, weight, mid, mid_vecs, block):
    pixels, depth = slope.shape
    width = hidden.shape[1]
    tasks = len(grads)
    column = lambda j: (0, j)
    fixed = lambda j: (0, 0)
    blocks = depth // block
    return pl.pallas_call(
        lambda *refs: expand_back_kernel(tasks, blocks, *refs),
        out_shape=[
            jax.ShapeDtypeStruct((pixels, depth), low),
            jax.ShapeDtypeStruct((width, depth), low),
            jax.ShapeDtypeStruct((pixels, width), full),
            jax.ShapeDtypeStruct((8, width), full),
        ],
        grid_spec=pltpu.PrefetchScalarGridSpec(
            num_scalar_prefetch=0,
            grid=(blocks,),
            in_specs=[spec((summed.shape[0], 128), fixed)]
            + [spec((pixels, block), column)] * tasks
            + [spec((summed.shape[0], block), column)]
            + [spec((pixels, block), column)] * 2
            + [
                spec((8, block), column),
                spec(masks.shape, fixed),
                spec((pixels, width), fixed),
                spec((width, block), column),
                spec((pixels, width), fixed),
                spec((8, width), fixed),
            ],
            out_specs=[
                spec((pixels, block), column),
                spec((width, block), column),
                spec((pixels, width), fixed),
                spec((8, width), fixed),
            ],
            scratch_shapes=[
                pltpu.VMEM((pixels, width), full),
                pltpu.VMEM((width, pixels), low),
                pltpu.VMEM((8, block), full),
            ],
        ),
        compiler_params=params(),
        cost_estimate=cost(4 * pixels * width, 14 * pixels),
    )(summed, *grads, summed, slope, normed, vecs, masks, hidden, weight, mid, mid_vecs)


def turn_kernel(*refs):
    out_ref = refs[-1]
    pixels = refs[0].shape[0]
    for i, ref in enumerate(refs[:-1]):
        out_ref[:, i * pixels : (i + 1) * pixels] = ref[...].T


def turn(pieces):
    pixels, depth = pieces[0].shape
    block = min(depth, 512)
    return pl.pallas_call(
        turn_kernel,
        out_shape=jax.ShapeDtypeStruct((depth, len(pieces) * pixels), low),
        grid=(depth // block,),
        in_specs=[spec((pixels, block), lambda i: (0, i))] * len(pieces),
        out_specs=spec((block, len(pieces) * pixels), lambda i: (i, 0)),
        compiler_params=params(),
        cost_estimate=cost(0, 4 * len(pieces) * pixels * depth),
    )(*pieces)


def weight_grad_kernel(members, side_tasks, tasks, groups, *refs):
    slot_ref, task_ref, x_ref = refs[:3]
    chips = groups // 2
    center_refs, side_refs = refs[3 : 3 + chips], refs[3 + chips : 3 + groups]
    mask_refs = refs[3 + groups : 3 + 2 * groups]
    out_ref, dy_ref, total_ref = refs[3 + 2 * groups :]
    pixels = center_refs[0].shape[0]
    lane = center_refs[0].shape[1] // (2 * tasks)
    slots = len(side_tasks)
    three = 3 * lane

    def spread(j, i, grad_ref, at, task):
        rows = slice(j * pixels, (j + 1) * pixels)
        held = grad_ref[:, at * lane : (at + 1) * lane]
        dy_ref[rows, i * three + lane : i * three + 2 * lane] = held
        rate = head_rates[task]
        for k, shift in ((0, pixels - rate), (2, rate)):
            piece = held.astype(full) * mask_refs[j][:, 3 * task + k : 3 * task + k + 1]
            columns = slice(i * three + k * lane, i * three + (k + 1) * lane)
            dy_ref[rows, columns] = pltpu.roll(piece, shift, 0).astype(low)

    @pl.when(pl.program_id(0) == 0)
    def _():
        for j in range(groups):
            for i, item in enumerate(members):
                if item < tasks:
                    spread(j, i, center_refs[j // 2], j % 2 * tasks + item, item)
                    continue
                at = item - tasks
                for task in side_tasks[at]:
                    move = lambda j=j, i=i, at=at, task=task: spread(
                        j, i, side_refs[j // 2], j % 2 * slots + at, task
                    )
                    if len(side_tasks[at]) == 1:
                        move()
                    else:
                        pl.when(task_ref[at] == task)(move)

    total_ref[...] = jnp.dot(x_ref[...], dy_ref[...], preferred_element_type=full)
    for g in range(out_ref.shape[1] // three):
        columns = slice(g * three, (g + 1) * three)

        @pl.when(slot_ref[g] >= 0)
        def _():
            start = pl.multiple_of(slot_ref[g] * three, 128)
            out_ref[:, columns] = total_ref[:, pl.ds(start, three)].astype(low)

        @pl.when(slot_ref[g] < 0)
        def _():
            out_ref[:, columns] = jnp.zeros((out_ref.shape[0], three), low)


def weight_grad(turned, centers, sides, masks, slot_of, side_task, side_tasks, tasks):
    three = 3 * centers[0].shape[1] // (2 * tasks)
    items = tasks + len(side_tasks)
    few = max(1, 2**24 // (turned.shape[1] * three * 2))
    total = None
    for start in range(0, items, few):
        members = list(range(start, min(start + few, items)))
        here = (slot_of >= start) & (slot_of < start + few)
        slots = jnp.where(here, slot_of - start, -1)
        part = some_weight_grad(
            turned, centers, sides, masks, slots, side_task, side_tasks, tasks, members
        )
        total = part if total is None else total + part
    return total


def some_weight_grad(
    turned, centers, sides, masks, slot_of, side_task, side_tasks, tasks, members
):
    depth, pixels = turned.shape
    groups = len(masks)
    parts = slot_of.shape[0]
    three = 3 * centers[0].shape[1] // (2 * tasks)
    items = len(members)
    block = min(depth, 512)
    fixed = lambda g, s, t: (0, 0)
    return pl.pallas_call(
        lambda *refs: weight_grad_kernel(members, side_tasks, tasks, groups, *refs),
        out_shape=jax.ShapeDtypeStruct((depth, parts * three), low),
        grid_spec=pltpu.PrefetchScalarGridSpec(
            num_scalar_prefetch=2,
            grid=(depth // block,),
            in_specs=[spec((block, pixels), lambda g, s, t: (g, 0))]
            + [spec(array.shape, fixed) for array in (*centers, *sides, *masks)],
            out_specs=spec((block, parts * three), lambda g, s, t: (g, 0)),
            scratch_shapes=[
                pltpu.VMEM((pixels, items * three), low),
                pltpu.VMEM((block, items * three), full),
            ],
        ),
        compiler_params=params(),
        cost_estimate=cost(
            2 * pixels * depth * items * three, 2 * depth * (pixels + parts * three)
        ),
    )(slot_of, side_task, turned, *centers, *sides, *masks)


def place_halves_kernel(core_ref, mine_ref, other_ref, out_ref):
    parts, half, _ = mine_ref.shape
    for i in range(parts):
        for ref, which in ((mine_ref, core_ref[0]), (other_ref, 1 - core_ref[0])):
            row = pl.multiple_of((2 * i + which) * half, half)
            out_ref[pl.ds(row, half), :] = ref[i]


def place_halves(mine, other, core, half):
    parts, _, width = mine.shape
    fixed = lambda i, c: (0, 0, 0)
    return pl.pallas_call(
        place_halves_kernel,
        out_shape=jax.ShapeDtypeStruct((parts * 2 * half, width), low),
        grid_spec=pltpu.PrefetchScalarGridSpec(
            num_scalar_prefetch=1,
            grid=(1,),
            in_specs=[spec((parts, half, width), fixed)] * 2,
            out_specs=spec((parts * 2 * half, width), lambda i, c: (0, 0)),
        ),
        compiler_params=params(),
        cost_estimate=cost(0, 8 * parts * half * width),
    )(core, mine, other)


def place_block_kernel(
    red_rows, mid_rows, exp_rows, ratio, core_ref, mine_ref, other_ref, mid_ref, exp_ref
):
    width = mid_ref.shape[0] // 3
    for i in range(mine_ref.shape[0]):
        for ref, which in ((mine_ref, core_ref[0]), (other_ref, 1 - core_ref[0])):
            row = pl.multiple_of((2 * i + which) * mid_rows, mid_rows)
            for tap in range(9):
                ir, ic = divmod(tap, 3)
                at = red_rows + tap * mid_rows
                mid_ref[pl.ds(ir * width + row, mid_rows), ic * width : (ic + 1) * width] = ref[
                    i, at : at + mid_rows
                ]
            row = pl.multiple_of((2 * i + which) * exp_rows, exp_rows)
            for part in range(ratio):
                at = red_rows + 9 * mid_rows + part * exp_rows
                exp_ref[pl.ds(row, exp_rows), part * width : (part + 1) * width] = ref[
                    i, at : at + exp_rows
                ]


def place_block(mine, other, core, red_rows, mid_rows, exp_rows, ratio):
    width = mine.shape[2]
    fixed = lambda i, c: (0, 0, 0)
    flat = lambda i, c: (0, 0)
    shapes = [(3 * width, 3 * width), (width, ratio * width)]
    return pl.pallas_call(
        lambda *refs: place_block_kernel(red_rows, mid_rows, exp_rows, ratio, *refs),
        out_shape=[jax.ShapeDtypeStruct(shape, low) for shape in shapes],
        grid_spec=pltpu.PrefetchScalarGridSpec(
            num_scalar_prefetch=1,
            grid=(1,),
            in_specs=[spec(mine.shape, fixed)] * 2,
            out_specs=[spec(shape, flat) for shape in shapes],
        ),
        compiler_params=params(),
        cost_estimate=cost(0, 8 * mine.size),
    )(core, mine, other)


def place_kernel(chips, part_ref, at_ref, *refs):
    at = pl.program_id(0)
    out_ref = refs[-1]
    taps, _, head = out_ref.shape
    share, lane = refs[0].shape[0], head // 2

    @pl.when(part_ref[at] >= 0)
    def _():
        for m in range(chips):
            row = pl.multiple_of((at_ref[0] ^ m) * share, share)
            for ref, core in ((refs[m], at_ref[1]), (refs[chips + m], 1 - at_ref[1])):
                column = pl.multiple_of(core * lane, lane)
                for k in range(taps):
                    out_ref[k, pl.ds(row, share), pl.ds(column, lane)] = ref[
                        :, k * lane : (k + 1) * lane
                    ].astype(full)

    @pl.when(part_ref[at] < 0)
    def _():
        out_ref[...] = jnp.zeros_like(out_ref)


def place_shares(mine, other, part_of, at, head):
    chips = len(mine)
    share = mine[0].shape[0]
    steps = part_of.shape[0]
    picked = lambda i, p, c: (0, jnp.maximum(p[i], 0))
    return pl.pallas_call(
        lambda *refs: place_kernel(chips, *refs),
        out_shape=jax.ShapeDtypeStruct((3 * steps, chips * share, head), full),
        grid_spec=pltpu.PrefetchScalarGridSpec(
            num_scalar_prefetch=2,
            grid=(steps,),
            in_specs=[spec((share, 3 * head // 2), picked)] * (2 * chips),
            out_specs=spec((3, chips * share, head), lambda i, p, c: (i, 0, 0)),
        ),
        compiler_params=params(),
        cost_estimate=cost(0, 36 * steps * chips * share * head // 2),
    )(part_of, at, *mine, *other)


def on_device(
    features,
    crop_scale,
    crop_group,
    labels,
    w_reduce,
    gain_reduce,
    bias_reduce,
    w_middle,
    gain_middle,
    bias_middle,
    w_expand,
    gain_expand,
    bias_expand,
    w_heads,
    gain_heads,
    bias_heads,
    w_class,
    b_class,
):
    rows = features.shape[1]
    cols = features.shape[2]
    depth = features.shape[3]
    width = w_reduce.shape[1]
    tasks = w_heads.shape[1]
    head = w_heads.shape[3]
    own = w_heads.shape[0]
    classes = w_class.shape[2]
    pixels = rows * cols
    line = line_size()
    place = lax.axis_index(LINE)
    group = lax.axis_index(("x", "c"))
    inside = crop_table(crop_scale, crop_group, group, W_UNIT, cols)

    def same(offset):
        return jnp.tile(jnp.sum(inside * along(inside, offset, 0), axis=1), rows)[:, None]

    valid = same(0)
    count = jnp.sum(crop_scale).astype(full) * float(W_UNIT * rows * line)
    crops = float(crop_scale.shape[0])

    core = lax.axis_index("c")
    core_at = core.reshape(1).astype(jnp.int32)
    ratio = depth // width
    red_rows, mid_rows, exp_rows = (w.shape[0] // 2 for w in (w_reduce, w_middle, w_expand))
    red_own = half_of(w_reduce, 0, core)
    mid_own = half_of(w_middle.transpose(1, 0, 2), 1, core).reshape(9 * mid_rows, width)
    exp_own = half_of(w_expand, 0, core).reshape(exp_rows, ratio, width).transpose(1, 0, 2)
    rest_own = jnp.concatenate([mid_own, exp_own.reshape(ratio * exp_rows, width)], axis=0)
    block_own = jnp.concatenate([red_own, rest_own], axis=0)
    source = features.reshape(pixels, depth) * valid.astype(low)
    block_mine = lax.all_gather(block_own, LINE, axis=0, tiled=False)
    block_mine, source = lax.optimization_barrier((block_mine, source))
    block_other = flip(block_mine, [("c", 1)])
    if mid_rows % 16 == 0 and red_rows % 16 == 0:
        red_all = place_halves(block_mine, block_other, core_at, red_rows)
        mid_all, exp_all = place_block(
            block_mine, block_other, core_at, red_rows, mid_rows, exp_rows, ratio
        )
    else:
        block_all = both_halves(block_mine, block_other, core, 1)
        cuts = np.cumsum([0, red_rows, 9 * mid_rows, ratio * exp_rows])
        red_all, mid_all, exp_all = (block_all[:, :, cuts[i] : cuts[i + 1]] for i in range(3))
        red_all = red_all.reshape(depth, width)
        mid_all = mid_all.reshape(line, 2, 3, 3, mid_rows, width).transpose(2, 0, 1, 4, 3, 5)
        mid_all = mid_all.reshape(3 * width, 3 * width)
        exp_all = exp_all.reshape(line, 2, ratio, exp_rows, width).transpose(0, 1, 3, 2, 4)
        exp_all = exp_all.reshape(width, depth)
    terms, table = head_plan(rows)
    slots = table.shape[0]
    three = 3 * head
    by_term = w_heads.reshape(own, tasks, 3, 3, head).transpose(1, 2, 0, 3, 4)
    by_term = by_term.reshape(tasks, 3, own, three)
    parts = [by_term[t, 1] for t in range(tasks)] + [by_term[t, s + 1] for t, s, _ in terms]
    quarter = own // lax.axis_size(("x", "c"))
    heads_own = jnp.concatenate(
        [lax.dynamic_slice_in_dim(part, group * quarter, quarter, axis=0) for part in parts], axis=1
    )
    heads_own, block_mine = lax.optimization_barrier((heads_own, block_mine))
    heads_all = lax.all_gather(heads_own, AXES, axis=0, tiled=True)
    term_tasks = np.array([task for task, _, _ in terms], np.int32)
    picked_term = jnp.asarray(table)[:, place]
    slot_tasks = [sorted({int(term_tasks[e]) for e in table[s]}) for s in range(slots)]
    side_task = jnp.asarray(term_tasks)[picked_term]
    centers = jnp.arange(tasks, dtype=jnp.int32)
    all_tasks = jnp.concatenate([centers, side_task])
    all_picked = jnp.concatenate([centers, tasks + picked_term])

    reduced = dot(source, red_all)
    mean1, scale1 = norm_scale(reduced, count)
    normed1 = (reduced - mean1) * scale1
    out1 = normed1 * gain_reduce + bias_reduce
    hidden1 = (silu(out1) * valid).astype(low)
    edge = mid_rate * cols
    down = [(i, i + 1) for i in range(line - 1)]
    up = [(i + 1, i) for i in range(line - 1)]
    before1 = rows_to(hidden1[pixels - edge :], down)
    after1 = rows_to(hidden1[:edge], up)
    tall = jnp.concatenate([before1, hidden1, after1], axis=0)
    wide1 = jnp.concatenate([tall[i * edge : i * edge + pixels] for i in range(3)], axis=1)
    spread = dot(wide1, mid_all)
    mid_masks = [same((k - 1) * mid_rate) for k in range(3)]
    middled = sum(
        along(spread[:, k * width : (k + 1) * width], (k - 1) * mid_rate, 0) * mid_masks[k]
        for k in range(3)
    )
    mean2, scale2 = norm_scale(middled, count)
    normed2 = (middled - mean2) * scale2
    out2 = normed2 * gain_middle + bias_middle
    hidden2 = (silu(out2) * valid).astype(low)
    expanded = dot(hidden2, exp_all)
    mean3, scale3 = norm_scale(expanded, count)
    normed3 = (expanded - mean3) * scale3
    before = normed3 * gain_expand + bias_expand + source.astype(full)
    grid = (silu(before) * valid).astype(low)

    chips = lax.axis_size("x")
    chip = lax.axis_index("x")
    share = own // chips

    def share_columns(which):
        cuts = [f * own + which * share for f in range(line)]
        return jnp.concatenate(
            [lax.dynamic_slice_in_dim(grid, cut, share, axis=1) for cut in cuts], axis=1
        )

    grid_pieces = []
    for m in range(chips):
        piece = share_columns(chip ^ m)
        piece = flip(piece, [("x", m)]) if m else piece
        grid_pieces += [piece, flip(piece, [("c", 1)])]

    def mask_table(group):
        inside = crop_table(crop_scale, crop_group, group, W_UNIT, cols)
        columns = [
            jnp.sum(inside * along(inside, (k - 1) * rate, 0), axis=1)
            for rate in head_rates
            for k in range(3)
        ]
        table = jnp.pad(jnp.stack(columns, axis=1), ((0, 0), (0, 128 - 3 * tasks)))
        return jnp.tile(table, (rows, 1))

    masks = mask_table(group)
    all_masks = [masks, mask_table(group ^ 1)]
    for m in range(1, chips):
        all_masks += [mask_table((chip ^ m) * 2 + core), mask_table((chip ^ m) * 2 + 1 - core)]
    slot_of = jnp.full((len(terms),), -1, jnp.int32)
    for s in range(slots):
        slot_of = jnp.where(jnp.arange(len(terms)) == picked_term[s], tasks + s, slot_of)
    slot_of = jnp.concatenate([centers, slot_of])
    side_here = (side_task[:, None] == centers[None, :]).astype(full).reshape(-1)
    vecs = jnp.pad(jnp.stack([mean3, scale3, gain_expand, bias_expand]), ((0, 4), (0, 0)))
    side_picked = tasks + picked_term
    grid, all_masks, slot_of, side_here, vecs, side_picked, side_task, picked_term = (
        lax.optimization_barrier(
            (grid, all_masks, slot_of, side_here, vecs, side_picked, side_task, picked_term)
        )
    )
    masks = all_masks[0]
    moves = row_moves(terms, line)
    side_terms = head_terms(grid, heads_all, masks, tasks + picked_term, side_task, head, low)
    moved = [None] * tasks
    for task, pairs, members in moves:
        sends = {f: s for e, froms in members for f in froms for s in range(slots) if table[s, f] == e}
        sent = None
        for s in sorted(set(sends.values())):
            part = side_terms[:, s * head : (s + 1) * head]
            here = jnp.asarray(np.array([sends.get(f) == s for f in range(line)]))[place]
            sent = part if sent is None else jnp.where(here, part, sent)
        got = rows_to(sent, pairs).astype(full)
        moved[task] = got if moved[task] is None else moved[task] + got
    middle_terms = head_terms(grid, heads_all, masks, centers, centers, head, full)
    middle_terms, grid_pieces = lax.optimization_barrier((middle_terms, grid_pieces))
    mixed = []
    for task in range(tasks):
        center = middle_terms[:, task * head : (task + 1) * head]
        mixed.append(center if moved[task] is None else center + moved[task])
    mixed = jnp.concatenate(mixed, axis=1)
    gain_h, bias_h = gain_heads.reshape(-1), bias_heads.reshape(-1)
    mean_h, scale_h = norm_scale(mixed, count)
    normed_h = (mixed - mean_h) * scale_h
    out_h = normed_h * gain_h + bias_h
    activ = (silu(out_h) * valid).astype(low)
    marks = labels.reshape(tasks, pixels)
    class_part, class_bias_part, dactiv = [], [], []
    for task in range(tasks):
        act = activ[:, task * head : (task + 1) * head]
        logits = dot(act, w_class[task]) + b_class[task]
        onehot = (marks[task][:, None] == jnp.arange(classes, dtype=jnp.int32)[None, :]).astype(full)
        dlogits = ((jax.nn.softmax(logits, axis=-1) - onehot) * valid / crops).astype(low)
        class_part.append(dot_tn(dlogits, act))
        class_bias_part.append(jnp.sum(dlogits.astype(full), axis=0))
        dactiv.append(dot_nt(dlogits, w_class[task]))
    dout_h = jnp.concatenate(dactiv, axis=1) * valid * silu_slope(out_h)
    sums_h = all_sum(jnp.stack([jnp.sum(dout_h * normed_h, axis=0), jnp.sum(dout_h, axis=0)]))
    dgain_h, dbias_h = sums_h[0], sums_h[1]
    dmixed = valid * (gain_h * scale_h) * (dout_h - dbias_h / count - normed_h * (dgain_h / count))
    dmixed = dmixed.astype(low)

    class_sums = jnp.concatenate(
        [jnp.concatenate(class_part, axis=0), jnp.pad(jnp.stack(class_bias_part), ((0, 0), (0, head - classes)))],
        axis=0,
    )
    class_sums = class_sums + flip(class_sums, [("c", 1)])
    class_sums = sum_along(class_sums, "y")
    lane = head // 2
    tap_half = 3 * lane

    def half_taps(grads, which):
        cuts = [i * head + which * lane for i in range(grads.shape[1] // head)]
        return jnp.concatenate(
            [lax.dynamic_slice_in_dim(grads, cut, lane, axis=1) for cut in cuts], axis=1
        )

    def from_groups(grads):
        halves = [half_taps(grads, core), flip(half_taps(grads, 1 - core), [("c", 1)])]
        halves = jnp.concatenate(halves, axis=1)
        return [halves] + [flip(halves, [("x", m)]) for m in range(1, chips)]

    center_halves = from_groups(dmixed)
    back = [None] * len(terms)
    for task, pairs, members in moves:
        got = rows_to(dmixed[:, task * head : (task + 1) * head], [(t, f) for f, t in pairs])
        for e, froms in members:
            here = jnp.asarray(np.array([f in froms for f in range(line)]))[place]
            back[e] = got if len(members) == 1 else jnp.where(here, got, jnp.zeros_like(got))
    dsides = []
    for s in range(slots):
        dside = back[table[s][0]]
        for e in sorted(set(table[s].tolist()) - {int(table[s][0])}):
            dside = jnp.where(picked_term[s] == e, back[e], dside)
        dsides.append(dside)
    dys = spread_back(dmixed, masks, centers, head, pixels)
    *center_grads, slope3, normed3 = center_back(
        dys, heads_all, tasks, expanded, source, vecs, masks, 512
    )
    center_grads, slope3, normed3, turned, dsides, center_halves, class_sums = (
        lax.optimization_barrier(
            (
                center_grads,
                slope3,
                normed3,
                turn(grid_pieces),
                jnp.concatenate(dsides, axis=1),
                center_halves,
                class_sums,
            )
        )
    )
    class_sums = sum_along(class_sums, "z")
    side_halves = from_groups(dsides)
    dys = spread_back(dsides, masks, side_task, head, pixels)
    shared_grads, sums = side_back(
        dys, heads_all, side_picked, side_here, slot_tasks, tasks, center_grads, slope3, normed3, 512
    )
    sums, center_halves, side_halves, class_sums = lax.optimization_barrier(
        (sums, center_halves, side_halves, class_sums)
    )
    class_sums = sum_along(class_sums, "x")
    gram_part = jnp.sum(sums[2 * tasks : 4 * tasks], axis=1)
    gram_row = jnp.pad(gram_part, (0, depth - gram_part.shape[0]))[None, :]
    summed = all_sum(jnp.concatenate([sums[: 2 * tasks], gram_row], axis=0))
    sums3 = summed[: 2 * tasks].reshape(tasks, 2, depth)
    weight_list = task_scales([summed[2 * tasks, i] for i in range(6)])
    task_weights = jnp.stack(weight_list)

    head_part = weight_grad(
        turned, center_halves, side_halves, all_masks, slot_of, side_task, slot_tasks, tasks
    )
    shared_grads, head_part = lax.optimization_barrier((shared_grads, head_part))
    head_part = head_part.reshape(line, share, len(parts) * tap_half)
    head_own = lax.psum_scatter(head_part, LINE, scatter_dimension=0, tiled=False)

    dgain3, dbias3 = (
        sum(weight_list[t] * sums3[t, j] for t in range(tasks)) for j in range(2)
    )
    vec_rows = [gain_expand * scale3, jnp.broadcast_to(1.0 / count, (depth,))]
    vecs = jnp.pad(jnp.stack(vec_rows), ((0, 6), (0, 0)))
    mid_vecs = jnp.pad(jnp.stack([mean2, scale2, gain_middle, bias_middle]), ((0, 4), (0, 0)))
    dbefore, exp_part, dout2, sums2 = expand_back(
        summed, shared_grads, slope3, normed3, vecs, masks, hidden2, exp_all, middled,
        mid_vecs, 512,
    )
    sums2 = all_sum(sums2[:2])
    dgain2, dbias2 = sums2[0], sums2[1]
    dmiddled = valid * (gain_middle * scale2) * (
        dout2 - dbias2 / count - normed2 * (dgain2 / count)
    )
    dmiddled = dmiddled.astype(low)
    dspread = jnp.concatenate(
        [along(dmiddled * mid_masks[k].astype(low), -(k - 1) * mid_rate, 0) for k in range(3)],
        axis=1,
    )
    dwide = dot_nt(dspread, mid_all)
    from_below = rows_to(dwide[:edge, :width].astype(low), up).astype(full)
    from_above = rows_to(dwide[pixels - edge :, 2 * width :].astype(low), down).astype(full)
    dspread, exp_part, dwide = lax.optimization_barrier((dspread, exp_part, dwide))
    mid_part = dot_tn(wide1, dspread).astype(low).reshape(3, line, 2, mid_rows, 3 * width)
    exp_part = exp_part.reshape(line, 2, exp_rows, depth)

    def later_half(which):
        mid_half = lax.dynamic_index_in_dim(mid_part, which, 2, keepdims=False)
        exp_half = lax.dynamic_index_in_dim(exp_part, which, 1, keepdims=False)
        pieces = [
            mid_half[i, :, :, k * width : (k + 1) * width] for i in range(3) for k in range(3)
        ]
        pieces += [exp_half[:, :, k * width : (k + 1) * width] for k in range(ratio)]
        return jnp.concatenate(pieces, axis=1)

    later_other = flip(later_half(1 - core), [("c", 1)])
    later = (later_half(core).astype(full) + later_other.astype(full)).astype(low)
    dhidden1 = (
        dwide[:, width : 2 * width]
        + jnp.concatenate([dwide[edge:, :width], from_below], axis=0)
        + jnp.concatenate([from_above, dwide[: pixels - edge, 2 * width :]], axis=0)
    )
    dout1 = dhidden1 * valid * silu_slope(out1)
    sums1 = all_sum(jnp.stack([jnp.sum(dout1 * normed1, axis=0), jnp.sum(dout1, axis=0)]))
    sums1, later = lax.optimization_barrier((sums1, later))
    cut = later.shape[1] // 64 * 32
    first, second = scatter_x(later[:, :cut], 1), scatter_x(later[:, cut:], 1)
    second, head_own = lax.optimization_barrier((second, head_own))
    head_shares = [head_own] + [flip(head_own, [("x", m)]) for m in range(1, chips)]
    head_others = [flip(part, [("c", 1)]) for part in head_shares]
    later_own = [scatter_z(scatter_y(piece)) for piece in (first, second)]
    dgain1, dbias1 = sums1[0], sums1[1]
    dreduced = valid * (gain_reduce * scale1) * (
        dout1 - dbias1 / count - normed1 * (dgain1 / count)
    )
    dreduced = dreduced.astype(low)
    dfeatures = dbefore.astype(full) + dot_nt(dreduced, red_all)

    red_part = dot_tn(source, dreduced).astype(low).reshape(line, -1, width)
    red_sum = over_groups(scatter_z(scatter_y(between_cores(red_part))))
    red_sum = both_halves(*red_sum, core, 0).astype(full)
    part_of = np.full((tasks, 3), -1, np.int32)
    part_of[:, 1] = np.arange(tasks)
    for e, (task, side, _) in enumerate(terms):
        part_of[task, side + 1] = tasks + e
    at = jnp.stack([chip, core]).astype(jnp.int32)
    heads_out = place_shares(head_shares, head_others, jnp.asarray(part_of.reshape(-1)), at, head)
    heads_out = heads_out.reshape(tasks, 9, own, head).transpose(2, 0, 1, 3)
    later_own = jnp.concatenate([gather_x(piece) for piece in later_own], axis=0)
    heads_out, later_own = lax.optimization_barrier((heads_out, later_own))
    later_other = flip(later_own, [("c", 1)])
    later_sum = both_halves(
        later_own.reshape(9 + ratio, mid_rows, width),
        later_other.reshape(9 + ratio, mid_rows, width),
        core,
        1,
    ).reshape(9 + ratio, 2 * mid_rows, width)
    mid_sum = later_sum[:9].transpose(1, 0, 2).astype(full)
    exp_sum = later_sum[9:].transpose(1, 0, 2).reshape(2 * exp_rows, depth).astype(full)
    grad_class = class_sums[: tasks * classes].reshape(tasks, classes, head).transpose(0, 2, 1)
    grad_class_bias = class_sums[tasks * classes :, :classes]
    return (
        dfeatures.reshape(1, rows, cols, depth),
        red_sum.reshape(w_reduce.shape),
        mid_sum,
        exp_sum,
        heads_out,
        dgain1,
        dbias1,
        dgain2,
        dbias2,
        dgain3,
        dbias3,
        dgain_h.reshape(tasks, head),
        dbias_h.reshape(tasks, head),
        grad_class,
        grad_class_bias,
        task_weights,
    )


def solution(mesh):
    line, groups = mesh.shape["fsdp"], mesh.shape["dp"]
    fine = Mesh(mesh.devices.reshape(line // 2, 2, groups // 2, 2), AXES)
    dp = ("x", "c")
    rows = P(LINE)
    in_specs = (
        P(dp, LINE, None, None),
        P(),
        P(),
        P(None, dp, LINE, None),
        rows,
        P(),
        P(),
        rows,
        P(),
        P(),
        rows,
        P(),
        P(),
        rows,
        P(),
        P(),
        P(),
        P(),
    )
    out_specs = (P(dp, LINE, None, None),) + (rows,) * 4 + (P(),) * 11
    return jax.shard_map(
        on_device, mesh=fine, in_specs=in_specs, out_specs=out_specs, check_vma=False
    )
```

```python
import itertools

import jax
import jax.numpy as jnp
import numpy as np
from jax import lax
from jax.experimental import pallas as pl
from jax.experimental.pallas import tpu as pltpu
from jax.sharding import Mesh
from jax.sharding import PartitionSpec as P

W_UNIT = 12


eps = 1e-05
mid_rate = 2
head_rates = (12, 24, 36)
AXES = ("z", "y", "x", "c")
LINE = ("z", "y")
low = jnp.bfloat16
full = jnp.float32


def coords(names):
    return list(itertools.product(*[range(lax.axis_size(name)) for name in names]))


def flip(value, moves):
    moves = sorted([m for m in moves if m[1]], key=lambda move: AXES.index(move[0]))
    names = tuple(name for name, _ in moves)
    places = coords(names)
    index = {place: i for i, place in enumerate(places)}
    pairs = [
        (i, index[tuple(at ^ bit for at, (_, bit) in zip(place, moves))])
        for i, place in enumerate(places)
    ]
    return lax.ppermute(value, names, pairs)


def all_sum(value):
    moves = []
    for name in ("y", "x", "z"):
        bit = 1
        while bit < lax.axis_size(name):
            moves.append((name, bit))
            bit *= 2
    value = value + flip(value, [("c", 1)])
    while moves:
        if len(moves) == 1:
            value = value + flip(value, moves)
            break
        first, second = moves[:2]
        moves = moves[2:]
        both = [(first[0], first[1] | second[1])] if first[0] == second[0] else [first, second]
        one, two, three = flip(value, [first]), flip(value, [second]), flip(value, both)
        value = (value + one) + (two + three)
    return value


def sum_along(value, name):
    bit = 1
    while bit < lax.axis_size(name):
        value = value + flip(value, [(name, bit)])
        bit *= 2
    return value


def rows_to(value, pairs):
    if not pairs:
        return jnp.zeros_like(value)
    return lax.ppermute(value, LINE, pairs)


def line_size():
    return lax.axis_size("z") * lax.axis_size("y")


def half_of(value, axis, core):
    size = value.shape[axis] // 2
    return lax.dynamic_slice_in_dim(value, core * size, size, axis=axis)


def both_halves(mine, other, core, axis):
    first = jnp.where(core == 0, mine, other)
    second = jnp.where(core == 0, other, mine)
    return jnp.stack([first, second], axis=axis)


def between_cores(partial):
    core = lax.axis_index("c")
    mine = half_of(partial, 1, core)
    other = flip(half_of(partial, 1, 1 - core), [("c", 1)])
    return (mine.astype(full) + other.astype(full)).astype(low)


def over_groups(own):
    bit = 1
    while bit < lax.axis_size("x"):
        own = (own.astype(full) + flip(own, [("x", bit)]).astype(full)).astype(low)
        bit *= 2
    return own, flip(own, [("c", 1)])


def scatter_y(partial):
    parts = partial.reshape(-1, 2, *partial.shape[1:])
    here = lax.axis_index("y")
    mine = lax.dynamic_index_in_dim(parts, here, 1, keepdims=False)
    other = lax.dynamic_index_in_dim(parts, 1 - here, 1, keepdims=False)
    return (mine.astype(full) + flip(other, [("y", 1)]).astype(full)).astype(low)


def scatter_x(partial, axis):
    chips, here = lax.axis_size("x"), lax.axis_index("x")
    size = partial.shape[axis] // chips
    total = lax.dynamic_slice_in_dim(partial, here * size, size, axis).astype(full)
    for m in range(1, chips):
        part = lax.dynamic_slice_in_dim(partial, (here ^ m) * size, size, axis)
        total = total + flip(part, [("x", m)]).astype(full)
    return total.astype(low)


def gather_x(own):
    chips, here = lax.axis_size("x"), lax.axis_index("x")
    parts = jnp.stack([own] + [flip(own, [("x", m)]) for m in range(1, chips)])
    ordered = [lax.dynamic_index_in_dim(parts, here ^ m, 0, keepdims=False) for m in range(chips)]
    return jnp.concatenate(ordered, axis=0)


def scatter_z(parts):
    here = lax.axis_index("z")
    total = lax.dynamic_index_in_dim(parts, here, 0, keepdims=False).astype(full)
    for m in range(1, lax.axis_size("z")):
        part = lax.dynamic_index_in_dim(parts, here ^ m, 0, keepdims=False)
        total = total + flip(part, [("z", m)]).astype(full)
    return total.astype(low)


def along(value, offset, axis):
    size = value.shape[axis]
    if offset == 0:
        return value
    widths = [(0, 0)] * value.ndim
    if offset > 0:
        widths[axis] = (0, offset)
        return lax.slice_in_dim(jnp.pad(value, widths), offset, offset + size, axis=axis)
    widths[axis] = (-offset, 0)
    return lax.slice_in_dim(jnp.pad(value, widths), 0, size, axis=axis)


def crop_table(crop_scale, crop_group, group, unit, cols):
    mine = (crop_group == group).astype(jnp.int32)
    widths = crop_scale * unit * mine
    ends = jnp.cumsum(widths)
    starts = ends - widths
    column = jnp.arange(cols, dtype=jnp.int32)[:, None]
    return ((column >= starts[None, :]) & (column < ends[None, :])).astype(full)


def silu(value):
    return value * (0.5 + 0.5 * jnp.tanh(0.5 * value))


def silu_slope(value):
    turn = jnp.tanh(0.5 * value)
    return 0.5 + 0.5 * turn + 0.25 * value * (1.0 - turn * turn)


def norm_scale(value, count):
    sums = all_sum(jnp.stack([jnp.sum(value, axis=0), jnp.sum(value * value, axis=0)]))
    mean = sums[0] / count
    return mean, lax.rsqrt(sums[1] / count - mean * mean + eps)


def head_plan(rows):
    line = line_size()
    terms = []
    for task, rate in enumerate(head_rates):
        hop = rate // rows
        for side in (-1, 1):
            if hop < line:
                terms.append((task, side, hop))
    last = lax.axis_size("y")
    planes = []
    for z in range(lax.axis_size("z")):
        need = []
        for e, (task, side, hop) in enumerate(terms):
            if any(0 <= z * last + y - side * hop < line for y in range(last)):
                need.append(e)
        planes.append(need)
    slots = max(len(need) for need in planes)
    table = np.zeros((slots, line), np.int32)
    for z, need in enumerate(planes):
        rest = [e for e in range(len(terms)) if e not in need]
        for s, e in enumerate((need + rest)[:slots]):
            table[s, z * last : (z + 1) * last] = e
    return terms, table


def row_moves(terms, line):
    moves = []
    for e, (task, side, hop) in enumerate(terms):
        pairs = [(f, f - side * hop) for f in range(line) if 0 <= f - side * hop < line]
        last = moves[-1] if moves else None
        if last and last[0] == task and not {t for _, t in last[1]} & {t for _, t in pairs}:
            if not {f for f, _ in last[1]} & {f for f, _ in pairs}:
                last[1].extend(pairs)
                last[2].append((e, [f for f, _ in pairs]))
                continue
        moves.append((task, pairs, [(e, [f for f, _ in pairs])]))
    return moves


def task_scales(products):
    g00, g01, g02, g11, g12, g22 = products
    n0, n1, n2 = (jnp.sqrt(g + 1e-12) for g in (g00, g11, g22))
    c00, c11, c22 = (g / (n * n) + 0.1 for g, n in ((g00, n0), (g11, n1), (g22, n2)))
    c01, c02, c12 = g01 / (n0 * n1), g02 / (n0 * n2), g12 / (n1 * n2)
    w0 = (c11 * c22 - c12 * c12) + (c12 * c02 - c01 * c22) + (c01 * c12 - c11 * c02)
    w1 = (c12 * c02 - c22 * c01) + (c22 * c00 - c02 * c02) + (c02 * c01 - c12 * c00)
    w2 = (c01 * c12 - c02 * c11) + (c02 * c01 - c00 * c12) + (c00 * c11 - c01 * c01)
    top = n0 + n1 + n2
    total = w0 + w1 + w2
    return [w * top / (n * total) for w, n in ((w0, n0), (w1, n1), (w2, n2))]


def dot(a, b):
    return jnp.dot(a, b, preferred_element_type=full)


def dot_nt(a, b):
    return lax.dot_general(a, b, (((1,), (1,)), ((), ())), preferred_element_type=full)


def dot_tn(a, b):
    return lax.dot_general(a, b, (((0,), (0,)), ((), ())), preferred_element_type=full)


def spec(shape, index):
    return pl.BlockSpec(shape, index)


def params(mib=56):
    return pltpu.CompilerParams(vmem_limit_bytes=mib * 2**20)


def cost(flops, moved):
    return pl.CostEstimate(flops=flops, bytes_accessed=moved, transcendentals=0)


def terms_kernel(picked_ref, task_ref, x_ref, w_ref, mask_ref, out_ref):
    at = pl.program_id(0)
    pixels, head = out_ref.shape

    def product(k):
        return jnp.dot(
            x_ref[...], w_ref[:, k * head : (k + 1) * head], preferred_element_type=full
        )

    for task, rate in enumerate(head_rates):

        @pl.when(task_ref[at] == task)
        def _():
            left = pltpu.roll(product(0), rate, 0) * mask_ref[:, 3 * task : 3 * task + 1]
            right = pltpu.roll(product(2), pixels - rate, 0)
            right = right * mask_ref[:, 3 * task + 2 : 3 * task + 3]
            out_ref[...] = (product(1) + left + right).astype(out_ref.dtype)


def head_terms(grid, heads_all, masks, picked, task_of, head, dtype):
    pixels, depth = grid.shape
    items = picked.shape[0]
    return pl.pallas_call(
        terms_kernel,
        out_shape=jax.ShapeDtypeStruct((pixels, items * head), dtype),
        grid_spec=pltpu.PrefetchScalarGridSpec(
            num_scalar_prefetch=2,
            grid=(items,),
            in_specs=[
                spec((pixels, depth), lambda i, p, t: (0, 0)),
                spec((depth, 3 * head), lambda i, p, t: (0, p[i])),
                spec(masks.shape, lambda i, p, t: (0, 0)),
            ],
            out_specs=spec((pixels, head), lambda i, p, t: (0, i)),
        ),
        compiler_params=params(),
        cost_estimate=cost(
            2 * pixels * depth * 3 * head * items, 2 * items * depth * 3 * head + 2 * pixels * depth
        ),
    )(picked, task_of, grid, heads_all, masks)


def spread_kernel(task_ref, d_ref, mask_ref, out_ref):
    at = pl.program_id(1)
    pixels, head = d_ref.shape
    for task, rate in enumerate(head_rates):

        @pl.when(task_ref[at] == task)
        def _():
            grad = d_ref[...].astype(full)
            out_ref[:, head : 2 * head] = d_ref[...]
            for k, shift in ((0, pixels - rate), (2, rate)):
                piece = grad * mask_ref[:, 3 * task + k : 3 * task + k + 1]
                out_ref[:, k * head : (k + 1) * head] = pltpu.roll(piece, shift, 0).astype(low)


def spread_back(grads, masks, task_of, head, pixels):
    rows = grads.shape[0]
    items = grads.shape[1] // head
    return pl.pallas_call(
        spread_kernel,
        out_shape=jax.ShapeDtypeStruct((rows, 3 * head * items), low),
        grid_spec=pltpu.PrefetchScalarGridSpec(
            num_scalar_prefetch=1,
            grid=(rows // pixels, items),
            in_specs=[
                spec((pixels, head), lambda j, i, t: (j, i)),
                spec((pixels, masks.shape[1]), lambda j, i, t: (j, 0)),
            ],
            out_specs=spec((pixels, 3 * head), lambda j, i, t: (j, i)),
        ),
        compiler_params=params(),
        cost_estimate=cost(30 * rows * head * items, 8 * rows * head * items),
    )(task_of, grads, masks)


def center_back_kernel(tasks, *refs):
    dy_ref = refs[0]
    w_refs = refs[1 : 1 + tasks]
    wide_ref, source_ref, vec_ref, mask_ref = refs[1 + tasks : 5 + tasks]
    out_refs = refs[5 + tasks : -2]
    slope_ref, normed_ref = refs[-2:]
    three = w_refs[0].shape[1]
    pixels = dy_ref.shape[0]
    for at in range(0, pixels, pixels // 3):
        rows = slice(at, at + pixels // 3)
        for t in range(tasks):
            out_refs[t][rows, :] = lax.dot_general(
                dy_ref[rows, t * three : (t + 1) * three],
                w_refs[t][...],
                (((1,), (1,)), ((), ())),
                preferred_element_type=full,
            ).astype(low)
        normed = (wide_ref[rows, :].astype(full) - vec_ref[0:1]) * vec_ref[1:2]
        value = normed * vec_ref[2:3] + vec_ref[3:4] + source_ref[rows, :].astype(full)
        slope_ref[rows, :] = (silu_slope(value) * mask_ref[rows, 1:2]).astype(low)
        normed_ref[rows, :] = normed.astype(low)


def center_back(dys, heads_all, tasks, wide, source, vecs, masks, block):
    pixels, depth = wide.shape
    three = dys.shape[1] // tasks
    column = lambda j: (0, j)
    fixed = lambda j: (0, 0)
    return pl.pallas_call(
        lambda *refs: center_back_kernel(tasks, *refs),
        out_shape=[jax.ShapeDtypeStruct((pixels, depth), low)] * (tasks + 2),
        grid=(depth // block,),
        in_specs=[spec(dys.shape, fixed)]
        + [spec((block, three), lambda j, i=i: (j, i)) for i in range(tasks)]
        + [spec((pixels, block), column)] * 2
        + [spec((8, block), column), spec(masks.shape, fixed)],
        out_specs=[spec((pixels, block), column)] * (tasks + 2),
        compiler_params=params(),
        cost_estimate=cost(2 * pixels * depth * three * tasks, 16 * pixels * depth),
    )(dys, *([heads_all] * tasks), wide, source, vecs, masks)


def side_back_kernel(tasks, side_tasks, touched, *refs):
    slots = len(side_tasks)
    here_ref, dy_ref = refs[1:3]
    w_refs = refs[3 : 3 + slots]
    held_refs = refs[3 + slots : 3 + slots + tasks]
    slope_ref, normed_ref = refs[3 + slots + tasks : 5 + slots + tasks]
    out_refs = refs[5 + slots + tasks : -1]
    sums_ref = refs[-1]
    pixels = dy_ref.shape[0]
    totals = None
    for at in range(0, pixels, pixels // 3):
        rows = slice(at, at + pixels // 3)
        grads = [ref[rows, :].astype(full) for ref in held_refs]
        for s, choices in enumerate(side_tasks):
            three = w_refs[s].shape[1]
            side = lax.dot_general(
                dy_ref[rows, s * three : (s + 1) * three],
                w_refs[s][...],
                (((1,), (1,)), ((), ())),
                preferred_element_type=full,
            )
            for t in choices:
                more = side if len(choices) == 1 else side * here_ref[s * tasks + t]
                grads[t] = grads[t] + more
        slope, normed = slope_ref[rows, :].astype(full), normed_ref[rows, :].astype(full)
        parts = []
        for t in range(tasks):
            part = grads[t] * slope
            parts += [jnp.sum(part * normed, axis=0), jnp.sum(part, axis=0)]
        for t in range(tasks):
            for u in range(t, tasks):
                parts.append(jnp.sum(grads[t] * grads[u], axis=0))
        for i, t in enumerate(touched):
            out_refs[i][rows, :] = grads[t].astype(low)
        totals = parts if totals is None else [a + b for a, b in zip(totals, parts)]
    sums_ref[...] = jnp.zeros_like(sums_ref)
    for i, row in enumerate(totals):
        sums_ref[i, :] = row


def side_back(dys, heads_all, picked, here, side_tasks, tasks, held, slope, normed, block):
    pixels, depth = slope.shape
    slots = len(side_tasks)
    three = dys.shape[1] // slots
    touched = sorted({t for choices in side_tasks for t in choices})
    column = lambda j, p, h: (0, j)
    *outs, sums = pl.pallas_call(
        lambda *refs: side_back_kernel(tasks, side_tasks, touched, *refs),
        out_shape=[jax.ShapeDtypeStruct((pixels, depth), low)] * len(touched)
        + [jax.ShapeDtypeStruct((16, depth), full)],
        grid_spec=pltpu.PrefetchScalarGridSpec(
            num_scalar_prefetch=2,
            grid=(depth // block,),
            in_specs=[spec(dys.shape, lambda j, p, h: (0, 0))]
            + [spec((block, three), lambda j, p, h, i=i: (j, p[i])) for i in range(slots)]
            + [spec((pixels, block), column)] * (tasks + 2),
            out_specs=[spec((pixels, block), column)] * len(touched) + [spec((16, block), column)],
        ),
        compiler_params=params(),
        cost_estimate=cost(2 * pixels * depth * three * slots, 14 * pixels * depth),
    )(picked, here, dys, *([heads_all] * slots), *held, slope, normed)
    return [outs[touched.index(t)] if t in touched else held[t] for t in range(tasks)], sums


def expand_back_kernel(tasks, blocks, *refs):
    gram_ref, sum_ref = refs[0], refs[1 + tasks]
    grad_refs = refs[1 : 1 + tasks]
    slope_ref, normed_ref, vec_ref, mask_ref, hidden_ref, w_ref, mid_ref, mid_vec_ref = refs[
        2 + tasks : 10 + tasks
    ]
    dbefore_ref, dweight_ref, dout_ref, sums_ref, total_ref, turned_ref, scale_ref = refs[
        10 + tasks :
    ]
    at = pl.program_id(0)

    @pl.when(at == 0)
    def _():
        turned_ref[...] = hidden_ref[...].T
        gram = 2 * tasks
        scales = task_scales([gram_ref[gram : gram + 1, i : i + 1] for i in range(6)])
        for t in range(tasks):
            scale_ref[t : t + 1, :] = jnp.broadcast_to(scales[t], (1, scale_ref.shape[1]))

    weights = [scale_ref[t : t + 1, :] for t in range(tasks)]
    combined = grad_refs[0][...].astype(full) * weights[0]
    dgain = sum_ref[0:1] * weights[0]
    dbias = sum_ref[1:2] * weights[0]
    for t in range(1, tasks):
        combined = combined + grad_refs[t][...].astype(full) * weights[t]
        dgain = dgain + sum_ref[2 * t : 2 * t + 1] * weights[t]
        dbias = dbias + sum_ref[2 * t + 1 : 2 * t + 2] * weights[t]
    normed = normed_ref[...].astype(full)
    valid = mask_ref[:, 1:2]
    dbefore = combined * slope_ref[...].astype(full)
    dbefore_ref[...] = dbefore.astype(low)
    per = vec_ref[1:2]
    dwide = (dbefore - dbias * per - normed * (dgain * per)) * vec_ref[0:1] * valid
    dwide = dwide.astype(low)
    dweight_ref[...] = jnp.dot(turned_ref[...], dwide, preferred_element_type=full).astype(low)
    part = lax.dot_general(
        dwide, w_ref[...], (((1,), (1,)), ((), ())), preferred_element_type=full
    )

    @pl.when(at == 0)
    def _():
        total_ref[...] = part

    @pl.when(at > 0)
    def _():
        total_ref[...] += part

    @pl.when(at == blocks - 1)
    def _():
        mid = (mid_ref[...] - mid_vec_ref[0:1]) * mid_vec_ref[1:2]
        dout = total_ref[...] * silu_slope(mid * mid_vec_ref[2:3] + mid_vec_ref[3:4]) * valid
        dout_ref[...] = dout
        sums_ref[...] = jnp.zeros_like(sums_ref)
        sums_ref[0, :] = jnp.sum(dout * mid, axis=0)
        sums_ref[1, :] = jnp.sum(dout, axis=0)


def expand_back(summed, grads, slope, normed, vecs, masks, hidden, weight, mid, mid_vecs, block):
    pixels, depth = slope.shape
    width = hidden.shape[1]
    tasks = len(grads)
    column = lambda j: (0, j)
    fixed = lambda j: (0, 0)
    blocks = depth // block
    return pl.pallas_call(
        lambda *refs: expand_back_kernel(tasks, blocks, *refs),
        out_shape=[
            jax.ShapeDtypeStruct((pixels, depth), low),
            jax.ShapeDtypeStruct((width, depth), low),
            jax.ShapeDtypeStruct((pixels, width), full),
            jax.ShapeDtypeStruct((8, width), full),
        ],
        grid_spec=pltpu.PrefetchScalarGridSpec(
            num_scalar_prefetch=0,
            grid=(blocks,),
            in_specs=[spec((summed.shape[0], 128), fixed)]
            + [spec((pixels, block), column)] * tasks
            + [spec((summed.shape[0], block), column)]
            + [spec((pixels, block), column)] * 2
            + [
                spec((8, block), column),
                spec(masks.shape, fixed),
                spec((pixels, width), fixed),
                spec((width, block), column),
                spec((pixels, width), fixed),
                spec((8, width), fixed),
            ],
            out_specs=[
                spec((pixels, block), column),
                spec((width, block), column),
                spec((pixels, width), fixed),
                spec((8, width), fixed),
            ],
            scratch_shapes=[
                pltpu.VMEM((pixels, width), full),
                pltpu.VMEM((width, pixels), low),
                pltpu.VMEM((8, block), full),
            ],
        ),
        compiler_params=params(),
        cost_estimate=cost(4 * pixels * width, 14 * pixels),
    )(summed, *grads, summed, slope, normed, vecs, masks, hidden, weight, mid, mid_vecs)


def turn_kernel(*refs):
    out_ref = refs[-1]
    pixels = refs[0].shape[0]
    for i, ref in enumerate(refs[:-1]):
        out_ref[:, i * pixels : (i + 1) * pixels] = ref[...].T


def turn(pieces):
    pixels, depth = pieces[0].shape
    block = min(depth, 512)
    return pl.pallas_call(
        turn_kernel,
        out_shape=jax.ShapeDtypeStruct((depth, len(pieces) * pixels), low),
        grid=(depth // block,),
        in_specs=[spec((pixels, block), lambda i: (0, i))] * len(pieces),
        out_specs=spec((block, len(pieces) * pixels), lambda i: (i, 0)),
        compiler_params=params(),
        cost_estimate=cost(0, 4 * len(pieces) * pixels * depth),
    )(*pieces)


def weight_grad_kernel(members, side_tasks, tasks, groups, *refs):
    slot_ref, task_ref, x_ref = refs[:3]
    chips = groups // 2
    center_refs, side_refs = refs[3 : 3 + chips], refs[3 + chips : 3 + groups]
    mask_refs = refs[3 + groups : 3 + 2 * groups]
    out_ref, dy_ref, total_ref = refs[3 + 2 * groups :]
    pixels = center_refs[0].shape[0]
    lane = center_refs[0].shape[1] // (2 * tasks)
    slots = len(side_tasks)
    three = 3 * lane

    def spread(j, i, grad_ref, at, task):
        rows = slice(j * pixels, (j + 1) * pixels)
        held = grad_ref[:, at * lane : (at + 1) * lane]
        dy_ref[rows, i * three + lane : i * three + 2 * lane] = held
        rate = head_rates[task]
        for k, shift in ((0, pixels - rate), (2, rate)):
            piece = held.astype(full) * mask_refs[j][:, 3 * task + k : 3 * task + k + 1]
            columns = slice(i * three + k * lane, i * three + (k + 1) * lane)
            dy_ref[rows, columns] = pltpu.roll(piece, shift, 0).astype(low)

    @pl.when(pl.program_id(0) == 0)
    def _():
        for j in range(groups):
            for i, item in enumerate(members):
                if item < tasks:
                    spread(j, i, center_refs[j // 2], j % 2 * tasks + item, item)
                    continue
                at = item - tasks
                for task in side_tasks[at]:
                    move = lambda j=j, i=i, at=at, task=task: spread(
                        j, i, side_refs[j // 2], j % 2 * slots + at, task
                    )
                    if len(side_tasks[at]) == 1:
                        move()
                    else:
                        pl.when(task_ref[at] == task)(move)

    total_ref[...] = jnp.dot(x_ref[...], dy_ref[...], preferred_element_type=full)
    for g in range(out_ref.shape[1] // three):
        columns = slice(g * three, (g + 1) * three)

        @pl.when(slot_ref[g] >= 0)
        def _():
            start = pl.multiple_of(slot_ref[g] * three, 128)
            out_ref[:, columns] = total_ref[:, pl.ds(start, three)].astype(low)

        @pl.when(slot_ref[g] < 0)
        def _():
            out_ref[:, columns] = jnp.zeros((out_ref.shape[0], three), low)


def weight_grad(turned, centers, sides, masks, slot_of, side_task, side_tasks, tasks):
    three = 3 * centers[0].shape[1] // (2 * tasks)
    items = tasks + len(side_tasks)
    few = max(1, 2**24 // (turned.shape[1] * three * 2))
    total = None
    for start in range(0, items, few):
        members = list(range(start, min(start + few, items)))
        here = (slot_of >= start) & (slot_of < start + few)
        slots = jnp.where(here, slot_of - start, -1)
        part = some_weight_grad(
            turned, centers, sides, masks, slots, side_task, side_tasks, tasks, members
        )
        total = part if total is None else total + part
    return total


def some_weight_grad(
    turned, centers, sides, masks, slot_of, side_task, side_tasks, tasks, members
):
    depth, pixels = turned.shape
    groups = len(masks)
    parts = slot_of.shape[0]
    three = 3 * centers[0].shape[1] // (2 * tasks)
    items = len(members)
    block = min(depth, 512)
    fixed = lambda g, s, t: (0, 0)
    return pl.pallas_call(
        lambda *refs: weight_grad_kernel(members, side_tasks, tasks, groups, *refs),
        out_shape=jax.ShapeDtypeStruct((depth, parts * three), low),
        grid_spec=pltpu.PrefetchScalarGridSpec(
            num_scalar_prefetch=2,
            grid=(depth // block,),
            in_specs=[spec((block, pixels), lambda g, s, t: (g, 0))]
            + [spec(array.shape, fixed) for array in (*centers, *sides, *masks)],
            out_specs=spec((block, parts * three), lambda g, s, t: (g, 0)),
            scratch_shapes=[
                pltpu.VMEM((pixels, items * three), low),
                pltpu.VMEM((block, items * three), full),
            ],
        ),
        compiler_params=params(),
        cost_estimate=cost(
            2 * pixels * depth * items * three, 2 * depth * (pixels + parts * three)
        ),
    )(slot_of, side_task, turned, *centers, *sides, *masks)


def place_halves_kernel(core_ref, mine_ref, other_ref, out_ref):
    parts, half, _ = mine_ref.shape
    for i in range(parts):
        for ref, which in ((mine_ref, core_ref[0]), (other_ref, 1 - core_ref[0])):
            row = pl.multiple_of((2 * i + which) * half, half)
            out_ref[pl.ds(row, half), :] = ref[i]


def place_halves(mine, other, core, half):
    parts, _, width = mine.shape
    fixed = lambda i, c: (0, 0, 0)
    return pl.pallas_call(
        place_halves_kernel,
        out_shape=jax.ShapeDtypeStruct((parts * 2 * half, width), low),
        grid_spec=pltpu.PrefetchScalarGridSpec(
            num_scalar_prefetch=1,
            grid=(1,),
            in_specs=[spec((parts, half, width), fixed)] * 2,
            out_specs=spec((parts * 2 * half, width), lambda i, c: (0, 0)),
        ),
        compiler_params=params(),
        cost_estimate=cost(0, 8 * parts * half * width),
    )(core, mine, other)


def place_block_kernel(
    red_rows, mid_rows, exp_rows, ratio, core_ref, mine_ref, other_ref, mid_ref, exp_ref
):
    width = mid_ref.shape[0] // 3
    for i in range(mine_ref.shape[0]):
        for ref, which in ((mine_ref, core_ref[0]), (other_ref, 1 - core_ref[0])):
            row = pl.multiple_of((2 * i + which) * mid_rows, mid_rows)
            for tap in range(9):
                ir, ic = divmod(tap, 3)
                at = red_rows + tap * mid_rows
                mid_ref[pl.ds(ir * width + row, mid_rows), ic * width : (ic + 1) * width] = ref[
                    i, at : at + mid_rows
                ]
            row = pl.multiple_of((2 * i + which) * exp_rows, exp_rows)
            for part in range(ratio):
                at = red_rows + 9 * mid_rows + part * exp_rows
                exp_ref[pl.ds(row, exp_rows), part * width : (part + 1) * width] = ref[
                    i, at : at + exp_rows
                ]


def place_block(mine, other, core, red_rows, mid_rows, exp_rows, ratio):
    width = mine.shape[2]
    fixed = lambda i, c: (0, 0, 0)
    flat = lambda i, c: (0, 0)
    shapes = [(3 * width, 3 * width), (width, ratio * width)]
    return pl.pallas_call(
        lambda *refs: place_block_kernel(red_rows, mid_rows, exp_rows, ratio, *refs),
        out_shape=[jax.ShapeDtypeStruct(shape, low) for shape in shapes],
        grid_spec=pltpu.PrefetchScalarGridSpec(
            num_scalar_prefetch=1,
            grid=(1,),
            in_specs=[spec(mine.shape, fixed)] * 2,
            out_specs=[spec(shape, flat) for shape in shapes],
        ),
        compiler_params=params(),
        cost_estimate=cost(0, 8 * mine.size),
    )(core, mine, other)


def place_kernel(chips, part_ref, at_ref, *refs):
    at = pl.program_id(0)
    out_ref = refs[-1]
    taps, _, head = out_ref.shape
    share, lane = refs[0].shape[0], head // 2

    @pl.when(part_ref[at] >= 0)
    def _():
        for m in range(chips):
            row = pl.multiple_of((at_ref[0] ^ m) * share, share)
            for ref, core in ((refs[m], at_ref[1]), (refs[chips + m], 1 - at_ref[1])):
                column = pl.multiple_of(core * lane, lane)
                for k in range(taps):
                    out_ref[k, pl.ds(row, share), pl.ds(column, lane)] = ref[
                        :, k * lane : (k + 1) * lane
                    ].astype(full)

    @pl.when(part_ref[at] < 0)
    def _():
        out_ref[...] = jnp.zeros_like(out_ref)


def place_shares(mine, other, part_of, at, head):
    chips = len(mine)
    share = mine[0].shape[0]
    steps = part_of.shape[0]
    picked = lambda i, p, c: (0, jnp.maximum(p[i], 0))
    return pl.pallas_call(
        lambda *refs: place_kernel(chips, *refs),
        out_shape=jax.ShapeDtypeStruct((3 * steps, chips * share, head), full),
        grid_spec=pltpu.PrefetchScalarGridSpec(
            num_scalar_prefetch=2,
            grid=(steps,),
            in_specs=[spec((share, 3 * head // 2), picked)] * (2 * chips),
            out_specs=spec((3, chips * share, head), lambda i, p, c: (i, 0, 0)),
        ),
        compiler_params=params(),
        cost_estimate=cost(0, 36 * steps * chips * share * head // 2),
    )(part_of, at, *mine, *other)


def on_device(
    features,
    crop_scale,
    crop_group,
    labels,
    w_reduce,
    gain_reduce,
    bias_reduce,
    w_middle,
    gain_middle,
    bias_middle,
    w_expand,
    gain_expand,
    bias_expand,
    w_heads,
    gain_heads,
    bias_heads,
    w_class,
    b_class,
):
    rows = features.shape[1]
    cols = features.shape[2]
    depth = features.shape[3]
    width = w_reduce.shape[1]
    tasks = w_heads.shape[1]
    head = w_heads.shape[3]
    own = w_heads.shape[0]
    classes = w_class.shape[2]
    pixels = rows * cols
    line = line_size()
    place = lax.axis_index(LINE)
    group = lax.axis_index(("x", "c"))
    inside = crop_table(crop_scale, crop_group, group, W_UNIT, cols)

    def same(offset):
        return jnp.tile(jnp.sum(inside * along(inside, offset, 0), axis=1), rows)[:, None]

    valid = same(0)
    count = jnp.sum(crop_scale).astype(full) * float(W_UNIT * rows * line)
    crops = float(crop_scale.shape[0])

    core = lax.axis_index("c")
    core_at = core.reshape(1).astype(jnp.int32)
    ratio = depth // width
    red_rows, mid_rows, exp_rows = (w.shape[0] // 2 for w in (w_reduce, w_middle, w_expand))
    red_own = half_of(w_reduce, 0, core)
    mid_own = half_of(w_middle.transpose(1, 0, 2), 1, core).reshape(9 * mid_rows, width)
    exp_own = half_of(w_expand, 0, core).reshape(exp_rows, ratio, width).transpose(1, 0, 2)
    rest_own = jnp.concatenate([mid_own, exp_own.reshape(ratio * exp_rows, width)], axis=0)
    block_own = jnp.concatenate([red_own, rest_own], axis=0)
    source = features.reshape(pixels, depth) * valid.astype(low)
    block_mine = lax.all_gather(block_own, LINE, axis=0, tiled=False)
    block_mine, source = lax.optimization_barrier((block_mine, source))
    block_other = flip(block_mine, [("c", 1)])
    if mid_rows % 16 == 0 and red_rows % 16 == 0:
        red_all = place_halves(block_mine, block_other, core_at, red_rows)
        mid_all, exp_all = place_block(
            block_mine, block_other, core_at, red_rows, mid_rows, exp_rows, ratio
        )
    else:
        block_all = both_halves(block_mine, block_other, core, 1)
        cuts = np.cumsum([0, red_rows, 9 * mid_rows, ratio * exp_rows])
        red_all, mid_all, exp_all = (block_all[:, :, cuts[i] : cuts[i + 1]] for i in range(3))
        red_all = red_all.reshape(depth, width)
        mid_all = mid_all.reshape(line, 2, 3, 3, mid_rows, width).transpose(2, 0, 1, 4, 3, 5)
        mid_all = mid_all.reshape(3 * width, 3 * width)
        exp_all = exp_all.reshape(line, 2, ratio, exp_rows, width).transpose(0, 1, 3, 2, 4)
        exp_all = exp_all.reshape(width, depth)
    terms, table = head_plan(rows)
    slots = table.shape[0]
    three = 3 * head
    by_term = w_heads.reshape(own, tasks, 3, 3, head).transpose(1, 2, 0, 3, 4)
    by_term = by_term.reshape(tasks, 3, own, three)
    parts = [by_term[t, 1] for t in range(tasks)] + [by_term[t, s + 1] for t, s, _ in terms]
    quarter = own // lax.axis_size(("x", "c"))
    heads_own = jnp.concatenate(
        [lax.dynamic_slice_in_dim(part, group * quarter, quarter, axis=0) for part in parts], axis=1
    )
    heads_own, block_mine = lax.optimization_barrier((heads_own, block_mine))
    heads_all = lax.all_gather(heads_own, AXES, axis=0, tiled=True)
    term_tasks = np.array([task for task, _, _ in terms], np.int32)
    picked_term = jnp.asarray(table)[:, place]
    slot_tasks = [sorted({int(term_tasks[e]) for e in table[s]}) for s in range(slots)]
    side_task = jnp.asarray(term_tasks)[picked_term]
    centers = jnp.arange(tasks, dtype=jnp.int32)
    all_tasks = jnp.concatenate([centers, side_task])
    all_picked = jnp.concatenate([centers, tasks + picked_term])

    reduced = dot(source, red_all)
    mean1, scale1 = norm_scale(reduced, count)
    normed1 = (reduced - mean1) * scale1
    out1 = normed1 * gain_reduce + bias_reduce
    hidden1 = (silu(out1) * valid).astype(low)
    edge = mid_rate * cols
    down = [(i, i + 1) for i in range(line - 1)]
    up = [(i + 1, i) for i in range(line - 1)]
    before1 = rows_to(hidden1[pixels - edge :], down)
    after1 = rows_to(hidden1[:edge], up)
    tall = jnp.concatenate([before1, hidden1, after1], axis=0)
    wide1 = jnp.concatenate([tall[i * edge : i * edge + pixels] for i in range(3)], axis=1)
    spread = dot(wide1, mid_all)
    mid_masks = [same((k - 1) * mid_rate) for k in range(3)]
    middled = sum(
        along(spread[:, k * width : (k + 1) * width], (k - 1) * mid_rate, 0) * mid_masks[k]
        for k in range(3)
    )
    mean2, scale2 = norm_scale(middled, count)
    normed2 = (middled - mean2) * scale2
    out2 = normed2 * gain_middle + bias_middle
    hidden2 = (silu(out2) * valid).astype(low)
    expanded = dot(hidden2, exp_all)
    mean3, scale3 = norm_scale(expanded, count)
    normed3 = (expanded - mean3) * scale3
    before = normed3 * gain_expand + bias_expand + source.astype(full)
    grid = (silu(before) * valid).astype(low)

    chips = lax.axis_size("x")
    chip = lax.axis_index("x")
    share = own // chips

    def share_columns(which):
        cuts = [f * own + which * share for f in range(line)]
        return jnp.concatenate(
            [lax.dynamic_slice_in_dim(grid, cut, share, axis=1) for cut in cuts], axis=1
        )

    grid_pieces = []
    for m in range(chips):
        piece = share_columns(chip ^ m)
        piece = flip(piece, [("x", m)]) if m else piece
        grid_pieces += [piece, flip(piece, [("c", 1)])]

    def mask_table(group):
        inside = crop_table(crop_scale, crop_group, group, W_UNIT, cols)
        columns = [
            jnp.sum(inside * along(inside, (k - 1) * rate, 0), axis=1)
            for rate in head_rates
            for k in range(3)
        ]
        table = jnp.pad(jnp.stack(columns, axis=1), ((0, 0), (0, 128 - 3 * tasks)))
        return jnp.tile(table, (rows, 1))

    masks = mask_table(group)
    all_masks = [masks, mask_table(group ^ 1)]
    for m in range(1, chips):
        all_masks += [mask_table((chip ^ m) * 2 + core), mask_table((chip ^ m) * 2 + 1 - core)]
    slot_of = jnp.full((len(terms),), -1, jnp.int32)
    for s in range(slots):
        slot_of = jnp.where(jnp.arange(len(terms)) == picked_term[s], tasks + s, slot_of)
    slot_of = jnp.concatenate([centers, slot_of])
    side_here = (side_task[:, None] == centers[None, :]).astype(full).reshape(-1)
    vecs = jnp.pad(jnp.stack([mean3, scale3, gain_expand, bias_expand]), ((0, 4), (0, 0)))
    side_picked = tasks + picked_term
    grid, all_masks, slot_of, side_here, vecs, side_picked, side_task, picked_term = (
        lax.optimization_barrier(
            (grid, all_masks, slot_of, side_here, vecs, side_picked, side_task, picked_term)
        )
    )
    masks = all_masks[0]
    moves = row_moves(terms, line)
    side_terms = head_terms(grid, heads_all, masks, tasks + picked_term, side_task, head, low)
    moved = [None] * tasks
    for task, pairs, members in moves:
        sends = {f: s for e, froms in members for f in froms for s in range(slots) if table[s, f] == e}
        sent = None
        for s in sorted(set(sends.values())):
            part = side_terms[:, s * head : (s + 1) * head]
            here = jnp.asarray(np.array([sends.get(f) == s for f in range(line)]))[place]
            sent = part if sent is None else jnp.where(here, part, sent)
        got = rows_to(sent, pairs).astype(full)
        moved[task] = got if moved[task] is None else moved[task] + got
    middle_terms = head_terms(grid, heads_all, masks, centers, centers, head, full)
    middle_terms, grid_pieces = lax.optimization_barrier((middle_terms, grid_pieces))
    mixed = []
    for task in range(tasks):
        center = middle_terms[:, task * head : (task + 1) * head]
        mixed.append(center if moved[task] is None else center + moved[task])
    mixed = jnp.concatenate(mixed, axis=1)
    gain_h, bias_h = gain_heads.reshape(-1), bias_heads.reshape(-1)
    mean_h, scale_h = norm_scale(mixed, count)
    normed_h = (mixed - mean_h) * scale_h
    out_h = normed_h * gain_h + bias_h
    activ = (silu(out_h) * valid).astype(low)
    marks = labels.reshape(tasks, pixels)
    class_part, class_bias_part, dactiv = [], [], []
    for task in range(tasks):
        act = activ[:, task * head : (task + 1) * head]
        logits = dot(act, w_class[task]) + b_class[task]
        onehot = (marks[task][:, None] == jnp.arange(classes, dtype=jnp.int32)[None, :]).astype(full)
        dlogits = ((jax.nn.softmax(logits, axis=-1) - onehot) * valid / crops).astype(low)
        class_part.append(dot_tn(dlogits, act))
        class_bias_part.append(jnp.sum(dlogits.astype(full), axis=0))
        dactiv.append(dot_nt(dlogits, w_class[task]))
    dout_h = jnp.concatenate(dactiv, axis=1) * valid * silu_slope(out_h)
    sums_h = all_sum(jnp.stack([jnp.sum(dout_h * normed_h, axis=0), jnp.sum(dout_h, axis=0)]))
    dgain_h, dbias_h = sums_h[0], sums_h[1]
    dmixed = valid * (gain_h * scale_h) * (dout_h - dbias_h / count - normed_h * (dgain_h / count))
    dmixed = dmixed.astype(low)

    class_sums = jnp.concatenate(
        [jnp.concatenate(class_part, axis=0), jnp.pad(jnp.stack(class_bias_part), ((0, 0), (0, head - classes)))],
        axis=0,
    )
    class_sums = class_sums + flip(class_sums, [("c", 1)])
    class_sums = sum_along(class_sums, "y")
    lane = head // 2
    tap_half = 3 * lane

    def half_taps(grads, which):
        cuts = [i * head + which * lane for i in range(grads.shape[1] // head)]
        return jnp.concatenate(
            [lax.dynamic_slice_in_dim(grads, cut, lane, axis=1) for cut in cuts], axis=1
        )

    def from_groups(grads):
        halves = [half_taps(grads, core), flip(half_taps(grads, 1 - core), [("c", 1)])]
        halves = jnp.concatenate(halves, axis=1)
        return [halves] + [flip(halves, [("x", m)]) for m in range(1, chips)]

    center_halves = from_groups(dmixed)
    back = [None] * len(terms)
    for task, pairs, members in moves:
        got = rows_to(dmixed[:, task * head : (task + 1) * head], [(t, f) for f, t in pairs])
        for e, froms in members:
            here = jnp.asarray(np.array([f in froms for f in range(line)]))[place]
            back[e] = got if len(members) == 1 else jnp.where(here, got, jnp.zeros_like(got))
    dsides = []
    for s in range(slots):
        dside = back[table[s][0]]
        for e in sorted(set(table[s].tolist()) - {int(table[s][0])}):
            dside = jnp.where(picked_term[s] == e, back[e], dside)
        dsides.append(dside)
    dys = spread_back(dmixed, masks, centers, head, pixels)
    *center_grads, slope3, normed3 = center_back(
        dys, heads_all, tasks, expanded, source, vecs, masks, 512
    )
    center_grads, slope3, normed3, turned, dsides, center_halves, class_sums = (
        lax.optimization_barrier(
            (
                center_grads,
                slope3,
                normed3,
                turn(grid_pieces),
                jnp.concatenate(dsides, axis=1),
                center_halves,
                class_sums,
            )
        )
    )
    class_sums = sum_along(class_sums, "z")
    side_halves = from_groups(dsides)
    dys = spread_back(dsides, masks, side_task, head, pixels)
    shared_grads, sums = side_back(
        dys, heads_all, side_picked, side_here, slot_tasks, tasks, center_grads, slope3, normed3, 512
    )
    sums, center_halves, side_halves, class_sums = lax.optimization_barrier(
        (sums, center_halves, side_halves, class_sums)
    )
    class_sums = sum_along(class_sums, "x")
    gram_part = jnp.sum(sums[2 * tasks : 4 * tasks], axis=1)
    gram_row = jnp.pad(gram_part, (0, depth - gram_part.shape[0]))[None, :]
    summed = all_sum(jnp.concatenate([sums[: 2 * tasks], gram_row], axis=0))
    sums3 = summed[: 2 * tasks].reshape(tasks, 2, depth)
    weight_list = task_scales([summed[2 * tasks, i] for i in range(6)])
    task_weights = jnp.stack(weight_list)

    head_part = weight_grad(
        turned, center_halves, side_halves, all_masks, slot_of, side_task, slot_tasks, tasks
    )
    shared_grads, head_part = lax.optimization_barrier((shared_grads, head_part))
    head_part = head_part.reshape(line, share, len(parts) * tap_half)
    head_own = lax.psum_scatter(head_part, LINE, scatter_dimension=0, tiled=False)

    dgain3, dbias3 = (
        sum(weight_list[t] * sums3[t, j] for t in range(tasks)) for j in range(2)
    )
    vec_rows = [gain_expand * scale3, jnp.broadcast_to(1.0 / count, (depth,))]
    vecs = jnp.pad(jnp.stack(vec_rows), ((0, 6), (0, 0)))
    mid_vecs = jnp.pad(jnp.stack([mean2, scale2, gain_middle, bias_middle]), ((0, 4), (0, 0)))
    dbefore, exp_part, dout2, sums2 = expand_back(
        summed, shared_grads, slope3, normed3, vecs, masks, hidden2, exp_all, middled,
        mid_vecs, 512,
    )
    sums2 = all_sum(sums2[:2])
    dgain2, dbias2 = sums2[0], sums2[1]
    dmiddled = valid * (gain_middle * scale2) * (
        dout2 - dbias2 / count - normed2 * (dgain2 / count)
    )
    dmiddled = dmiddled.astype(low)
    dspread = jnp.concatenate(
        [along(dmiddled * mid_masks[k].astype(low), -(k - 1) * mid_rate, 0) for k in range(3)],
        axis=1,
    )
    dwide = dot_nt(dspread, mid_all)
    from_below = rows_to(dwide[:edge, :width].astype(low), up).astype(full)
    from_above = rows_to(dwide[pixels - edge :, 2 * width :].astype(low), down).astype(full)
    dspread, exp_part, dwide = lax.optimization_barrier((dspread, exp_part, dwide))
    mid_part = dot_tn(wide1, dspread).astype(low).reshape(3, line, 2, mid_rows, 3 * width)
    exp_part = exp_part.reshape(line, 2, exp_rows, depth)

    def later_half(which):
        mid_half = lax.dynamic_index_in_dim(mid_part, which, 2, keepdims=False)
        exp_half = lax.dynamic_index_in_dim(exp_part, which, 1, keepdims=False)
        pieces = [
            mid_half[i, :, :, k * width : (k + 1) * width] for i in range(3) for k in range(3)
        ]
        pieces += [exp_half[:, :, k * width : (k + 1) * width] for k in range(ratio)]
        return jnp.concatenate(pieces, axis=1)

    later_other = flip(later_half(1 - core), [("c", 1)])
    later = (later_half(core).astype(full) + later_other.astype(full)).astype(low)
    dhidden1 = (
        dwide[:, width : 2 * width]
        + jnp.concatenate([dwide[edge:, :width], from_below], axis=0)
        + jnp.concatenate([from_above, dwide[: pixels - edge, 2 * width :]], axis=0)
    )
    dout1 = dhidden1 * valid * silu_slope(out1)
    sums1 = all_sum(jnp.stack([jnp.sum(dout1 * normed1, axis=0), jnp.sum(dout1, axis=0)]))
    sums1, later = lax.optimization_barrier((sums1, later))
    cut = later.shape[1] // 64 * 32
    first, second = scatter_x(later[:, :cut], 1), scatter_x(later[:, cut:], 1)
    second, head_own = lax.optimization_barrier((second, head_own))
    head_shares = [head_own] + [flip(head_own, [("x", m)]) for m in range(1, chips)]
    head_others = [flip(part, [("c", 1)]) for part in head_shares]
    later_own = [scatter_z(scatter_y(piece)) for piece in (first, second)]
    dgain1, dbias1 = sums1[0], sums1[1]
    dreduced = valid * (gain_reduce * scale1) * (
        dout1 - dbias1 / count - normed1 * (dgain1 / count)
    )
    dreduced = dreduced.astype(low)
    dfeatures = dbefore.astype(full) + dot_nt(dreduced, red_all)

    red_part = dot_tn(source, dreduced).astype(low).reshape(line, -1, width)
    red_sum = over_groups(scatter_z(scatter_y(between_cores(red_part))))
    red_sum = both_halves(*red_sum, core, 0).astype(full)
    part_of = np.full((tasks, 3), -1, np.int32)
    part_of[:, 1] = np.arange(tasks)
    for e, (task, side, _) in enumerate(terms):
        part_of[task, side + 1] = tasks + e
    at = jnp.stack([chip, core]).astype(jnp.int32)
    heads_out = place_shares(head_shares, head_others, jnp.asarray(part_of.reshape(-1)), at, head)
    heads_out = heads_out.reshape(tasks, 9, own, head).transpose(2, 0, 1, 3)
    first, second = later_own
    first, (heads_out, second) = gather_x(first), lax.optimization_barrier((heads_out, second))
    later_own = jnp.concatenate([first, gather_x(second)], axis=0)
    later_other = flip(later_own, [("c", 1)])
    later_sum = both_halves(
        later_own.reshape(9 + ratio, mid_rows, width),
        later_other.reshape(9 + ratio, mid_rows, width),
        core,
        1,
    ).reshape(9 + ratio, 2 * mid_rows, width)
    mid_sum = later_sum[:9].transpose(1, 0, 2).astype(full)
    exp_sum = later_sum[9:].transpose(1, 0, 2).reshape(2 * exp_rows, depth).astype(full)
    grad_class = class_sums[: tasks * classes].reshape(tasks, classes, head).transpose(0, 2, 1)
    grad_class_bias = class_sums[tasks * classes :, :classes]
    return (
        dfeatures.reshape(1, rows, cols, depth),
        red_sum.reshape(w_reduce.shape),
        mid_sum,
        exp_sum,
        heads_out,
        dgain1,
        dbias1,
        dgain2,
        dbias2,
        dgain3,
        dbias3,
        dgain_h.reshape(tasks, head),
        dbias_h.reshape(tasks, head),
        grad_class,
        grad_class_bias,
        task_weights,
    )


def solution(mesh):
    line, groups = mesh.shape["fsdp"], mesh.shape["dp"]
    fine = Mesh(mesh.devices.reshape(line // 2, 2, groups // 2, 2), AXES)
    dp = ("x", "c")
    rows = P(LINE)
    in_specs = (
        P(dp, LINE, None, None),
        P(),
        P(),
        P(None, dp, LINE, None),
        rows,
        P(),
        P(),
        rows,
        P(),
        P(),
        rows,
        P(),
        P(),
        rows,
        P(),
        P(),
        P(),
        P(),
    )
    out_specs = (P(dp, LINE, None, None),) + (rows,) * 4 + (P(),) * 11
    return jax.shard_map(
        on_device, mesh=fine, in_specs=in_specs, out_specs=out_specs, check_vma=False
    )
```
